32 devices in a mesh: context: 8 (over z, core), heads: 4 (over y, x).
Axes of the slice: x: 2, y: 2, z: 4, core: 2. Of those that a mesh axis runs over, the one named last changes fastest.
Arguments:
- main_query: bfloat16 [64, 128, 576], P('context', 'heads'), may hold values from -6 to 6
- latent_keys: bfloat16 [16384, 576], P('context'), may hold values from -6 to 6
- head_lse: float32 [64, 128], P(None, 'heads'), may hold values from 4 to 8
- lengths: int32 [64], replicated, may hold values from 1 to 16384, as said below
- index_query: bfloat16 [64, 64, 128], P('heads'), may hold values from -256 to 256
- index_key: bfloat16 [16384, 128], P('context'), may hold values from -8 to 8
- index_weight: float32 [64, 64], P('heads'), may hold values from -2.4 to 2.4
Outputs:
- grad_index_query: float32 [64, 64, 128], P('heads', 'context')
- grad_index_key: float32 [16384, 128], P(('context', 'heads'))
The draws below stay inside these ranges and needn't reach their ends.
Inputs may be any that keep to these rules, and one draw needn't show every extreme that they name: Query rows come in blocks of 16 consecutive rows whose lengths rise by one from row to row; some block ends at the last key.
All inputs are finite; a program needn't handle non-finite values.
Results may differ from the reference program's by a relative error of at most 0.0029.
Values may be sent and summed in bfloat16 or wider, within the bound.
No kernel may reach another device: no remote copies, remote signals or barrier semaphores. Data moves between devices by JAX's collectives and lax.ppermute only.
A program may use at most 64 MiB of HBM per device.

```python
import math
import jax
import jax.numpy as jnp
from jax import lax

HEADS = 128
LATENT = 576
IDX_HEADS = 64
IDX_DIM = 128
GROUP = 16
QUERIES = 64
KEYS = 16384


def index_draws(key):
    base = jax.random.fold_in(key, 4099)
    key_query, key_keys, key_weight = jax.random.split(base, 3)
    query_vals = jnp.clip(jax.random.normal(key_query, (QUERIES, IDX_HEADS, IDX_DIM), jnp.float32), -4.0, 4.0)
    key_vals = jnp.clip(jax.random.normal(key_keys, (KEYS, IDX_DIM), jnp.float32), -4.0, 4.0)
    weight_vals = jnp.clip(0.6 * jax.random.normal(key_weight, (QUERIES, IDX_HEADS), jnp.float32), -2.4, 2.4)
    query_vals = query_vals.astype(jnp.bfloat16).astype(jnp.float32)
    key_vals = key_vals.astype(jnp.bfloat16).astype(jnp.float32)
    return (query_vals, key_vals, weight_vals)


def draw_index_query(key, part):
    return index_draws(key)[0].astype(jnp.bfloat16)


def draw_index_key(key, part):
    return index_draws(key)[1].astype(jnp.bfloat16)


def draw_index_weight(key, part):
    return index_draws(key)[2]


def draw_lengths(key, part):
    group_total = QUERIES // GROUP
    key_offset, key_first = jax.random.split(jax.random.fold_in(key, 1201), 2)
    offsets = jax.random.randint(key_offset, (group_total,), 0, KEYS - GROUP + 1, dtype=jnp.int32)
    first_group = jax.random.randint(key_first, (), 0, group_total, dtype=jnp.int32)
    offsets = offsets.at[first_group].set(KEYS - GROUP)
    within = jnp.arange(QUERIES, dtype=jnp.int32)
    return offsets[within // GROUP] + within % GROUP + 1


def shard_levels(own_key, dims, pieces, low, largest):
    level, own = 1.0, jax.random.fold_in(own_key, 6)
    for position, blocks in pieces:
        draws = jnp.exp(jax.random.uniform(jax.random.fold_in(own, position), (blocks,), jnp.float32, low / len(pieces), largest / len(pieces)))
        level = level * jnp.repeat(draws, dims[position] // blocks).reshape([-1 if axis == position else 1 for axis in range(len(dims))])
    return level


def scatter_about(key, shape, deviation, limit, pieces=(), kind=jnp.bfloat16):
    values = jax.random.normal(key, shape, jnp.float32) * deviation
    if len(pieces) > 0:
        values = shard_levels(key, shape, pieces, -0.22, 0.18) * values
    return jnp.clip(values, min=-limit, max=limit).astype(kind)


def setup_inputs(seed: int = 0) -> dict:
    keys = jax.random.split(jax.random.key(seed), 8)
    return {
        "main_query": scatter_about(keys[0], (QUERIES, HEADS, LATENT), 1.0, 6.0, ((0, 8), (1, 4))),
        "latent_keys": scatter_about(keys[1], (KEYS, LATENT), 1.0, 6.0, ((0, 8),)),
        "head_lse": jnp.clip(4.0 + 4.0 * jax.random.uniform(keys[2], (QUERIES, HEADS), jnp.float32) ** shard_levels(keys[2], (QUERIES, HEADS), ((1, 4),), -0.2, 0.2), 4.0, 8.0),
        "lengths": draw_lengths(jax.random.fold_in(keys[7], 71), 0),
        "index_query": draw_index_query(jax.random.fold_in(keys[7], 71), 0),
        "index_key": draw_index_key(jax.random.fold_in(keys[7], 71), 0),
        "index_weight": draw_index_weight(jax.random.fold_in(keys[7], 71), 0),
    }


main_scale = 192.0 ** -0.5
loss_scale = 64.0
masked_low = -1e30


def reference(main_query, latent_keys, head_lse, lengths, index_query, index_key, index_weight):
    block_keys = math.gcd(KEYS, 512)
    block_total = KEYS // block_keys
    key_pos = jnp.arange(KEYS, dtype=jnp.int32)
    visible = key_pos[None, :] < lengths.astype(jnp.int32)[:, None]
    query_wide = main_query.astype(jnp.float32)

    def mass_block(latent_block):
        scores = jnp.einsum("thd,sd->ths", query_wide, latent_block.astype(jnp.float32), precision=lax.Precision.HIGHEST) * main_scale
        return jnp.sum(jnp.exp(scores - head_lse[:, :, None]), axis=1)

    stacked = lax.map(mass_block, latent_keys.reshape(block_total, block_keys, LATENT))
    row_mass = jnp.moveaxis(stacked, 0, 1).reshape(QUERIES, KEYS)
    row_mass = jnp.where(visible, row_mass, 0.0)
    target = row_mass / jnp.sum(row_mass, axis=1)[:, None]

    index_scale = IDX_DIM ** -0.5
    index_wide = index_query.astype(jnp.float32)
    key_blocks = index_key.reshape(block_total, block_keys, IDX_DIM)

    def block_dots(key_block):
        return jnp.einsum("tjd,sd->tjs", index_wide, key_block.astype(jnp.float32), precision=lax.Precision.HIGHEST)

    def block_logits(key_block):
        return jnp.einsum("tj,tjs->ts", index_weight, jax.nn.relu(block_dots(key_block)), precision=lax.Precision.HIGHEST) * index_scale

    logits = jnp.moveaxis(lax.map(block_logits, key_blocks), 0, 1).reshape(QUERIES, KEYS)
    top = jnp.max(jnp.where(visible, logits, masked_low), axis=1)
    weights_exp = jnp.where(visible, jnp.exp(logits - top[:, None]), 0.0)
    probability = weights_exp / jnp.sum(weights_exp, axis=1)[:, None]
    slopes = loss_scale * (probability - target)
    slope_blocks = slopes.reshape(QUERIES, block_total, block_keys).transpose(1, 0, 2)

    def back_step(query_grad, inputs):
        key_block, slope_block = inputs
        products = block_dots(key_block)
        terms = jnp.where(products > 0, slope_block[:, None, :] * index_weight[:, :, None] * index_scale, 0.0)
        terms = lax.optimization_barrier(terms.astype(jnp.bfloat16)).astype(jnp.float32)
        key_wide = key_block.astype(jnp.float32)
        query_grad = query_grad + jnp.einsum("tjs,sd->tjd", terms, key_wide, precision=lax.Precision.HIGHEST)
        key_grad = jnp.einsum("tjs,tjd->sd", terms, index_wide, precision=lax.Precision.HIGHEST)
        return query_grad, key_grad

    start_grad = jnp.zeros((QUERIES, IDX_HEADS, IDX_DIM), jnp.float32)
    query_grad, key_grads = lax.scan(back_step, start_grad, (key_blocks, slope_blocks))
    return query_grad, key_grads.reshape(KEYS, IDX_DIM)
```

```python
import functools
import math

import jax
import jax.numpy as jnp
from jax import lax
from jax.experimental import pallas as pl
from jax.experimental.pallas import tpu as pltpu
from jax.sharding import PartitionSpec as P

main_scale = 192.0 ** (-0.5)
loss_scale = 64.0
masked_low = -1e30
log2_e = math.log2(math.e)
lanes = 128
vmem_bytes = 48 * 1024 * 1024

def joined(part, axis, combine):
    gathered = jax.tree.map(lambda a: lax.all_gather(a, axis), part)

    def take(source):
        return jax.tree.map(lambda a: lax.dynamic_index_in_dim(a, source, 0, False), gathered)

    return lax.fori_loop(
        1, lax.axis_size(axis), lambda source, state: combine(state, take(source)), take(0)
    )


def head_mass(queries, lse_rows, len_rows, latent, first_key):
    row_count = queries.shape[0]
    block_rows = math.gcd(row_count, 64)
    steps_count = row_count // block_rows
    key_pos = first_key + jnp.arange(latent.shape[0], dtype=jnp.int32)

    def one_block(inputs):
        query_block, lse_block, len_block = inputs
        scores = (
            jnp.einsum("rhd,sd->rhs", query_block, latent, preferred_element_type=jnp.float32)
            * main_scale
        )
        summed = jnp.sum(jnp.exp(scores - lse_block[:, :, None]), axis=1)
        return jnp.where(key_pos[None, :] < len_block[:, None], summed, 0.0)

    stacked = lax.map(
        one_block,
        (
            queries.reshape((steps_count, block_rows) + queries.shape[1:]),
            lse_rows.reshape(steps_count, block_rows, lse_rows.shape[1]),
            len_rows.reshape(steps_count, block_rows),
        ),
    )
    return stacked.reshape(row_count, latent.shape[0])


def general_on_device(main_query, latent_keys, head_lse, lengths, index_query, index_key, index_weight):
    key_count = latent_keys.shape[0]
    first_key = lax.axis_index("context") * key_count
    own_rows = index_query.shape[0]
    row_first = lax.axis_index("heads") * own_rows
    partial_mass = head_mass(
        lax.all_gather(main_query, "context", axis=0, tiled=True),
        head_lse,
        lengths,
        latent_keys,
        first_key,
    )
    summed_mass = lax.psum(partial_mass, "heads")
    row_mass = lax.dynamic_slice_in_dim(summed_mass, row_first, own_rows, 0)
    own_len = lax.dynamic_slice_in_dim(lengths, row_first, own_rows, 0)
    visible = (first_key + jnp.arange(key_count, dtype=jnp.int32))[None, :] < own_len[:, None]
    heads_count = index_query.shape[1]
    width = index_query.shape[2]
    index_scale = width ** (-0.5)
    flat_query = index_query.reshape(own_rows * heads_count, width)
    block_keys = math.gcd(key_count, 512)
    block_total = key_count // block_keys
    key_blocks = index_key.reshape(block_total, block_keys, width)

    def block_dots(key_block):
        products = lax.dot_general(
            flat_query, key_block, (((1,), (1,)), ((), ())), preferred_element_type=jnp.float32
        )
        return products.reshape(own_rows, heads_count, key_block.shape[0])

    def block_logits(key_block):
        return (
            jnp.einsum(
                "tj,tjs->ts",
                index_weight,
                jax.nn.relu(block_dots(key_block)),
                precision=lax.Precision.HIGHEST,
            )
            * index_scale
        )

    logits = jnp.moveaxis(lax.map(block_logits, key_blocks), 0, 1).reshape(own_rows, key_count)
    local_top = jnp.max(jnp.where(visible, logits, masked_low), axis=1)
    mass_local = jnp.sum(row_mass, axis=1)
    local_exp = jnp.where(visible, jnp.exp(logits - local_top[:, None]), 0.0)

    def combine(first, second):
        highest = jnp.maximum(first[0], second[0])
        merged = first[1] * jnp.exp(first[0] - highest) + second[1] * jnp.exp(second[0] - highest)
        return (highest, merged, first[2] + second[2])

    top, share_sum, mass_total = joined(
        (local_top, jnp.sum(local_exp, axis=1), mass_local), "context", combine
    )
    weights_exp = jnp.where(visible, jnp.exp(logits - top[:, None]), 0.0)
    probability = weights_exp / share_sum[:, None]
    target = row_mass / mass_total[:, None]
    slopes = loss_scale * (probability - target)
    slope_blocks = slopes.reshape(own_rows, block_total, block_keys).transpose(1, 0, 2)

    def back_step(query_grad, inputs):
        key_block, slope_block = inputs
        products = block_dots(key_block)
        terms = jnp.where(
            products > 0, slope_block[:, None, :] * index_weight[:, :, None] * index_scale, 0.0
        )
        terms = terms.astype(jnp.bfloat16).reshape(own_rows * heads_count, key_block.shape[0])
        query_grad = query_grad + jnp.dot(terms, key_block, preferred_element_type=jnp.float32)
        key_grad = lax.dot_general(
            terms, flat_query, (((0,), (0,)), ((), ())), preferred_element_type=jnp.float32
        )
        return (query_grad, key_grad)

    start_grad = jnp.zeros((own_rows * heads_count, width), jnp.float32)
    query_grad, key_grads = lax.scan(back_step, start_grad, (key_blocks, slope_blocks))
    query_grad = query_grad.reshape(own_rows, heads_count, width)
    key_grad = key_grads.reshape(key_count, width)
    out_query = lax.psum_scatter(query_grad, "context", scatter_dimension=1, tiled=True)
    out_key = lax.psum_scatter(key_grad, "heads", scatter_dimension=0, tiled=True)
    return (out_query, out_key)


def local_call(kernel, out_shape, name, grid=None, in_specs=None, out_specs=None, scratch=(), flops=0, moved=0):
    settings = dict(
        out_shape=out_shape,
        scratch_shapes=list(scratch),
        name=name,
        compiler_params=pltpu.CompilerParams(vmem_limit_bytes=vmem_bytes),
        cost_estimate=pl.CostEstimate(flops=flops, bytes_accessed=moved, transcendentals=0),
    )
    if grid is not None:
        settings["grid"] = grid
    if in_specs is not None:
        settings["in_specs"] = in_specs
    if out_specs is not None:
        settings["out_specs"] = out_specs
    return pl.pallas_call(kernel, **settings)


def whole():
    return pl.BlockSpec(memory_space=pltpu.VMEM)


def scalars():
    return pl.BlockSpec(memory_space=pltpu.SMEM)


def fixed(shape):
    return pl.BlockSpec(shape, lambda step: (0,) * len(shape))


def f32(shape):
    return jax.ShapeDtypeStruct(shape, jnp.float32)


def bf16(shape):
    return jax.ShapeDtypeStruct(shape, jnp.bfloat16)


info_first, info_plane, info_core, info_heads, info_lengths = 0, 1, 2, 3, 4


def pack_kernel(query_ref, out_ref):
    rows, heads, width = query_ref.shape
    total = rows * heads
    columns = width // lanes
    stacked = jnp.swapaxes(query_ref[...].astype(jnp.float32), 0, 1).reshape(total, width)
    for i in range(columns):
        out_ref[i * total : (i + 1) * total, :] = stacked[:, i * lanes : (i + 1) * lanes].astype(jnp.bfloat16)
    rest = stacked[:, columns * lanes :]
    out_ref[columns * total :, :] = jnp.concatenate([rest[: total // 2], rest[total // 2 :]], axis=1).astype(
        jnp.bfloat16
    )


def packed_queries(queries):
    rows, heads, width = queries.shape
    return local_call(
        pack_kernel,
        bf16((rows * heads * width // lanes, lanes)),
        "pack_queries",
        in_specs=[whole()],
        out_specs=whole(),
        moved=4 * queries.size,
    )(queries)


def unpack(packed, wide_ref, place, total, width):
    columns = width // lanes
    half = total // 2
    for i in range(columns):
        wide_ref[place * total : (place + 1) * total, i * lanes : (i + 1) * lanes] = packed[
            i * total : (i + 1) * total, :
        ]
    rest = packed[columns * total :, :]
    wide_ref[place * total : place * total + half, columns * lanes :] = rest[:, : lanes // 2]
    wide_ref[place * total + half : (place + 1) * total, columns * lanes :] = rest[:, lanes // 2 :]


def length_column(info_ref, first_row, rows, width):
    spread = lax.broadcasted_iota(jnp.int32, (rows, lanes), 0)
    column = jnp.zeros((rows, lanes), jnp.int32)
    for i in range(rows):
        column = jnp.where(spread == i, info_ref[info_lengths + first_row + i], column)
    return widened(column, width)


def widened(column, width):
    return jnp.concatenate([column] * (width // lanes), axis=1)


def shard_mass(info_ref, scores, lse_ref, context, rows, heads, tile, step):
    shifted = scores * (main_scale * log2_e) - widened(lse_ref[context], tile)
    summed = jnp.sum(jnp.exp2(shifted).reshape(heads, rows, tile), axis=0)
    positions = info_ref[info_first] + step * tile + lax.broadcasted_iota(jnp.int32, (rows, tile), 1)
    visible = positions < length_column(info_ref, context * rows, rows, tile)
    return jnp.where(visible, summed, 0.0)


def mass_kernel(flip, places, choose, rows, heads, info_ref, *refs):
    count = len(places)
    packs = refs[: count * (2 if choose else 1)]
    lse_ref, key_ref, out_ref, wide_ref = refs[len(packs) :]
    step = pl.program_id(0)
    tile, width = key_ref.shape
    total = rows * heads

    @pl.when(step == 0)
    def _():
        for n in range(count):
            if choose:
                inner = (info_ref[info_plane] == 1) | (info_ref[info_plane] == 2)
                packed = jnp.where(inner, packs[2 * n][...], packs[2 * n + 1][...])
            else:
                packed = packs[n][...]
            unpack(packed, wide_ref, n, total, width)

    scores = lax.dot_general(
        wide_ref[...], key_ref[...], (((1,), (1,)), ((), ())), preferred_element_type=jnp.float32
    )
    plane = info_ref[info_plane] ^ flip
    for n, place in enumerate(places):
        core = info_ref[info_core] ^ place
        mass = shard_mass(
            info_ref, scores[n * total : (n + 1) * total], lse_ref, 2 * plane + core, rows, heads, tile, step
        )
        if count == 1:
            out_ref[...] = mass
        else:
            out_ref[pl.ds(pl.multiple_of(core * rows, rows), rows), :] = mass


def chunk_mass(info, packs, lse_wide, keys, flip, places, rows, heads, name, choose=False):
    key_count, width = keys.shape
    tile = math.gcd(key_count, 512)
    count = len(places)
    total = rows * heads
    return local_call(
        functools.partial(mass_kernel, flip, places, choose, rows, heads),
        f32((count * rows, key_count)),
        name,
        grid=(key_count // tile,),
        in_specs=[scalars()]
        + [fixed(p.shape) for p in packs]
        + [fixed(lse_wide.shape), pl.BlockSpec((tile, width), lambda step: (step, 0))],
        out_specs=pl.BlockSpec((count * rows, tile), lambda step: (0, step)),
        scratch=[pltpu.VMEM((count * total, width), jnp.bfloat16)],
        flops=2 * count * total * key_count * width,
        moved=2 * keys.size,
    )(info, *packs, lse_wide, keys)


def share_kernel(rows, heads, info_ref, pack_ref, lse_ref, own_ref, near_ref, far_ref, half_ref, key_ref, *refs):
    outs = refs[:-2]
    wide_ref, chunks_ref = refs[-2:]
    step = pl.program_id(0)
    tile, width = key_ref.shape
    total = rows * heads

    @pl.when(step == 0)
    def _():
        unpack(pack_ref[...], wide_ref, 0, total, width)

    scores = lax.dot_general(
        wide_ref[...], key_ref[...], (((1,), (1,)), ((), ())), preferred_element_type=jnp.float32
    )
    core = info_ref[info_core]
    plane = info_ref[info_plane]
    other = 1 - core
    last = shard_mass(info_ref, scores, lse_ref, 2 * (plane ^ 2) + other, rows, heads, tile, step)
    chunks_ref[0] = own_ref[...]
    chunks_ref[1] = near_ref[...]
    chunks_ref[3] = far_ref[...]
    chunks_ref[2, pl.ds(pl.multiple_of(other * rows, rows), rows), :] = last
    chunks_ref[2, pl.ds(pl.multiple_of(core * rows, rows), rows), :] = half_ref[...]
    for e, out_ref in enumerate(outs):
        out_ref[...] = chunks_ref[plane ^ info_ref[info_heads] ^ e].astype(out_ref.dtype)


def shared_mass(info, pack, lse_wide, own, near, far, half, keys, rows, heads, partners):
    key_count, width = keys.shape
    tile = math.gcd(key_count, 512)
    total = rows * heads
    both = 2 * rows
    block = pl.BlockSpec((both, tile), lambda step: (0, step))
    return local_call(
        functools.partial(share_kernel, rows, heads),
        [f32((both, key_count))] + [bf16((both, key_count))] * (partners - 1),
        "mass_and_share",
        grid=(key_count // tile,),
        in_specs=[scalars(), fixed(pack.shape), fixed(lse_wide.shape), block, block, block]
        + [pl.BlockSpec((rows, tile), lambda step: (0, step)), pl.BlockSpec((tile, width), lambda step: (step, 0))],
        out_specs=[block] * partners,
        scratch=[pltpu.VMEM((total, width), jnp.bfloat16), pltpu.VMEM((4, both, tile), jnp.float32)],
        flops=2 * total * key_count * width,
        moved=2 * keys.size,
    )(info, pack, lse_wide, own, near, far, half, keys)


def visible_tile(info_ref, rows, first, width):
    positions = info_ref[info_first] + first + lax.broadcasted_iota(jnp.int32, (rows, width), 1)
    return positions < length_column(info_ref, info_ref[info_heads] * rows, rows, width)


def logits_kernel(info_ref, query_ref, key_ref, weight_ref, logits_ref, stats_ref):
    rows, key_count = logits_ref.shape
    heads = query_ref.shape[0] // rows
    tile = math.gcd(key_count, 256)
    best = jnp.full((rows, 1), masked_low, jnp.float32)
    for first in range(0, key_count, tile):
        dots = lax.dot_general(
            query_ref[...], key_ref[first : first + tile, :], (((1,), (1,)), ((), ())),
            preferred_element_type=jnp.float32,
        )
        weighed = jnp.maximum(dots, 0.0) * widened(weight_ref[...], tile)
        logits = jnp.sum(weighed.reshape(rows, heads, tile), axis=1)
        logits_ref[:, first : first + tile] = logits
        seen = jnp.where(visible_tile(info_ref, rows, first, tile), logits, masked_low)
        best = jnp.maximum(best, jnp.max(seen, axis=1, keepdims=True))
    shares = jnp.where(visible_tile(info_ref, rows, 0, key_count), jnp.exp(logits_ref[...] - best), 0.0)
    total = jnp.sum(shares, axis=1, keepdims=True)
    place = lax.broadcasted_iota(jnp.int32, (rows, lanes), 1)
    stats_ref[...] = jnp.where(place == 0, best, total)


def index_logits(info, flat_query, index_key, weight_wide, rows):
    key_count = index_key.shape[0]
    return local_call(
        logits_kernel,
        [f32((rows, key_count)), f32((rows, lanes))],
        "index_logits",
        in_specs=[scalars()] + [whole()] * 3,
        out_specs=[whole()] * 2,
        flops=2 * flat_query.size * key_count,
        moved=2 * index_key.size,
    )(info, flat_query, index_key, weight_wide)


def join_kernel(stats_ref, own_ref, *refs):
    parts, (mass_ref, out_ref) = refs[:-2], refs[-2:]
    mass = own_ref[...]
    for part in parts:
        mass = mass + part[...].astype(jnp.float32)
    mass_ref[...] = mass
    place = lax.broadcasted_iota(jnp.int32, out_ref.shape, 1)
    out_ref[...] = jnp.where(place == 2, jnp.sum(mass, axis=1, keepdims=True), stats_ref[...])


def joined_mass(stats, own, parts):
    return local_call(
        join_kernel,
        [f32(own.shape), f32(stats.shape)],
        "join_mass",
        in_specs=[whole()] * (2 + len(parts)),
        out_specs=[whole()] * 2,
        moved=8 * own.size,
    )(stats, own, *parts)


def back_kernel(sources, info_ref, mass_ref, logits_ref, query_ref, turned_ref, key_ref, weight_ref, *refs):
    stats = [ref[...] for ref in refs[:sources]]
    partners = len(refs) - sources - 4
    key_outs = refs[sources : sources + partners]
    keep_ref, send_ref, slope_ref, grad_ref = refs[sources + partners :]
    rows, key_count = mass_ref.shape
    flat, width = query_ref.shape
    heads = flat // rows
    tile = math.gcd(key_count, 256)
    top = functools.reduce(jnp.maximum, [s[:, 0:1] for s in stats])
    shares = sum(s[:, 1:2] * jnp.exp(s[:, 0:1] - top) for s in stats)
    total = sum(s[:, 2:3] for s in stats)
    visible = visible_tile(info_ref, rows, 0, key_count)
    weights_exp = jnp.where(visible, jnp.exp(logits_ref[...] - top), 0.0)
    slope_ref[...] = loss_scale * (weights_exp / shares - mass_ref[...] / total)
    query_grad = jnp.zeros((flat, width), jnp.float32)
    for first in range(0, key_count, tile):
        keys = key_ref[first : first + tile, :]
        dots = lax.dot_general(query_ref[...], keys, (((1,), (1,)), ((), ())), preferred_element_type=jnp.float32)
        slopes = jnp.broadcast_to(slope_ref[:, first : first + tile][:, None, :], (rows, heads, tile))
        scaled = slopes.reshape(flat, tile) * widened(weight_ref[...], tile)
        terms = jnp.where(dots > 0, scaled, 0.0).astype(jnp.bfloat16)
        query_grad = query_grad + jnp.dot(terms, keys, preferred_element_type=jnp.float32)
        key_grad = jnp.dot(turned_ref[...], terms, preferred_element_type=jnp.float32)
        grad_ref[first : first + tile, :] = key_grad.T
    block = key_count // partners
    for e, out_ref in enumerate(key_outs):
        begin = pl.multiple_of((info_ref[info_heads] ^ e) * block, block)
        out_ref[...] = grad_ref[pl.ds(begin, block), :].astype(out_ref.dtype)
    planes = keep_ref.shape[0]
    part = heads // (2 * planes)
    split = query_grad.reshape(rows, planes, 2, part, width)
    first_core = info_ref[info_core] == 0
    for plane in range(planes):
        low, high = split[:, plane, 0], split[:, plane, 1]
        keep_ref[plane] = jnp.where(first_core, low, high).reshape(rows * part, width)
        send_ref[plane] = jnp.where(first_core, high, low).reshape(rows * part, width).astype(jnp.bfloat16)


def back_pass(info, mass, logits, flat_query, turned, index_key, weight_wide, stats, partners, planes):
    rows, key_count = mass.shape
    flat, width = flat_query.shape
    part = flat // (2 * planes)
    return local_call(
        functools.partial(back_kernel, len(stats)),
        [f32((key_count // partners, width))]
        + [bf16((key_count // partners, width))] * (partners - 1)
        + [f32((planes, part, width)), bf16((planes, part, width))],
        "index_back",
        in_specs=[scalars()] + [whole()] * (6 + len(stats)),
        out_specs=[whole()] * (partners + 2),
        scratch=[pltpu.VMEM((rows, key_count), jnp.float32), pltpu.VMEM((key_count, width), jnp.float32)],
        flops=6 * flat * width * key_count,
        moved=8 * key_count * width,
    )(info, mass, logits, flat_query, turned, index_key, weight_wide, *stats)


def pair_kernel(info_ref, keep_ref, got_ref, *outs):
    for e, out_ref in enumerate(outs):
        plane = info_ref[info_plane] ^ e
        out_ref[...] = (keep_ref[plane] + got_ref[plane].astype(jnp.float32)).astype(out_ref.dtype)


def pair_sums(info, keep, got):
    planes, part, width = keep.shape
    return local_call(
        pair_kernel,
        [f32((part, width))] + [bf16((part, width))] * (planes - 1),
        "pair_sums",
        in_specs=[scalars(), whole(), whole()],
        out_specs=[whole()] * planes,
        moved=8 * keep.size,
    )(info, keep, got)


def last_kernel(key_parts, *refs):
    query_out, key_out = refs[-2:]
    key_refs, query_refs = refs[:key_parts], refs[key_parts:-2]
    key_out[...] = sum(ref[...].astype(jnp.float32) for ref in key_refs)
    query_out[...] = sum(ref[...].astype(jnp.float32) for ref in query_refs).reshape(query_out.shape)


def last_sums(key_parts, query_parts, query_shape):
    return local_call(
        functools.partial(last_kernel, len(key_parts)),
        [f32(query_shape), f32(key_parts[0].shape)],
        "last_sums",
        in_specs=[whole()] * (len(key_parts) + len(query_parts)),
        out_specs=[whole()] * 2,
        moved=8 * key_parts[0].size,
    )(*key_parts, *query_parts)


def block_device(main_query, latent_keys, head_lse, lengths, index_query, index_key, index_weight):
    contexts = lax.axis_size("context")
    planes = contexts // 2
    partners = lax.axis_size("heads")
    context = lax.axis_index("context")
    rows, heads, _ = main_query.shape
    own_rows, index_heads, width = index_query.shape
    key_count = latent_keys.shape[0]
    flat = own_rows * index_heads

    def planes_move(array, pairs):
        return lax.ppermute(array, "context", [(2 * a + k, 2 * b + k) for a, b in pairs for k in (0, 1)])

    def context_flip(array, e):
        return lax.ppermute(array, "context", [(c, c ^ e) for c in range(contexts)])

    def heads_flip(array, e):
        return lax.ppermute(array, "heads", [(h, h ^ e) for h in range(partners)])

    info = jnp.concatenate(
        [
            jnp.stack([context * key_count, context // 2, context % 2, lax.axis_index("heads")]).astype(jnp.int32),
            lengths,
        ]
    )
    pack = packed_queries(main_query)
    inner = planes_move(pack, [(1, 2), (2, 1), (0, 0), (3, 3)])
    near = planes_move(pack, [(0, 1), (1, 0), (2, 3), (3, 2)])
    ends = planes_move(pack, [(0, 3), (3, 0)])
    far = planes_move(inner, [(0, 2), (3, 1), (1, 0), (2, 3)])
    own_pair, near_pair, inner_pair, ends_pair, far_pair = (
        context_flip(a, 1) for a in (pack, near, inner, ends, far)
    )

    lse_wide = head_lse.reshape(contexts, rows, heads).transpose(0, 2, 1).reshape(contexts, rows * heads, 1)
    lse_wide = jnp.broadcast_to(lse_wide * log2_e, (contexts, rows * heads, lanes))
    weight_wide = jnp.broadcast_to(index_weight.reshape(flat, 1) * width ** (-0.5), (flat, lanes))
    flat_query = index_query.reshape(flat, width)
    turned = flat_query.T

    logits, stats = index_logits(info, flat_query, index_key, weight_wide, own_rows)
    common = (lse_wide, latent_keys)
    own_mass = chunk_mass(info, [pack, own_pair], *common, 0, (0, 1), rows, heads, "mass_own")
    near_mass = chunk_mass(info, [near, near_pair], *common, 1, (0, 1), rows, heads, "mass_near")
    ends_mass = chunk_mass(
        info, [inner, ends, inner_pair, ends_pair], *common, 3, (0, 1), rows, heads, "mass_ends", choose=True
    )
    far_mass = chunk_mass(info, [far], *common, 2, (0,), rows, heads, "mass_far")
    shared = shared_mass(
        info, far_pair, lse_wide, own_mass, near_mass, ends_mass, far_mass, latent_keys, rows, heads, partners
    )
    mass, stats = joined_mass(stats, shared[0], [heads_flip(shared[e], e) for e in range(1, partners)])
    every = [stats] + [context_flip(stats, e) for e in range(1, contexts)]
    *key_grads, keep, send = back_pass(
        info, mass, logits, flat_query, turned, index_key, weight_wide, every, partners, planes
    )
    got = context_flip(send, 1)
    key_parts = [key_grads[0]] + [heads_flip(key_grads[e], e) for e in range(1, partners)]
    sums = pair_sums(info, keep, got)
    query_parts = [sums[0]] + [context_flip(sums[e], 2 * e) for e in range(1, planes)]
    return last_sums(key_parts, query_parts, (own_rows, index_heads // contexts, width))


def fits(mesh):
    return mesh.shape["context"] == 8 and mesh.shape["heads"] == 4


def solution(mesh):
    placed = (
        P("context", "heads", None),
        P("context", None),
        P(None, "heads"),
        P(),
        P("heads", None, None),
        P("context", None),
        P("heads", None),
    )
    return jax.shard_map(
        block_device if fits(mesh) else general_on_device,
        mesh=mesh,
        in_specs=placed,
        out_specs=(P("heads", "context", None), P(("context", "heads"), None)),
        check_vma=False,
    )
```

```python
import functools
import math

import jax
import jax.numpy as jnp
from jax import lax
from jax.experimental import pallas as pl
from jax.experimental.pallas import tpu as pltpu
from jax.sharding import PartitionSpec as P

main_scale = 192.0 ** (-0.5)
loss_scale = 64.0
masked_low = -1e30
log2_e = math.log2(math.e)
lanes = 128
vmem_bytes = 20 * 1024 * 1024
most_bytes = 60 * 1024 * 1024

def joined(part, axis, combine):
    gathered = jax.tree.map(lambda a: lax.all_gather(a, axis), part)

    def take(source):
        return jax.tree.map(lambda a: lax.dynamic_index_in_dim(a, source, 0, False), gathered)

    return lax.fori_loop(
        1, lax.axis_size(axis), lambda source, state: combine(state, take(source)), take(0)
    )


def head_mass(queries, lse_rows, len_rows, latent, first_key):
    row_count = queries.shape[0]
    block_rows = math.gcd(row_count, 64)
    steps_count = row_count // block_rows
    key_pos = first_key + jnp.arange(latent.shape[0], dtype=jnp.int32)

    def one_block(inputs):
        query_block, lse_block, len_block = inputs
        scores = (
            jnp.einsum("rhd,sd->rhs", query_block, latent, preferred_element_type=jnp.float32)
            * main_scale
        )
        summed = jnp.sum(jnp.exp(scores - lse_block[:, :, None]), axis=1)
        return jnp.where(key_pos[None, :] < len_block[:, None], summed, 0.0)

    stacked = lax.map(
        one_block,
        (
            queries.reshape((steps_count, block_rows) + queries.shape[1:]),
            lse_rows.reshape(steps_count, block_rows, lse_rows.shape[1]),
            len_rows.reshape(steps_count, block_rows),
        ),
    )
    return stacked.reshape(row_count, latent.shape[0])


def general_on_device(main_query, latent_keys, head_lse, lengths, index_query, index_key, index_weight):
    key_count = latent_keys.shape[0]
    first_key = lax.axis_index("context") * key_count
    own_rows = index_query.shape[0]
    row_first = lax.axis_index("heads") * own_rows
    partial_mass = head_mass(
        lax.all_gather(main_query, "context", axis=0, tiled=True),
        head_lse,
        lengths,
        latent_keys,
        first_key,
    )
    summed_mass = lax.psum(partial_mass, "heads")
    row_mass = lax.dynamic_slice_in_dim(summed_mass, row_first, own_rows, 0)
    own_len = lax.dynamic_slice_in_dim(lengths, row_first, own_rows, 0)
    visible = (first_key + jnp.arange(key_count, dtype=jnp.int32))[None, :] < own_len[:, None]
    heads_count = index_query.shape[1]
    width = index_query.shape[2]
    index_scale = width ** (-0.5)
    flat_query = index_query.reshape(own_rows * heads_count, width)
    block_keys = math.gcd(key_count, 512)
    block_total = key_count // block_keys
    key_blocks = index_key.reshape(block_total, block_keys, width)

    def block_dots(key_block):
        products = lax.dot_general(
            flat_query, key_block, (((1,), (1,)), ((), ())), preferred_element_type=jnp.float32
        )
        return products.reshape(own_rows, heads_count, key_block.shape[0])

    def block_logits(key_block):
        return (
            jnp.einsum(
                "tj,tjs->ts",
                index_weight,
                jax.nn.relu(block_dots(key_block)),
                precision=lax.Precision.HIGHEST,
            )
            * index_scale
        )

    logits = jnp.moveaxis(lax.map(block_logits, key_blocks), 0, 1).reshape(own_rows, key_count)
    local_top = jnp.max(jnp.where(visible, logits, masked_low), axis=1)
    mass_local = jnp.sum(row_mass, axis=1)
    local_exp = jnp.where(visible, jnp.exp(logits - local_top[:, None]), 0.0)

    def combine(first, second):
        highest = jnp.maximum(first[0], second[0])
        merged = first[1] * jnp.exp(first[0] - highest) + second[1] * jnp.exp(second[0] - highest)
        return (highest, merged, first[2] + second[2])

    top, share_sum, mass_total = joined(
        (local_top, jnp.sum(local_exp, axis=1), mass_local), "context", combine
    )
    weights_exp = jnp.where(visible, jnp.exp(logits - top[:, None]), 0.0)
    probability = weights_exp / share_sum[:, None]
    target = row_mass / mass_total[:, None]
    slopes = loss_scale * (probability - target)
    slope_blocks = slopes.reshape(own_rows, block_total, block_keys).transpose(1, 0, 2)

    def back_step(query_grad, inputs):
        key_block, slope_block = inputs
        products = block_dots(key_block)
        terms = jnp.where(
            products > 0, slope_block[:, None, :] * index_weight[:, :, None] * index_scale, 0.0
        )
        terms = terms.astype(jnp.bfloat16).reshape(own_rows * heads_count, key_block.shape[0])
        query_grad = query_grad + jnp.dot(terms, key_block, preferred_element_type=jnp.float32)
        key_grad = lax.dot_general(
            terms, flat_query, (((0,), (0,)), ((), ())), preferred_element_type=jnp.float32
        )
        return (query_grad, key_grad)

    start_grad = jnp.zeros((own_rows * heads_count, width), jnp.float32)
    query_grad, key_grads = lax.scan(back_step, start_grad, (key_blocks, slope_blocks))
    query_grad = query_grad.reshape(own_rows, heads_count, width)
    key_grad = key_grads.reshape(key_count, width)
    out_query = lax.psum_scatter(query_grad, "context", scatter_dimension=1, tiled=True)
    out_key = lax.psum_scatter(key_grad, "heads", scatter_dimension=0, tiled=True)
    return (out_query, out_key)


def local_call(kernel, out_shape, name, grid=None, in_specs=None, out_specs=None, scratch=(), flops=0, moved=0, room=vmem_bytes):
    settings = dict(
        out_shape=out_shape,
        scratch_shapes=list(scratch),
        name=name,
        compiler_params=pltpu.CompilerParams(vmem_limit_bytes=room),
        cost_estimate=pl.CostEstimate(flops=flops, bytes_accessed=moved, transcendentals=0),
    )
    if grid is not None:
        settings["grid"] = grid
    if in_specs is not None:
        settings["in_specs"] = in_specs
    if out_specs is not None:
        settings["out_specs"] = out_specs
    return pl.pallas_call(kernel, **settings)


def whole():
    return pl.BlockSpec(memory_space=pltpu.VMEM)


def scalars():
    return pl.BlockSpec(memory_space=pltpu.SMEM)


def fixed(shape):
    return pl.BlockSpec(shape, lambda step: (0,) * len(shape))


def f32(shape):
    return jax.ShapeDtypeStruct(shape, jnp.float32)


def bf16(shape):
    return jax.ShapeDtypeStruct(shape, jnp.bfloat16)


def place():
    context = lax.axis_index("context")
    return context >> 1, context & 1, lax.axis_index("heads")


def hbm():
    return pl.BlockSpec(memory_space=pltpu.HBM)


def pack_kernel(query_ref, out_ref):
    rows, heads, width = query_ref.shape
    total = rows * heads
    columns = width // lanes
    stacked = jnp.swapaxes(query_ref[...].astype(jnp.float32), 0, 1).reshape(total, width)
    for i in range(columns):
        out_ref[i * total : (i + 1) * total, :] = stacked[:, i * lanes : (i + 1) * lanes].astype(jnp.bfloat16)
    rest = stacked[:, columns * lanes :]
    out_ref[columns * total :, :] = jnp.concatenate([rest[: total // 2], rest[total // 2 :]], axis=1).astype(
        jnp.bfloat16
    )


def packed_queries(queries):
    rows, heads, width = queries.shape
    return local_call(
        pack_kernel,
        bf16((rows * heads * width // lanes, lanes)),
        "pack_queries",
        in_specs=[whole()],
        out_specs=whole(),
        flops=2 * queries.size * queries.size // width,
    )(queries)


def pick_kernel(own_ref, got_ref, out_ref):
    plane, _, _ = place()
    inner = (plane == 1) | (plane == 2)

    @pl.when(inner)
    def _():
        out_ref[...] = got_ref[...]

    @pl.when(jnp.logical_not(inner))
    def _():
        out_ref[...] = own_ref[...]


def picked(own, got):
    return local_call(
        pick_kernel, bf16(own.shape), "pick_queries", in_specs=[whole()] * 2, out_specs=whole(), moved=4 * own.size
    )(own, got)


def unpack(packed, wide_ref, slot, total, width):
    columns = width // lanes
    half = total // 2
    for i in range(columns):
        wide_ref[slot * total : (slot + 1) * total, i * lanes : (i + 1) * lanes] = packed[
            i * total : (i + 1) * total, :
        ]
    rest = packed[columns * total :, :]
    wide_ref[slot * total : slot * total + half, columns * lanes :] = rest[:, : lanes // 2]
    wide_ref[slot * total + half : (slot + 1) * total, columns * lanes :] = rest[:, lanes // 2 :]


def widened(column, width):
    return jnp.concatenate([column] * (width // lanes), axis=1)


def shard_mass(length_ref, wide_ref, slot, lse, key_ref, context, rows, heads, first, tile):
    total = rows * heads
    scores = jnp.dot(
        wide_ref[slot * total : (slot + 1) * total, :],
        key_ref[:, first : first + tile],
        preferred_element_type=jnp.float32,
    )
    summed = jnp.zeros((rows, tile), jnp.float32)
    for h in range(heads):
        summed = summed + jnp.exp2(scores[h * rows : (h + 1) * rows] * (main_scale * log2_e) - lse[:, h : h + 1])
    visible = visible_tile(length_ref, context, rows, first, tile, key_ref.shape[1])
    return jnp.where(visible, summed, 0.0)


def rows_at(ref, index, rows):
    return ref[pl.ds(pl.multiple_of(index * rows, rows), rows), :]


def visible_tile(length_ref, block, rows, first, width, key_count):
    positions = lax.axis_index("context") * key_count + first + lax.broadcasted_iota(jnp.int32, (rows, width), 1)
    return positions < widened(rows_at(length_ref, block, rows), width)


def mass_kernel(flip, places, rows, heads, length_ref, *refs):
    count = len(places)
    packs = refs[:count]
    lse_ref, key_ref, out_ref, wide_ref = refs[len(packs) :]
    width, key_count = key_ref.shape
    tile = math.gcd(key_count, 512)
    total = rows * heads
    own_plane, own_core, _ = place()
    plane = own_plane ^ flip
    for n, other in enumerate(places):
        unpack(packs[n][...], wide_ref, n, total, width)
        core = own_core ^ other
        context = 2 * plane + core
        lse = rows_at(lse_ref, context, rows)
        for first in range(0, key_count, tile):
            mass = shard_mass(length_ref, wide_ref, n, lse, key_ref, context, rows, heads, first, tile)
            if count == 1:
                out_ref[:, first : first + tile] = mass
            else:
                out_ref[pl.ds(pl.multiple_of(core * rows, rows), rows), first : first + tile] = mass


def chunk_mass(lengths, packs, lse, keys, flip, places, rows, heads, name):
    width, key_count = keys.shape
    count = len(places)
    total = rows * heads
    return local_call(
        functools.partial(mass_kernel, flip, places, rows, heads),
        f32((count * rows, key_count)),
        name,
        in_specs=[whole()] * (len(packs) + 3),
        out_specs=whole(),
        scratch=[pltpu.VMEM((count * total, width), jnp.bfloat16)],
        flops=2 * count * total * key_count * width,
        moved=2 * keys.size,
    )(lengths, *packs, lse, keys)


def share_kernel(rows, heads, length_ref, pack_ref, lse_ref, own_ref, near_ref, far_ref, half_ref, key_ref, *refs):
    outs = refs[:-2]
    wide_ref, chunks_ref = refs[-2:]
    width, key_count = key_ref.shape
    tile = math.gcd(key_count, 512)
    total = rows * heads
    unpack(pack_ref[...], wide_ref, 0, total, width)
    plane, core, group = place()
    other = 1 - core
    context = 2 * (plane ^ 2) + other
    lse = rows_at(lse_ref, context, rows)
    chunks_ref[0] = own_ref[...]
    chunks_ref[1] = near_ref[...]
    chunks_ref[3] = far_ref[...]
    chunks_ref[2, pl.ds(pl.multiple_of(core * rows, rows), rows), :] = half_ref[...]
    for first in range(0, key_count, tile):
        chunks_ref[2, pl.ds(pl.multiple_of(other * rows, rows), rows), first : first + tile] = shard_mass(
            length_ref, wide_ref, 0, lse, key_ref, context, rows, heads, first, tile
        )
    for e, out_ref in enumerate(outs):
        out_ref[...] = chunks_ref[plane ^ group ^ e].astype(out_ref.dtype)


def shared_mass(lengths, pack, lse, own, near, far, half, keys, rows, heads, partners):
    width, key_count = keys.shape
    total = rows * heads
    both = 2 * rows
    return local_call(
        functools.partial(share_kernel, rows, heads),
        [f32((both, key_count))] + [bf16((both, key_count))] * (partners - 1),
        "mass_and_share",
        in_specs=[whole()] * 8,
        out_specs=[whole()] * partners,
        scratch=[
            pltpu.VMEM((total, width), jnp.bfloat16),
            pltpu.VMEM((4, both, key_count), jnp.float32),
        ],
        flops=2 * total * key_count * width,
        moved=2 * keys.size,
    )(lengths, pack, lse, own, near, far, half, keys)


def logits_kernel(length_ref, query_ref, key_ref, weight_ref, logits_ref, masked_ref, stats_ref):
    rows, key_count = logits_ref.shape
    heads = query_ref.shape[0] // rows
    tile = math.gcd(key_count, 256)
    group = lax.axis_index("heads")
    best = jnp.full((rows, 1), masked_low, jnp.float32)
    weights = widened(weight_ref[...], tile)
    for first in range(0, key_count, tile):
        dots = lax.dot_general(
            query_ref[...], key_ref[first : first + tile, :], (((1,), (1,)), ((), ())),
            preferred_element_type=jnp.float32,
        )
        masked = jnp.where(dots > 0, weights, 0.0)
        masked_ref[:, first : first + tile] = masked
        logits = jnp.sum((dots * masked).reshape(rows, heads, tile), axis=1)
        logits_ref[:, first : first + tile] = logits
        visible = visible_tile(length_ref, group, rows, first, tile, key_count)
        best = jnp.maximum(best, jnp.max(jnp.where(visible, logits, masked_low), axis=1, keepdims=True))
    visible = visible_tile(length_ref, group, rows, 0, key_count, key_count)
    total = jnp.sum(jnp.where(visible, jnp.exp(logits_ref[...] - best), 0.0), axis=1, keepdims=True)
    column = lax.broadcasted_iota(jnp.int32, (rows, lanes), 1)
    stats_ref[...] = jnp.where(column == 0, best, total)


def index_logits(lengths, flat_query, index_key, weight_wide, rows):
    key_count = index_key.shape[0]
    flat = flat_query.shape[0]
    return local_call(
        logits_kernel,
        [f32((rows, key_count)), f32((flat, key_count)), f32((rows, lanes))],
        "index_logits",
        in_specs=[whole()] * 4,
        out_specs=[whole()] * 3,
        flops=2 * flat_query.size * key_count,
        moved=2 * index_key.size,
    )(lengths, flat_query, index_key, weight_wide)


def load_kernel(
    length_ref, lse_ref, weight_ref, query_hbm, key_hbm, latent_hbm,
    length_out, lse_out, weight_out, query_out, turned_out, key_out, latent_out, semaphores,
):
    copies = [
        pltpu.make_async_copy(source, target, semaphores.at[i])
        for i, (source, target) in enumerate(
            [(query_hbm, query_out), (key_hbm, key_out), (latent_hbm, latent_out)]
        )
    ]
    for copy in copies:
        copy.start()
    total = length_out.shape[0]
    spread = lax.broadcasted_iota(jnp.int32, (8, lanes), 0)
    for first in range(0, total, 8):
        column = jnp.zeros((8, lanes), jnp.int32)
        for i in range(8):
            column = jnp.where(spread == i, length_ref[first + i], column)
        length_out[first : first + 8, :] = column
    lse_out[...] = lse_ref[...].T * log2_e
    rows, heads = weight_ref.shape
    width = key_out.shape[1]
    weights = weight_ref[...].T * width ** (-0.5)
    for t in range(rows):
        weight_out[t * heads : (t + 1) * heads, :] = jnp.broadcast_to(weights[:, t : t + 1], (heads, lanes))
    copies[0].wait()
    turned_out[...] = query_out[...].reshape(rows * heads, width).astype(jnp.float32).T.astype(jnp.bfloat16)
    copies[1].wait()
    copies[2].wait()


def load_inputs(lengths, lse, weights, query, key, latent):
    rows, heads, width = query.shape
    flat = rows * heads
    return local_call(
        load_kernel,
        [
            jax.ShapeDtypeStruct((lengths.shape[0], lanes), jnp.int32),
            f32(lse.shape[::-1]),
            f32((flat, lanes)),
            bf16(query.shape),
            bf16((width, flat)),
            bf16(key.shape),
            bf16(latent.shape),
        ],
        "load_inputs",
        in_specs=[scalars(), whole(), whole(), hbm(), hbm(), hbm()],
        out_specs=[whole()] * 7,
        scratch=[pltpu.SemaphoreType.DMA((3,))],
        moved=4 * (key.size + latent.size),
    )(lengths, lse, weights, query, key, latent)


def join_kernel(stats_ref, own_ref, *refs):
    parts, (mass_ref, out_ref) = refs[:-2], refs[-2:]
    mass = own_ref[...]
    for part in parts:
        mass = mass + part[...].astype(jnp.float32)
    mass_ref[...] = mass
    column = lax.broadcasted_iota(jnp.int32, out_ref.shape, 1)
    out_ref[...] = jnp.where(column == 2, jnp.sum(mass, axis=1, keepdims=True), stats_ref[...])


def joined_mass(stats, own, parts):
    return local_call(
        join_kernel,
        [f32(own.shape), f32(stats.shape)],
        "join_mass",
        in_specs=[whole()] * (2 + len(parts)),
        out_specs=[whole()] * 2,
        moved=8 * own.size,
    )(stats, own, *parts)


def pair_stats_kernel(own_ref, got_ref, out_ref):
    own, got = own_ref[...], got_ref[...]
    top = jnp.maximum(own[:, 0:1], got[:, 0:1])
    shares = own[:, 1:2] * jnp.exp(own[:, 0:1] - top) + got[:, 1:2] * jnp.exp(got[:, 0:1] - top)
    column = lax.broadcasted_iota(jnp.int32, out_ref.shape, 1)
    out_ref[...] = jnp.where(column == 0, top, jnp.where(column == 1, shares, own + got))


def pair_stats(own, got):
    return local_call(
        pair_stats_kernel, f32(own.shape), "pair_stats", in_specs=[whole()] * 2, out_specs=whole(), moved=8 * own.size
    )(own, got)


def back_kernel(sources, length_ref, mass_ref, logits_ref, turned_ref, key_ref, masked_ref, *refs):
    stats = [ref[...] for ref in refs[:sources]]
    partners = len(refs) - sources - 4
    key_outs = refs[sources : sources + partners]
    keep_ref, send_ref, slope_ref, grad_ref = refs[sources + partners :]
    rows, key_count = mass_ref.shape
    width, flat = turned_ref.shape
    heads = flat // rows
    tile = math.gcd(key_count, 256)
    _, core, group = place()
    top = functools.reduce(jnp.maximum, [s[:, 0:1] for s in stats])
    shares = sum(s[:, 1:2] * jnp.exp(s[:, 0:1] - top) for s in stats)
    total = sum(s[:, 2:3] for s in stats)
    visible = visible_tile(length_ref, group, rows, 0, key_count, key_count)
    weights_exp = jnp.where(visible, jnp.exp(logits_ref[...] - top), 0.0)
    slope_ref[...] = loss_scale * (weights_exp / shares - mass_ref[...] / total)
    query_grad = jnp.zeros((flat, width), jnp.float32)
    for first in range(0, key_count, tile):
        keys = key_ref[first : first + tile, :]
        slopes = jnp.broadcast_to(slope_ref[:, first : first + tile][:, None, :], (rows, heads, tile))
        terms = (slopes.reshape(flat, tile) * masked_ref[:, first : first + tile]).astype(jnp.bfloat16)
        query_grad = query_grad + jnp.dot(terms, keys, preferred_element_type=jnp.float32)
        key_grad = jnp.dot(turned_ref[...], terms, preferred_element_type=jnp.float32)
        grad_ref[first : first + tile, :] = key_grad.T
    block = key_count // partners
    for e, out_ref in enumerate(key_outs):
        out_ref[...] = rows_at(grad_ref, group ^ e, block).astype(out_ref.dtype)
    planes = keep_ref.shape[0]
    part = heads // (2 * planes)
    split = query_grad.reshape(rows, planes, 2, part, width)
    first_core = core == 0
    for plane in range(planes):
        low, high = split[:, plane, 0], split[:, plane, 1]
        keep_ref[plane] = jnp.where(first_core, low, high).reshape(rows * part, width)
        send_ref[plane] = jnp.where(first_core, high, low).reshape(rows * part, width).astype(jnp.bfloat16)


def back_pass(lengths, mass, logits, turned, index_key, masked, stats, partners, planes):
    rows, key_count = mass.shape
    width, flat = turned.shape
    part = flat // (2 * planes)
    return local_call(
        functools.partial(back_kernel, len(stats)),
        [f32((key_count // partners, width))]
        + [bf16((key_count // partners, width))] * (partners - 1)
        + [f32((planes, part, width)), bf16((planes, part, width))],
        "index_back",
        in_specs=[whole()] * (6 + len(stats)),
        out_specs=[whole()] * (partners + 2),
        scratch=[pltpu.VMEM((rows, key_count), jnp.float32), pltpu.VMEM((key_count, width), jnp.float32)],
        flops=6 * flat * width * key_count,
        moved=8 * key_count * width,
    )(lengths, mass, logits, turned, index_key, masked, *stats)


def pair_kernel(keep_ref, got_ref, *outs):
    own_plane, _, _ = place()
    for e, out_ref in enumerate(outs):
        plane = own_plane ^ e
        out_ref[...] = (keep_ref[plane] + got_ref[plane].astype(jnp.float32)).astype(out_ref.dtype)


def pair_sums(keep, got):
    planes, part, width = keep.shape
    return local_call(
        pair_kernel,
        [f32((part, width))] + [bf16((part, width))] * (planes - 1),
        "pair_sums",
        in_specs=[whole(), whole()],
        out_specs=[whole()] * planes,
        moved=8 * keep.size,
    )(keep, got)


def last_kernel(key_parts, *refs):
    query_out, key_out = refs[-2:]
    key_refs, query_refs = refs[:key_parts], refs[key_parts:-2]
    key_out[...] = sum(ref[...].astype(jnp.float32) for ref in key_refs)
    query_out[...] = sum(ref[...].astype(jnp.float32) for ref in query_refs).reshape(query_out.shape)


def last_sums(key_parts, query_parts, query_shape):
    return local_call(
        functools.partial(last_kernel, len(key_parts)),
        [f32(query_shape), f32(key_parts[0].shape)],
        "last_sums",
        in_specs=[whole()] * (len(key_parts) + len(query_parts)),
        out_specs=[whole()] * 2,
        moved=8 * key_parts[0].size,
    )(*key_parts, *query_parts)


def after(array, *others):
    return lax.optimization_barrier((array, *others))[0]


def block_device(main_query, latent_keys, head_lse, lengths, index_query, index_key, index_weight):
    contexts = lax.axis_size("context")
    planes = contexts // 2
    partners = lax.axis_size("heads")
    context = lax.axis_index("context")
    rows, heads, _ = main_query.shape
    own_rows, index_heads, width = index_query.shape
    key_count = latent_keys.shape[0]
    flat = own_rows * index_heads

    def planes_move(array, pairs):
        return lax.ppermute(array, "context", [(2 * a + k, 2 * b + k) for a, b in pairs for k in (0, 1)])

    def context_flip(array, e):
        return lax.ppermute(array, "context", [(c, c ^ e) for c in range(contexts)])

    def heads_flip(array, e):
        return lax.ppermute(array, "heads", [(h, h ^ e) for h in range(partners)])

    def mass_of(packs, *rest):
        return chunk_mass(lengths, packs, lse, keys, *rest[:2], rows, heads, rest[2])

    pack = packed_queries(main_query)
    across = planes_move(pack, [(1, 2), (2, 1), (0, 3), (3, 0)])
    near = planes_move(pack, [(0, 1), (1, 0), (2, 3), (3, 2)])
    own_pair = context_flip(pack, 1)
    lengths, lse, weight_wide, query, turned, index_key, keys = load_inputs(
        lengths, head_lse.T, index_weight, index_query, index_key, after(latent_keys, pack).T
    )
    logits, masked, stats = index_logits(lengths, query.reshape(flat, width), index_key, weight_wide, own_rows)
    own_mass = mass_of([pack, after(own_pair, stats)], 0, (0, 1), "mass_own")
    across = after(across, own_mass)
    far = planes_move(picked(pack, across), [(0, 2), (3, 1), (1, 0), (2, 3)])
    near = after(near, own_mass)
    near_mass = mass_of([near, context_flip(near, 1)], 1, (0, 1), "mass_near")
    across_mass = mass_of([across, context_flip(across, 1)], 3, (0, 1), "mass_across")
    far = after(far, near_mass, across_mass)
    far_pair = context_flip(far, 1)
    far_mass = mass_of([far], 2, (0,), "mass_far")
    shared = shared_mass(
        lengths, far_pair, lse, own_mass, near_mass, across_mass, far_mass, keys, rows, heads, partners
    )
    mass, stats = joined_mass(stats, shared[0], [heads_flip(shared[e], e) for e in range(1, partners)])
    stats = pair_stats(stats, context_flip(stats, 1))
    every = [stats] + [context_flip(stats, 2 * e) for e in range(1, planes)]
    *key_grads, keep, send = back_pass(
        lengths, mass, logits, turned, index_key, masked, every, partners, planes
    )
    got = context_flip(send, 1)
    key_parts = [key_grads[0]] + [heads_flip(key_grads[e], e) for e in range(1, partners)]
    sums = pair_sums(keep, got)
    query_parts = [sums[0]] + [context_flip(sums[e], 2 * e) for e in range(1, planes)]
    return last_sums(key_parts, query_parts, (own_rows, index_heads // contexts, width))


def fits(mesh):
    return mesh.shape["context"] == 8 and mesh.shape["heads"] == 4


def solution(mesh):
    placed = (
        P("context", "heads", None),
        P("context", None),
        P(None, "heads"),
        P(),
        P("heads", None, None),
        P("context", None),
        P("heads", None),
    )
    return jax.shard_map(
        block_device if fits(mesh) else general_on_device,
        mesh=mesh,
        in_specs=placed,
        out_specs=(P("heads", "context", None), P(("context", "heads"), None)),
        check_vma=False,
    )
```

```python
import functools
import math

import jax
import jax.numpy as jnp
from jax import lax
from jax.experimental import pallas as pl
from jax.experimental.pallas import tpu as pltpu
from jax.sharding import PartitionSpec as P

main_scale = 192.0 ** (-0.5)
loss_scale = 64.0
masked_low = -1e30
log2_e = math.log2(math.e)
lanes = 128
vmem_bytes = 20 * 1024 * 1024
most_bytes = 60 * 1024 * 1024
load_bytes = 58 * 1024 * 1024

def joined(part, axis, combine):
    gathered = jax.tree.map(lambda a: lax.all_gather(a, axis), part)

    def take(source):
        return jax.tree.map(lambda a: lax.dynamic_index_in_dim(a, source, 0, False), gathered)

    return lax.fori_loop(
        1, lax.axis_size(axis), lambda source, state: combine(state, take(source)), take(0)
    )


def head_mass(queries, lse_rows, len_rows, latent, first_key):
    row_count = queries.shape[0]
    block_rows = math.gcd(row_count, 64)
    steps_count = row_count // block_rows
    key_pos = first_key + jnp.arange(latent.shape[0], dtype=jnp.int32)

    def one_block(inputs):
        query_block, lse_block, len_block = inputs
        scores = (
            jnp.einsum("rhd,sd->rhs", query_block, latent, preferred_element_type=jnp.float32)
            * main_scale
        )
        summed = jnp.sum(jnp.exp(scores - lse_block[:, :, None]), axis=1)
        return jnp.where(key_pos[None, :] < len_block[:, None], summed, 0.0)

    stacked = lax.map(
        one_block,
        (
            queries.reshape((steps_count, block_rows) + queries.shape[1:]),
            lse_rows.reshape(steps_count, block_rows, lse_rows.shape[1]),
            len_rows.reshape(steps_count, block_rows),
        ),
    )
    return stacked.reshape(row_count, latent.shape[0])


def general_on_device(main_query, latent_keys, head_lse, lengths, index_query, index_key, index_weight):
    key_count = latent_keys.shape[0]
    first_key = lax.axis_index("context") * key_count
    own_rows = index_query.shape[0]
    row_first = lax.axis_index("heads") * own_rows
    partial_mass = head_mass(
        lax.all_gather(main_query, "context", axis=0, tiled=True),
        head_lse,
        lengths,
        latent_keys,
        first_key,
    )
    summed_mass = lax.psum(partial_mass, "heads")
    row_mass = lax.dynamic_slice_in_dim(summed_mass, row_first, own_rows, 0)
    own_len = lax.dynamic_slice_in_dim(lengths, row_first, own_rows, 0)
    visible = (first_key + jnp.arange(key_count, dtype=jnp.int32))[None, :] < own_len[:, None]
    heads_count = index_query.shape[1]
    width = index_query.shape[2]
    index_scale = width ** (-0.5)
    flat_query = index_query.reshape(own_rows * heads_count, width)
    block_keys = math.gcd(key_count, 512)
    block_total = key_count // block_keys
    key_blocks = index_key.reshape(block_total, block_keys, width)

    def block_dots(key_block):
        products = lax.dot_general(
            flat_query, key_block, (((1,), (1,)), ((), ())), preferred_element_type=jnp.float32
        )
        return products.reshape(own_rows, heads_count, key_block.shape[0])

    def block_logits(key_block):
        return (
            jnp.einsum(
                "tj,tjs->ts",
                index_weight,
                jax.nn.relu(block_dots(key_block)),
                precision=lax.Precision.HIGHEST,
            )
            * index_scale
        )

    logits = jnp.moveaxis(lax.map(block_logits, key_blocks), 0, 1).reshape(own_rows, key_count)
    local_top = jnp.max(jnp.where(visible, logits, masked_low), axis=1)
    mass_local = jnp.sum(row_mass, axis=1)
    local_exp = jnp.where(visible, jnp.exp(logits - local_top[:, None]), 0.0)

    def combine(first, second):
        highest = jnp.maximum(first[0], second[0])
        merged = first[1] * jnp.exp(first[0] - highest) + second[1] * jnp.exp(second[0] - highest)
        return (highest, merged, first[2] + second[2])

    top, share_sum, mass_total = joined(
        (local_top, jnp.sum(local_exp, axis=1), mass_local), "context", combine
    )
    weights_exp = jnp.where(visible, jnp.exp(logits - top[:, None]), 0.0)
    probability = weights_exp / share_sum[:, None]
    target = row_mass / mass_total[:, None]
    slopes = loss_scale * (probability - target)
    slope_blocks = slopes.reshape(own_rows, block_total, block_keys).transpose(1, 0, 2)

    def back_step(query_grad, inputs):
        key_block, slope_block = inputs
        products = block_dots(key_block)
        terms = jnp.where(
            products > 0, slope_block[:, None, :] * index_weight[:, :, None] * index_scale, 0.0
        )
        terms = terms.astype(jnp.bfloat16).reshape(own_rows * heads_count, key_block.shape[0])
        query_grad = query_grad + jnp.dot(terms, key_block, preferred_element_type=jnp.float32)
        key_grad = lax.dot_general(
            terms, flat_query, (((0,), (0,)), ((), ())), preferred_element_type=jnp.float32
        )
        return (query_grad, key_grad)

    start_grad = jnp.zeros((own_rows * heads_count, width), jnp.float32)
    query_grad, key_grads = lax.scan(back_step, start_grad, (key_blocks, slope_blocks))
    query_grad = query_grad.reshape(own_rows, heads_count, width)
    key_grad = key_grads.reshape(key_count, width)
    out_query = lax.psum_scatter(query_grad, "context", scatter_dimension=1, tiled=True)
    out_key = lax.psum_scatter(key_grad, "heads", scatter_dimension=0, tiled=True)
    return (out_query, out_key)


def local_call(kernel, out_shape, name, grid=None, in_specs=None, out_specs=None, scratch=(), flops=1, moved=0, room=vmem_bytes):
    settings = dict(
        out_shape=out_shape,
        scratch_shapes=list(scratch),
        name=name,
        compiler_params=pltpu.CompilerParams(vmem_limit_bytes=room),
        cost_estimate=pl.CostEstimate(flops=flops, bytes_accessed=1, transcendentals=0),
    )
    if grid is not None:
        settings["grid"] = grid
    if in_specs is not None:
        settings["in_specs"] = in_specs
    if out_specs is not None:
        settings["out_specs"] = out_specs
    return pl.pallas_call(kernel, **settings)


def whole():
    return pl.BlockSpec(memory_space=pltpu.VMEM)


def scalars():
    return pl.BlockSpec(memory_space=pltpu.SMEM)


def fixed(shape):
    return pl.BlockSpec(shape, lambda step: (0,) * len(shape))


def f32(shape):
    return jax.ShapeDtypeStruct(shape, jnp.float32)


def bf16(shape):
    return jax.ShapeDtypeStruct(shape, jnp.bfloat16)


def place():
    context = lax.axis_index("context")
    return context >> 1, context & 1, lax.axis_index("heads")


def hbm():
    return pl.BlockSpec(memory_space=pltpu.HBM)


def pack_kernel(query_ref, out_ref):
    rows, heads, width = query_ref.shape
    total = rows * heads
    columns = width // lanes
    stacked = jnp.swapaxes(query_ref[...].astype(jnp.float32), 0, 1).reshape(total, width)
    for i in range(columns):
        out_ref[i * total : (i + 1) * total, :] = stacked[:, i * lanes : (i + 1) * lanes].astype(jnp.bfloat16)
    rest = stacked[:, columns * lanes :]
    out_ref[columns * total :, :] = jnp.concatenate([rest[: total // 2], rest[total // 2 :]], axis=1).astype(
        jnp.bfloat16
    )


def packed_queries(queries):
    rows, heads, width = queries.shape
    return local_call(
        pack_kernel,
        bf16((rows * heads * width // lanes, lanes)),
        "pack_queries",
        in_specs=[whole()],
        out_specs=whole(),
        flops=30_000_000_000,
    )(queries)


def pick_kernel(ends_ref, inner_ref, *outs):
    plane, _, _ = place()
    inner = (plane == 1) | (plane == 2)

    def fill(source_ref):
        for i, out_ref in enumerate(outs):
            rows = out_ref.shape[0]
            out_ref[...] = source_ref[i * rows : (i + 1) * rows, :]

    @pl.when(inner)
    def _():
        fill(inner_ref)

    @pl.when(jnp.logical_not(inner))
    def _():
        fill(ends_ref)


def picked(ends, inner, parts):
    rows, width = ends.shape
    return local_call(
        pick_kernel,
        [bf16((rows // parts, width))] * parts,
        "pick_queries",
        in_specs=[whole()] * 2,
        out_specs=[whole()] * parts,
        moved=4 * ends.size,
    )(ends, inner)


def parts_kernel(source_ref, *outs):
    first = 0
    for out_ref in outs:
        rows = out_ref.shape[0]
        out_ref[...] = source_ref[first : first + rows, :]
        first += rows


def in_parts(source):
    rows, width = source.shape
    large = rows * 5 // 8 // 16 * 16
    return local_call(
        parts_kernel,
        [bf16((large, width)), bf16((rows - large, width))],
        "query_parts",
        in_specs=[whole()],
        out_specs=[whole()] * 2,
    )(source)


def unpack(packed, wide_ref, slot, total, width):
    columns = width // lanes
    half = total // 2
    for i in range(columns):
        wide_ref[slot * total : (slot + 1) * total, i * lanes : (i + 1) * lanes] = packed[
            i * total : (i + 1) * total, :
        ]
    rest = packed[columns * total :, :]
    wide_ref[slot * total : slot * total + half, columns * lanes :] = rest[:, : lanes // 2]
    wide_ref[slot * total + half : (slot + 1) * total, columns * lanes :] = rest[:, lanes // 2 :]


def widened(column, width):
    return jnp.concatenate([column] * (width // lanes), axis=1)


def shard_mass(length_ref, wide_ref, slot, lse, key_ref, context, rows, heads, first, tile):
    total = rows * heads
    scores = jnp.dot(
        wide_ref[slot * total : (slot + 1) * total, :],
        key_ref[:, first : first + tile],
        preferred_element_type=jnp.float32,
    )
    summed = jnp.zeros((rows, tile), jnp.float32)
    for h in range(heads):
        summed = summed + jnp.exp2(scores[h * rows : (h + 1) * rows] * (main_scale * log2_e) - lse[:, h : h + 1])
    visible = visible_tile(length_ref, context, rows, first, tile, key_ref.shape[1])
    return jnp.where(visible, summed, 0.0)


def rows_at(ref, index, rows):
    return ref[pl.ds(pl.multiple_of(index * rows, rows), rows), :]


def visible_tile(length_ref, block, rows, first, width, key_count):
    positions = lax.axis_index("context") * key_count + first + lax.broadcasted_iota(jnp.int32, (rows, width), 1)
    return positions < widened(rows_at(length_ref, block, rows), width)


def mass_kernel(flip, places, rows, heads, length_ref, *refs):
    count = len(places)
    parts = (len(refs) - 4) // count
    packs = [refs[n * parts : (n + 1) * parts] for n in range(count)]
    lse_ref, key_ref, out_ref, wide_ref = refs[count * parts :]
    width, key_count = key_ref.shape
    tile = math.gcd(key_count, 512)
    total = rows * heads
    own_plane, own_core, _ = place()
    plane = own_plane ^ flip
    for n, other in enumerate(places):
        unpack(jnp.concatenate([ref[...] for ref in packs[n]], axis=0), wide_ref, n, total, width)
        core = own_core ^ other
        context = 2 * plane + core
        lse = rows_at(lse_ref, context, rows)
        for first in range(0, key_count, tile):
            mass = shard_mass(length_ref, wide_ref, n, lse, key_ref, context, rows, heads, first, tile)
            if count == 1:
                out_ref[:, first : first + tile] = mass
            else:
                out_ref[pl.ds(pl.multiple_of(core * rows, rows), rows), first : first + tile] = mass


def chunk_mass(lengths, packs, lse, keys, flip, places, rows, heads, name, flops=1):
    width, key_count = keys.shape
    count = len(places)
    total = rows * heads
    return local_call(
        functools.partial(mass_kernel, flip, places, rows, heads),
        f32((count * rows, key_count)),
        name,
        in_specs=[whole()] * (len(packs) + 3),
        out_specs=whole(),
        scratch=[pltpu.VMEM((count * total, width), jnp.bfloat16)],
        flops=flops,
    )(lengths, *packs, lse, keys)


def share_kernel(rows, heads, length_ref, pack_ref, lse_ref, own_ref, near_ref, far_ref, half_ref, key_ref, *refs):
    outs = refs[:-2]
    wide_ref, chunks_ref = refs[-2:]
    width, key_count = key_ref.shape
    tile = math.gcd(key_count, 512)
    total = rows * heads
    unpack(pack_ref[...], wide_ref, 0, total, width)
    plane, core, group = place()
    other = 1 - core
    context = 2 * (plane ^ 2) + other
    lse = rows_at(lse_ref, context, rows)
    chunks_ref[0] = own_ref[...]
    chunks_ref[1] = near_ref[...]
    chunks_ref[3] = far_ref[...]
    chunks_ref[2, pl.ds(pl.multiple_of(core * rows, rows), rows), :] = half_ref[...]
    for first in range(0, key_count, tile):
        chunks_ref[2, pl.ds(pl.multiple_of(other * rows, rows), rows), first : first + tile] = shard_mass(
            length_ref, wide_ref, 0, lse, key_ref, context, rows, heads, first, tile
        )
    for e, out_ref in enumerate(outs):
        out_ref[...] = chunks_ref[plane ^ group ^ e].astype(out_ref.dtype)


def shared_mass(lengths, pack, lse, own, near, far, half, keys, rows, heads, partners):
    width, key_count = keys.shape
    total = rows * heads
    both = 2 * rows
    return local_call(
        functools.partial(share_kernel, rows, heads),
        [f32((both, key_count))] + [bf16((both, key_count))] * (partners - 1),
        "mass_and_share",
        in_specs=[whole()] * 8,
        out_specs=[whole()] * partners,
        scratch=[
            pltpu.VMEM((total, width), jnp.bfloat16),
            pltpu.VMEM((4, both, key_count), jnp.float32),
        ],
        moved=2 * keys.size,
    )(lengths, pack, lse, own, near, far, half, keys)


def logits_kernel(length_ref, query_ref, key_ref, weight_ref, logits_ref, masked_ref, stats_ref):
    rows, key_count = logits_ref.shape
    heads = query_ref.shape[0] // rows
    tile = math.gcd(key_count, 256)
    group = lax.axis_index("heads")
    best = jnp.full((rows, 1), masked_low, jnp.float32)
    weights = widened(weight_ref[...], tile)
    for first in range(0, key_count, tile):
        dots = lax.dot_general(
            query_ref[...], key_ref[first : first + tile, :], (((1,), (1,)), ((), ())),
            preferred_element_type=jnp.float32,
        )
        masked = jnp.where(dots > 0, weights, 0.0)
        masked_ref[:, first : first + tile] = masked
        logits = jnp.sum((dots * masked).reshape(rows, heads, tile), axis=1)
        logits_ref[:, first : first + tile] = logits
        visible = visible_tile(length_ref, group, rows, first, tile, key_count)
        best = jnp.maximum(best, jnp.max(jnp.where(visible, logits, masked_low), axis=1, keepdims=True))
    visible = visible_tile(length_ref, group, rows, 0, key_count, key_count)
    total = jnp.sum(jnp.where(visible, jnp.exp(logits_ref[...] - best), 0.0), axis=1, keepdims=True)
    column = lax.broadcasted_iota(jnp.int32, (rows, lanes), 1)
    stats_ref[...] = jnp.where(column == 0, best, total)


def index_logits(lengths, flat_query, index_key, weight_wide, rows):
    key_count = index_key.shape[0]
    flat = flat_query.shape[0]
    return local_call(
        logits_kernel,
        [f32((rows, key_count)), f32((flat, key_count)), f32((rows, lanes))],
        "index_logits",
        in_specs=[whole()] * 4,
        out_specs=[whole()] * 3,
        moved=2 * index_key.size,
    )(lengths, flat_query, index_key, weight_wide)


def load_kernel(
    length_ref, lse_ref, weight_ref, query_hbm, key_hbm, latent_hbm,
    length_out, lse_out, weight_out, query_out, turned_out, key_out, latent_out, semaphores,
):
    copies = [
        pltpu.make_async_copy(source, target, semaphores.at[i])
        for i, (source, target) in enumerate(
            [(query_hbm, query_out), (key_hbm, key_out), (latent_hbm, latent_out)]
        )
    ]
    for copy in copies:
        copy.start()
    total = length_out.shape[0]
    spread = lax.broadcasted_iota(jnp.int32, (8, lanes), 0)
    for first in range(0, total, 8):
        column = jnp.zeros((8, lanes), jnp.int32)
        for i in range(8):
            column = jnp.where(spread == i, length_ref[first + i], column)
        length_out[first : first + 8, :] = column
    lse_out[...] = lse_ref[...].T * log2_e
    rows, heads = weight_ref.shape
    width = key_out.shape[1]
    weights = weight_ref[...].T * width ** (-0.5)
    for t in range(rows):
        weight_out[t * heads : (t + 1) * heads, :] = jnp.broadcast_to(weights[:, t : t + 1], (heads, lanes))
    copies[0].wait()
    turned_out[...] = query_out[...].reshape(rows * heads, width).astype(jnp.float32).T.astype(jnp.bfloat16)
    copies[1].wait()
    copies[2].wait()


def load_inputs(lengths, lse, weights, query, key, latent):
    rows, heads, width = query.shape
    flat = rows * heads
    return local_call(
        load_kernel,
        [
            jax.ShapeDtypeStruct((lengths.shape[0], lanes), jnp.int32),
            f32(lse.shape[::-1]),
            f32((flat, lanes)),
            bf16(query.shape),
            bf16((width, flat)),
            bf16(key.shape),
            bf16(latent.shape),
        ],
        "load_inputs",
        in_specs=[scalars(), whole(), whole(), hbm(), hbm(), hbm()],
        out_specs=[whole()] * 7,
        scratch=[pltpu.SemaphoreType.DMA((3,))],
        moved=4 * (key.size + latent.size),
    )(lengths, lse, weights, query, key, latent)


def join_kernel(stats_ref, own_ref, *refs):
    parts, (mass_ref, out_ref) = refs[:-2], refs[-2:]
    mass = own_ref[...]
    for part in parts:
        mass = mass + part[...].astype(jnp.float32)
    mass_ref[...] = mass
    column = lax.broadcasted_iota(jnp.int32, out_ref.shape, 1)
    out_ref[...] = jnp.where(column == 2, jnp.sum(mass, axis=1, keepdims=True), stats_ref[...])


def joined_mass(stats, own, parts):
    return local_call(
        join_kernel,
        [f32(own.shape), f32(stats.shape)],
        "join_mass",
        in_specs=[whole()] * (2 + len(parts)),
        out_specs=[whole()] * 2,
        moved=8 * own.size,
    )(stats, own, *parts)


def pair_stats_kernel(own_ref, got_ref, out_ref):
    own, got = own_ref[...], got_ref[...]
    top = jnp.maximum(own[:, 0:1], got[:, 0:1])
    shares = own[:, 1:2] * jnp.exp(own[:, 0:1] - top) + got[:, 1:2] * jnp.exp(got[:, 0:1] - top)
    column = lax.broadcasted_iota(jnp.int32, out_ref.shape, 1)
    out_ref[...] = jnp.where(column == 0, top, jnp.where(column == 1, shares, own + got))


def pair_stats(own, got):
    return local_call(
        pair_stats_kernel, f32(own.shape), "pair_stats", in_specs=[whole()] * 2, out_specs=whole(), moved=8 * own.size
    )(own, got)


def back_kernel(sources, length_ref, mass_ref, logits_ref, turned_ref, key_ref, masked_ref, *refs):
    stats = [ref[...] for ref in refs[:sources]]
    partners = len(refs) - sources - 4
    key_outs = refs[sources : sources + partners]
    keep_ref, send_ref, slope_ref, grad_ref = refs[sources + partners :]
    rows, key_count = mass_ref.shape
    width, flat = turned_ref.shape
    heads = flat // rows
    tile = math.gcd(key_count, 256)
    _, core, group = place()
    top = functools.reduce(jnp.maximum, [s[:, 0:1] for s in stats])
    shares = sum(s[:, 1:2] * jnp.exp(s[:, 0:1] - top) for s in stats)
    total = sum(s[:, 2:3] for s in stats)
    visible = visible_tile(length_ref, group, rows, 0, key_count, key_count)
    weights_exp = jnp.where(visible, jnp.exp(logits_ref[...] - top), 0.0)
    slope_ref[...] = loss_scale * (weights_exp / shares - mass_ref[...] / total)
    query_grad = jnp.zeros((flat, width), jnp.float32)
    for first in range(0, key_count, tile):
        keys = key_ref[first : first + tile, :]
        slopes = jnp.broadcast_to(slope_ref[:, first : first + tile][:, None, :], (rows, heads, tile))
        terms = (slopes.reshape(flat, tile) * masked_ref[:, first : first + tile]).astype(jnp.bfloat16)
        query_grad = query_grad + jnp.dot(terms, keys, preferred_element_type=jnp.float32)
        key_grad = jnp.dot(turned_ref[...], terms, preferred_element_type=jnp.float32)
        grad_ref[first : first + tile, :] = key_grad.T
    block = key_count // partners
    for e, out_ref in enumerate(key_outs):
        out_ref[...] = rows_at(grad_ref, group ^ e, block).astype(out_ref.dtype)
    planes = keep_ref.shape[0]
    part = heads // (2 * planes)
    split = query_grad.reshape(rows, planes, 2, part, width)
    first_core = core == 0
    for plane in range(planes):
        low, high = split[:, plane, 0], split[:, plane, 1]
        keep_ref[plane] = jnp.where(first_core, low, high).reshape(rows * part, width)
        send_ref[plane] = jnp.where(first_core, high, low).reshape(rows * part, width).astype(jnp.bfloat16)


def back_pass(lengths, mass, logits, turned, index_key, masked, stats, partners, planes):
    rows, key_count = mass.shape
    width, flat = turned.shape
    part = flat // (2 * planes)
    return local_call(
        functools.partial(back_kernel, len(stats)),
        [f32((key_count // partners, width))]
        + [bf16((key_count // partners, width))] * (partners - 1)
        + [f32((planes, part, width)), bf16((planes, part, width))],
        "index_back",
        in_specs=[whole()] * (6 + len(stats)),
        out_specs=[whole()] * (partners + 2),
        scratch=[pltpu.VMEM((rows, key_count), jnp.float32), pltpu.VMEM((key_count, width), jnp.float32)],
        moved=8 * key_count * width,
    )(lengths, mass, logits, turned, index_key, masked, *stats)


def pair_kernel(keep_ref, got_ref, *outs):
    own_plane, _, _ = place()
    for e, out_ref in enumerate(outs):
        plane = own_plane ^ e
        out_ref[...] = (keep_ref[plane] + got_ref[plane].astype(jnp.float32)).astype(out_ref.dtype)


def pair_sums(keep, got):
    planes, part, width = keep.shape
    return local_call(
        pair_kernel,
        [f32((part, width))] + [bf16((part, width))] * (planes - 1),
        "pair_sums",
        in_specs=[whole(), whole()],
        out_specs=[whole()] * planes,
        moved=8 * keep.size,
    )(keep, got)


def last_kernel(key_parts, *refs):
    query_out, key_out = refs[-2:]
    key_refs, query_refs = refs[:key_parts], refs[key_parts:-2]
    key_out[...] = sum(ref[...].astype(jnp.float32) for ref in key_refs)
    query_out[...] = sum(ref[...].astype(jnp.float32) for ref in query_refs).reshape(query_out.shape)


def last_sums(key_parts, query_parts, query_shape):
    return local_call(
        functools.partial(last_kernel, len(key_parts)),
        [f32(query_shape), f32(key_parts[0].shape)],
        "last_sums",
        in_specs=[whole()] * (len(key_parts) + len(query_parts)),
        out_specs=[whole()] * 2,
        moved=8 * key_parts[0].size,
    )(*key_parts, *query_parts)


def after(array, *others):
    return lax.optimization_barrier((array, *others))[0]


def block_device(main_query, latent_keys, head_lse, lengths, index_query, index_key, index_weight):
    contexts = lax.axis_size("context")
    planes = contexts // 2
    partners = lax.axis_size("heads")
    context = lax.axis_index("context")
    rows, heads, _ = main_query.shape
    own_rows, index_heads, width = index_query.shape
    key_count = latent_keys.shape[0]
    flat = own_rows * index_heads

    def planes_move(array, pairs):
        return lax.ppermute(array, "context", [(2 * a + k, 2 * b + k) for a, b in pairs for k in (0, 1)])

    def context_flip(array, e):
        return lax.ppermute(array, "context", [(c, c ^ e) for c in range(contexts)])

    def heads_flip(array, e):
        return lax.ppermute(array, "heads", [(h, h ^ e) for h in range(partners)])

    def mass_of(packs, *rest):
        return chunk_mass(lengths, packs, lse, keys, *rest[:2], rows, heads, *rest[2:])

    pack = packed_queries(main_query)
    near = planes_move(pack, [(0, 1), (1, 0), (2, 3), (3, 2)])
    inner = planes_move(pack, [(1, 2), (2, 1), (0, 0), (3, 3)])
    ends = planes_move(pack, [(0, 3), (3, 0)])
    own_pair = context_flip(pack, 1)
    lengths, lse, weight_wide, query, turned, index_key, keys = load_inputs(
        lengths, head_lse.T, index_weight, index_query, index_key, after(latent_keys, pack).T
    )
    inner = after(inner, lse)
    far = planes_move(inner, [(0, 2), (3, 1), (1, 0), (2, 3)])
    logits, masked, stats = index_logits(lengths, query.reshape(flat, width), index_key, weight_wide, own_rows)
    own_mass = mass_of([pack, own_pair], 0, (0, 1), "mass_own")
    across = picked(after(ends, own_mass, stats), inner, 2)
    near = in_parts(after(near, stats))
    near_mass = mass_of([*near, *(context_flip(a, 1) for a in near)], 1, (0, 1), "mass_near", 500_000_000)
    across_mass = mass_of([*across, *(context_flip(a, 1) for a in across)], 3, (0, 1), "mass_across")
    far = after(far, near_mass, across_mass)
    far_pair = context_flip(far, 1)
    far_mass = mass_of([far], 2, (0,), "mass_far")
    shared = shared_mass(
        lengths, far_pair, lse, own_mass, near_mass, across_mass, far_mass, keys, rows, heads, partners
    )
    mass, stats = joined_mass(stats, shared[0], [heads_flip(shared[e], e) for e in reversed(range(1, partners))])
    stats = pair_stats(stats, context_flip(stats, 1))
    every = [stats] + [context_flip(stats, 2 * e) for e in reversed(range(1, planes))]
    *key_grads, keep, send = back_pass(
        lengths, mass, logits, turned, index_key, masked, every, partners, planes
    )
    got = context_flip(send, 1)
    key_parts = [key_grads[0]] + [heads_flip(key_grads[e], e) for e in reversed(range(1, partners))]
    sums = pair_sums(keep, got)
    query_parts = [sums[0]] + [context_flip(sums[e], 2 * e) for e in reversed(range(1, planes))]
    return last_sums(key_parts, query_parts, (own_rows, index_heads // contexts, width))


def fits(mesh):
    return mesh.shape["context"] == 8 and mesh.shape["heads"] == 4


def solution(mesh):
    placed = (
        P("context", "heads", None),
        P("context", None),
        P(None, "heads"),
        P(),
        P("heads", None, None),
        P("context", None),
        P("heads", None),
    )
    return jax.shard_map(
        block_device if fits(mesh) else general_on_device,
        mesh=mesh,
        in_specs=placed,
        out_specs=(P("heads", "context", None), P(("context", "heads"), None)),
        check_vma=False,
    )
```

```python
import functools
import math

import jax
import jax.numpy as jnp
from jax import lax
from jax.experimental import pallas as pl
from jax.experimental.pallas import tpu as pltpu
from jax.sharding import PartitionSpec as P

main_scale = 192.0 ** (-0.5)
loss_scale = 64.0
masked_low = -1e30
log2_e = math.log2(math.e)
lanes = 128
vmem_bytes = 20 * 1024 * 1024
most_bytes = 60 * 1024 * 1024
load_bytes = 58 * 1024 * 1024

def joined(part, axis, combine):
    gathered = jax.tree.map(lambda a: lax.all_gather(a, axis), part)

    def take(source):
        return jax.tree.map(lambda a: lax.dynamic_index_in_dim(a, source, 0, False), gathered)

    return lax.fori_loop(
        1, lax.axis_size(axis), lambda source, state: combine(state, take(source)), take(0)
    )


def head_mass(queries, lse_rows, len_rows, latent, first_key):
    row_count = queries.shape[0]
    block_rows = math.gcd(row_count, 64)
    steps_count = row_count // block_rows
    key_pos = first_key + jnp.arange(latent.shape[0], dtype=jnp.int32)

    def one_block(inputs):
        query_block, lse_block, len_block = inputs
        scores = (
            jnp.einsum("rhd,sd->rhs", query_block, latent, preferred_element_type=jnp.float32)
            * main_scale
        )
        summed = jnp.sum(jnp.exp(scores - lse_block[:, :, None]), axis=1)
        return jnp.where(key_pos[None, :] < len_block[:, None], summed, 0.0)

    stacked = lax.map(
        one_block,
        (
            queries.reshape((steps_count, block_rows) + queries.shape[1:]),
            lse_rows.reshape(steps_count, block_rows, lse_rows.shape[1]),
            len_rows.reshape(steps_count, block_rows),
        ),
    )
    return stacked.reshape(row_count, latent.shape[0])


def general_on_device(main_query, latent_keys, head_lse, lengths, index_query, index_key, index_weight):
    key_count = latent_keys.shape[0]
    first_key = lax.axis_index("context") * key_count
    own_rows = index_query.shape[0]
    row_first = lax.axis_index("heads") * own_rows
    partial_mass = head_mass(
        lax.all_gather(main_query, "context", axis=0, tiled=True),
        head_lse,
        lengths,
        latent_keys,
        first_key,
    )
    summed_mass = lax.psum(partial_mass, "heads")
    row_mass = lax.dynamic_slice_in_dim(summed_mass, row_first, own_rows, 0)
    own_len = lax.dynamic_slice_in_dim(lengths, row_first, own_rows, 0)
    visible = (first_key + jnp.arange(key_count, dtype=jnp.int32))[None, :] < own_len[:, None]
    heads_count = index_query.shape[1]
    width = index_query.shape[2]
    index_scale = width ** (-0.5)
    flat_query = index_query.reshape(own_rows * heads_count, width)
    block_keys = math.gcd(key_count, 512)
    block_total = key_count // block_keys
    key_blocks = index_key.reshape(block_total, block_keys, width)

    def block_dots(key_block):
        products = lax.dot_general(
            flat_query, key_block, (((1,), (1,)), ((), ())), preferred_element_type=jnp.float32
        )
        return products.reshape(own_rows, heads_count, key_block.shape[0])

    def block_logits(key_block):
        return (
            jnp.einsum(
                "tj,tjs->ts",
                index_weight,
                jax.nn.relu(block_dots(key_block)),
                precision=lax.Precision.HIGHEST,
            )
            * index_scale
        )

    logits = jnp.moveaxis(lax.map(block_logits, key_blocks), 0, 1).reshape(own_rows, key_count)
    local_top = jnp.max(jnp.where(visible, logits, masked_low), axis=1)
    mass_local = jnp.sum(row_mass, axis=1)
    local_exp = jnp.where(visible, jnp.exp(logits - local_top[:, None]), 0.0)

    def combine(first, second):
        highest = jnp.maximum(first[0], second[0])
        merged = first[1] * jnp.exp(first[0] - highest) + second[1] * jnp.exp(second[0] - highest)
        return (highest, merged, first[2] + second[2])

    top, share_sum, mass_total = joined(
        (local_top, jnp.sum(local_exp, axis=1), mass_local), "context", combine
    )
    weights_exp = jnp.where(visible, jnp.exp(logits - top[:, None]), 0.0)
    probability = weights_exp / share_sum[:, None]
    target = row_mass / mass_total[:, None]
    slopes = loss_scale * (probability - target)
    slope_blocks = slopes.reshape(own_rows, block_total, block_keys).transpose(1, 0, 2)

    def back_step(query_grad, inputs):
        key_block, slope_block = inputs
        products = block_dots(key_block)
        terms = jnp.where(
            products > 0, slope_block[:, None, :] * index_weight[:, :, None] * index_scale, 0.0
        )
        terms = terms.astype(jnp.bfloat16).reshape(own_rows * heads_count, key_block.shape[0])
        query_grad = query_grad + jnp.dot(terms, key_block, preferred_element_type=jnp.float32)
        key_grad = lax.dot_general(
            terms, flat_query, (((0,), (0,)), ((), ())), preferred_element_type=jnp.float32
        )
        return (query_grad, key_grad)

    start_grad = jnp.zeros((own_rows * heads_count, width), jnp.float32)
    query_grad, key_grads = lax.scan(back_step, start_grad, (key_blocks, slope_blocks))
    query_grad = query_grad.reshape(own_rows, heads_count, width)
    key_grad = key_grads.reshape(key_count, width)
    out_query = lax.psum_scatter(query_grad, "context", scatter_dimension=1, tiled=True)
    out_key = lax.psum_scatter(key_grad, "heads", scatter_dimension=0, tiled=True)
    return (out_query, out_key)


def local_call(kernel, out_shape, name, grid=None, in_specs=None, out_specs=None, scratch=(), flops=1, moved=0, room=vmem_bytes):
    settings = dict(
        out_shape=out_shape,
        scratch_shapes=list(scratch),
        name=name,
        compiler_params=pltpu.CompilerParams(vmem_limit_bytes=room),
        cost_estimate=pl.CostEstimate(flops=flops, bytes_accessed=1, transcendentals=0),
    )
    if grid is not None:
        settings["grid"] = grid
    if in_specs is not None:
        settings["in_specs"] = in_specs
    if out_specs is not None:
        settings["out_specs"] = out_specs
    return pl.pallas_call(kernel, **settings)


def whole():
    return pl.BlockSpec(memory_space=pltpu.VMEM)


def scalars():
    return pl.BlockSpec(memory_space=pltpu.SMEM)


def fixed(shape):
    return pl.BlockSpec(shape, lambda step: (0,) * len(shape))


def f32(shape):
    return jax.ShapeDtypeStruct(shape, jnp.float32)


def bf16(shape):
    return jax.ShapeDtypeStruct(shape, jnp.bfloat16)


def place():
    context = lax.axis_index("context")
    return context >> 1, context & 1, lax.axis_index("heads")


def hbm():
    return pl.BlockSpec(memory_space=pltpu.HBM)


def pack_kernel(query_ref, out_ref):
    rows, heads, width = query_ref.shape
    total = rows * heads
    columns = width // lanes
    stacked = jnp.swapaxes(query_ref[...].astype(jnp.float32), 0, 1).reshape(total, width)
    for i in range(columns):
        out_ref[i * total : (i + 1) * total, :] = stacked[:, i * lanes : (i + 1) * lanes].astype(jnp.bfloat16)
    rest = stacked[:, columns * lanes :]
    out_ref[columns * total :, :] = jnp.concatenate([rest[: total // 2], rest[total // 2 :]], axis=1).astype(
        jnp.bfloat16
    )


def packed_queries(queries):
    rows, heads, width = queries.shape
    return local_call(
        pack_kernel,
        bf16((rows * heads * width // lanes, lanes)),
        "pack_queries",
        in_specs=[whole()],
        out_specs=whole(),
        flops=30_000_000_000,
    )(queries)


def pick_kernel(ends_ref, inner_ref, *outs):
    plane, _, _ = place()
    inner = (plane == 1) | (plane == 2)

    def fill(source_ref):
        for i, out_ref in enumerate(outs):
            rows = out_ref.shape[0]
            out_ref[...] = source_ref[i * rows : (i + 1) * rows, :]

    @pl.when(inner)
    def _():
        fill(inner_ref)

    @pl.when(jnp.logical_not(inner))
    def _():
        fill(ends_ref)


def picked(ends, inner, parts):
    rows, width = ends.shape
    return local_call(
        pick_kernel,
        [bf16((rows // parts, width))] * parts,
        "pick_queries",
        in_specs=[whole()] * 2,
        out_specs=[whole()] * parts,
        moved=4 * ends.size,
    )(ends, inner)


def parts_kernel(source_ref, *outs):
    first = 0
    for out_ref in outs:
        rows = out_ref.shape[0]
        out_ref[...] = source_ref[first : first + rows, :]
        first += rows


def in_parts(source):
    rows, width = source.shape
    large = rows * 5 // 8 // 16 * 16
    return local_call(
        parts_kernel,
        [bf16((large, width)), bf16((rows - large, width))],
        "query_parts",
        in_specs=[whole()],
        out_specs=[whole()] * 2,
    )(source)


def unpack(packed, wide_ref, slot, total, width):
    columns = width // lanes
    half = total // 2
    for i in range(columns):
        wide_ref[slot * total : (slot + 1) * total, i * lanes : (i + 1) * lanes] = packed[
            i * total : (i + 1) * total, :
        ]
    rest = packed[columns * total :, :]
    wide_ref[slot * total : slot * total + half, columns * lanes :] = rest[:, : lanes // 2]
    wide_ref[slot * total + half : (slot + 1) * total, columns * lanes :] = rest[:, lanes // 2 :]


def widened(column, width):
    return jnp.concatenate([column] * (width // lanes), axis=1)


def shard_mass(length_ref, wide_ref, slot, lse, key_ref, context, rows, heads, first, tile):
    total = rows * heads
    scores = jnp.dot(
        wide_ref[slot * total : (slot + 1) * total, :],
        key_ref[:, first : first + tile],
        preferred_element_type=jnp.float32,
    )
    summed = jnp.zeros((rows, tile), jnp.float32)
    for h in range(heads):
        summed = summed + jnp.exp2(scores[h * rows : (h + 1) * rows] * (main_scale * log2_e) - lse[:, h : h + 1])
    visible = visible_tile(length_ref, context, rows, first, tile, key_ref.shape[1])
    return jnp.where(visible, summed, 0.0)


def rows_at(ref, index, rows):
    return ref[pl.ds(pl.multiple_of(index * rows, rows), rows), :]


def visible_tile(length_ref, block, rows, first, width, key_count):
    positions = lax.axis_index("context") * key_count + first + lax.broadcasted_iota(jnp.int32, (rows, width), 1)
    return positions < widened(rows_at(length_ref, block, rows), width)


def mass_kernel(flip, places, rows, heads, length_ref, *refs):
    count = len(places)
    parts = (len(refs) - 4) // count
    packs = [refs[n * parts : (n + 1) * parts] for n in range(count)]
    lse_ref, key_ref, out_ref, wide_ref = refs[count * parts :]
    width, key_count = key_ref.shape
    tile = math.gcd(key_count, 512)
    total = rows * heads
    own_plane, own_core, _ = place()
    plane = own_plane ^ flip
    for n, other in enumerate(places):
        unpack(jnp.concatenate([ref[...] for ref in packs[n]], axis=0), wide_ref, n, total, width)
        core = own_core ^ other
        context = 2 * plane + core
        lse = rows_at(lse_ref, context, rows)
        for first in range(0, key_count, tile):
            mass = shard_mass(length_ref, wide_ref, n, lse, key_ref, context, rows, heads, first, tile)
            if count == 1:
                out_ref[:, first : first + tile] = mass
            else:
                out_ref[pl.ds(pl.multiple_of(core * rows, rows), rows), first : first + tile] = mass


def chunk_mass(lengths, packs, lse, keys, flip, places, rows, heads, name, flops=1):
    width, key_count = keys.shape
    count = len(places)
    total = rows * heads
    return local_call(
        functools.partial(mass_kernel, flip, places, rows, heads),
        f32((count * rows, key_count)),
        name,
        in_specs=[whole()] * (len(packs) + 3),
        out_specs=whole(),
        scratch=[pltpu.VMEM((count * total, width), jnp.bfloat16)],
        flops=flops,
    )(lengths, *packs, lse, keys)


def share_kernel(rows, heads, length_ref, pack_ref, lse_ref, own_ref, near_ref, far_ref, half_ref, key_ref, *refs):
    outs = refs[:-2]
    wide_ref, chunks_ref = refs[-2:]
    width, key_count = key_ref.shape
    tile = math.gcd(key_count, 512)
    total = rows * heads
    unpack(pack_ref[...], wide_ref, 0, total, width)
    plane, core, group = place()
    other = 1 - core
    context = 2 * (plane ^ 2) + other
    lse = rows_at(lse_ref, context, rows)
    chunks_ref[0] = own_ref[...]
    chunks_ref[1] = near_ref[...]
    chunks_ref[3] = far_ref[...]
    chunks_ref[2, pl.ds(pl.multiple_of(core * rows, rows), rows), :] = half_ref[...]
    for first in range(0, key_count, tile):
        chunks_ref[2, pl.ds(pl.multiple_of(other * rows, rows), rows), first : first + tile] = shard_mass(
            length_ref, wide_ref, 0, lse, key_ref, context, rows, heads, first, tile
        )
    for e, out_ref in enumerate(outs):
        out_ref[...] = chunks_ref[plane ^ group ^ e].astype(out_ref.dtype)


def shared_mass(lengths, pack, lse, own, near, far, half, keys, rows, heads, partners):
    width, key_count = keys.shape
    total = rows * heads
    both = 2 * rows
    return local_call(
        functools.partial(share_kernel, rows, heads),
        [f32((both, key_count))] + [bf16((both, key_count))] * (partners - 1),
        "mass_and_share",
        in_specs=[whole()] * 8,
        out_specs=[whole()] * partners,
        scratch=[
            pltpu.VMEM((total, width), jnp.bfloat16),
            pltpu.VMEM((4, both, key_count), jnp.float32),
        ],
        moved=2 * keys.size,
    )(lengths, pack, lse, own, near, far, half, keys)


def logits_kernel(length_ref, query_ref, key_ref, weight_ref, logits_ref, masked_ref, stats_ref):
    rows, key_count = logits_ref.shape
    heads = query_ref.shape[0] // rows
    tile = math.gcd(key_count, 256)
    group = lax.axis_index("heads")
    best = jnp.full((rows, 1), masked_low, jnp.float32)
    weights = widened(weight_ref[...], tile)
    for first in range(0, key_count, tile):
        dots = lax.dot_general(
            query_ref[...], key_ref[first : first + tile, :], (((1,), (1,)), ((), ())),
            preferred_element_type=jnp.float32,
        )
        masked = jnp.where(dots > 0, weights, 0.0)
        masked_ref[:, first : first + tile] = masked
        logits = jnp.sum((dots * masked).reshape(rows, heads, tile), axis=1)
        logits_ref[:, first : first + tile] = logits
        visible = visible_tile(length_ref, group, rows, first, tile, key_count)
        best = jnp.maximum(best, jnp.max(jnp.where(visible, logits, masked_low), axis=1, keepdims=True))
    visible = visible_tile(length_ref, group, rows, 0, key_count, key_count)
    total = jnp.sum(jnp.where(visible, jnp.exp(logits_ref[...] - best), 0.0), axis=1, keepdims=True)
    column = lax.broadcasted_iota(jnp.int32, (rows, lanes), 1)
    stats_ref[...] = jnp.where(column == 0, best, total)


def index_logits(lengths, flat_query, index_key, weight_wide, rows):
    key_count = index_key.shape[0]
    flat = flat_query.shape[0]
    return local_call(
        logits_kernel,
        [f32((rows, key_count)), f32((flat, key_count)), f32((rows, lanes))],
        "index_logits",
        in_specs=[whole()] * 4,
        out_specs=[whole()] * 3,
        moved=2 * index_key.size,
    )(lengths, flat_query, index_key, weight_wide)


def load_kernel(
    length_ref, lse_ref, weight_ref, query_hbm, key_hbm, latent_hbm,
    length_out, lse_out, weight_out, query_out, turned_out, key_out, latent_out, semaphores,
):
    copies = [
        pltpu.make_async_copy(source, target, semaphores.at[i])
        for i, (source, target) in enumerate(
            [(query_hbm, query_out), (key_hbm, key_out), (latent_hbm, latent_out)]
        )
    ]
    for copy in copies:
        copy.start()
    total = length_out.shape[0]
    spread = lax.broadcasted_iota(jnp.int32, (8, lanes), 0)
    for first in range(0, total, 8):
        column = jnp.zeros((8, lanes), jnp.int32)
        for i in range(8):
            column = jnp.where(spread == i, length_ref[first + i], column)
        length_out[first : first + 8, :] = column
    lse_out[...] = lse_ref[...].T * log2_e
    rows, heads = weight_ref.shape
    width = key_out.shape[1]
    weights = weight_ref[...].T * width ** (-0.5)
    for t in range(rows):
        weight_out[t * heads : (t + 1) * heads, :] = jnp.broadcast_to(weights[:, t : t + 1], (heads, lanes))
    copies[0].wait()
    turned_out[...] = query_out[...].reshape(rows * heads, width).astype(jnp.float32).T.astype(jnp.bfloat16)
    copies[1].wait()
    copies[2].wait()


def load_inputs(lengths, lse, weights, query, key, latent):
    rows, heads, width = query.shape
    flat = rows * heads
    return local_call(
        load_kernel,
        [
            jax.ShapeDtypeStruct((lengths.shape[0], lanes), jnp.int32),
            f32(lse.shape[::-1]),
            f32((flat, lanes)),
            bf16(query.shape),
            bf16((width, flat)),
            bf16(key.shape),
            bf16(latent.shape),
        ],
        "load_inputs",
        in_specs=[scalars(), whole(), whole(), hbm(), hbm(), hbm()],
        out_specs=[whole()] * 7,
        scratch=[pltpu.SemaphoreType.DMA((3,))],
        moved=4 * (key.size + latent.size),
    )(lengths, lse, weights, query, key, latent)


def join_kernel(stats_ref, own_ref, *refs):
    parts, (mass_ref, out_ref) = refs[:-2], refs[-2:]
    mass = own_ref[...]
    for part in parts:
        mass = mass + part[...].astype(jnp.float32)
    mass_ref[...] = mass
    column = lax.broadcasted_iota(jnp.int32, out_ref.shape, 1)
    out_ref[...] = jnp.where(column == 2, jnp.sum(mass, axis=1, keepdims=True), stats_ref[...])


def joined_mass(stats, own, parts):
    return local_call(
        join_kernel,
        [f32(own.shape), f32(stats.shape)],
        "join_mass",
        in_specs=[whole()] * (2 + len(parts)),
        out_specs=[whole()] * 2,
        moved=8 * own.size,
    )(stats, own, *parts)


def pair_stats_kernel(own_ref, got_ref, out_ref):
    own, got = own_ref[...], got_ref[...]
    top = jnp.maximum(own[:, 0:1], got[:, 0:1])
    shares = own[:, 1:2] * jnp.exp(own[:, 0:1] - top) + got[:, 1:2] * jnp.exp(got[:, 0:1] - top)
    column = lax.broadcasted_iota(jnp.int32, out_ref.shape, 1)
    out_ref[...] = jnp.where(column == 0, top, jnp.where(column == 1, shares, own + got))


def pair_stats(own, got):
    return local_call(
        pair_stats_kernel, f32(own.shape), "pair_stats", in_specs=[whole()] * 2, out_specs=whole(), moved=8 * own.size
    )(own, got)


def back_kernel(sources, length_ref, mass_ref, logits_ref, turned_ref, key_ref, masked_ref, *refs):
    stats = [ref[...] for ref in refs[:sources]]
    partners = len(refs) - sources - 4
    key_outs = refs[sources : sources + partners]
    keep_ref, send_ref, slope_ref, grad_ref = refs[sources + partners :]
    rows, key_count = mass_ref.shape
    width, flat = turned_ref.shape
    heads = flat // rows
    tile = math.gcd(key_count, 256)
    _, core, group = place()
    top = functools.reduce(jnp.maximum, [s[:, 0:1] for s in stats])
    shares = sum(s[:, 1:2] * jnp.exp(s[:, 0:1] - top) for s in stats)
    total = sum(s[:, 2:3] for s in stats)
    visible = visible_tile(length_ref, group, rows, 0, key_count, key_count)
    weights_exp = jnp.where(visible, jnp.exp(logits_ref[...] - top), 0.0)
    slope_ref[...] = loss_scale * (weights_exp / shares - mass_ref[...] / total)
    query_grad = jnp.zeros((flat, width), jnp.float32)
    for first in range(0, key_count, tile):
        keys = key_ref[first : first + tile, :]
        slopes = jnp.broadcast_to(slope_ref[:, first : first + tile][:, None, :], (rows, heads, tile))
        terms = (slopes.reshape(flat, tile) * masked_ref[:, first : first + tile]).astype(jnp.bfloat16)
        query_grad = query_grad + jnp.dot(terms, keys, preferred_element_type=jnp.float32)
        key_grad = jnp.dot(turned_ref[...], terms, preferred_element_type=jnp.float32)
        grad_ref[first : first + tile, :] = key_grad.T
    block = key_count // partners
    for e, out_ref in enumerate(key_outs):
        out_ref[...] = rows_at(grad_ref, group ^ e, block).astype(out_ref.dtype)
    planes = keep_ref.shape[0]
    part = heads // (2 * planes)
    split = query_grad.reshape(rows, planes, 2, part, width)
    first_core = core == 0
    for plane in range(planes):
        low, high = split[:, plane, 0], split[:, plane, 1]
        keep_ref[plane] = jnp.where(first_core, low, high).reshape(rows * part, width)
        send_ref[plane] = jnp.where(first_core, high, low).reshape(rows * part, width).astype(jnp.bfloat16)


def back_pass(lengths, mass, logits, turned, index_key, masked, stats, partners, planes):
    rows, key_count = mass.shape
    width, flat = turned.shape
    part = flat // (2 * planes)
    return local_call(
        functools.partial(back_kernel, len(stats)),
        [f32((key_count // partners, width))]
        + [bf16((key_count // partners, width))] * (partners - 1)
        + [f32((planes, part, width)), bf16((planes, part, width))],
        "index_back",
        in_specs=[whole()] * (6 + len(stats)),
        out_specs=[whole()] * (partners + 2),
        scratch=[pltpu.VMEM((rows, key_count), jnp.float32), pltpu.VMEM((key_count, width), jnp.float32)],
        moved=8 * key_count * width,
    )(lengths, mass, logits, turned, index_key, masked, *stats)


def pair_kernel(keep_ref, got_ref, *outs):
    own_plane, _, _ = place()
    for e, out_ref in enumerate(outs):
        plane = own_plane ^ e
        out_ref[...] = (keep_ref[plane] + got_ref[plane].astype(jnp.float32)).astype(out_ref.dtype)


def pair_sums(keep, got):
    planes, part, width = keep.shape
    return local_call(
        pair_kernel,
        [f32((part, width))] + [bf16((part, width))] * (planes - 1),
        "pair_sums",
        in_specs=[whole(), whole()],
        out_specs=[whole()] * planes,
        moved=8 * keep.size,
    )(keep, got)


def last_kernel(key_parts, *refs):
    query_out, key_out = refs[-2:]
    key_refs, query_refs = refs[:key_parts], refs[key_parts:-2]
    key_out[...] = sum(ref[...].astype(jnp.float32) for ref in key_refs)
    query_out[...] = sum(ref[...].astype(jnp.float32) for ref in query_refs).reshape(query_out.shape)


def last_sums(key_parts, query_parts, query_shape):
    return local_call(
        functools.partial(last_kernel, len(key_parts)),
        [f32(query_shape), f32(key_parts[0].shape)],
        "last_sums",
        in_specs=[whole()] * (len(key_parts) + len(query_parts)),
        out_specs=[whole()] * 2,
        moved=8 * key_parts[0].size,
    )(*key_parts, *query_parts)


def after(array, *others):
    return lax.optimization_barrier((array, *others))[0]


def block_device(main_query, latent_keys, head_lse, lengths, index_query, index_key, index_weight):
    contexts = lax.axis_size("context")
    planes = contexts // 2
    partners = lax.axis_size("heads")
    context = lax.axis_index("context")
    rows, heads, _ = main_query.shape
    own_rows, index_heads, width = index_query.shape
    key_count = latent_keys.shape[0]
    flat = own_rows * index_heads

    def planes_move(array, pairs):
        return lax.ppermute(array, "context", [(2 * a + k, 2 * b + k) for a, b in pairs for k in (0, 1)])

    def context_flip(array, e):
        return lax.ppermute(array, "context", [(c, c ^ e) for c in range(contexts)])

    def heads_flip(array, e):
        return lax.ppermute(array, "heads", [(h, h ^ e) for h in range(partners)])

    def mass_of(packs, *rest):
        return chunk_mass(lengths, packs, lse, keys, *rest[:2], rows, heads, *rest[2:])

    pack = packed_queries(main_query)
    near = planes_move(pack, [(0, 1), (1, 0), (2, 3), (3, 2)])
    inner = planes_move(pack, [(1, 2), (2, 1), (0, 0), (3, 3)])
    ends = planes_move(pack, [(0, 3), (3, 0)])
    own_pair = context_flip(pack, 1)
    lengths, lse, weight_wide, query, turned, index_key, keys = load_inputs(
        lengths, head_lse.T, index_weight, index_query, index_key, after(latent_keys, pack).T
    )
    inner = after(inner, lse)
    far = planes_move(inner, [(0, 2), (3, 1), (1, 0), (2, 3)])
    logits, masked, stats = index_logits(lengths, query.reshape(flat, width), index_key, weight_wide, own_rows)
    own_mass = mass_of([pack, own_pair], 0, (0, 1), "mass_own")
    near = in_parts(after(near, stats))
    near_mass = mass_of([*near, *(context_flip(a, 1) for a in near)], 1, (0, 1), "mass_near")
    across = picked(after(ends, own_mass, near_mass), inner, 3)
    across_mass = mass_of([*across, *(context_flip(a, 1) for a in across)], 3, (0, 1), "mass_across")
    far = after(far, near_mass, across_mass)
    far_pair = context_flip(far, 1)
    far_mass = mass_of([far], 2, (0,), "mass_far")
    shared = shared_mass(
        lengths, far_pair, lse, own_mass, near_mass, across_mass, far_mass, keys, rows, heads, partners
    )
    mass, stats = joined_mass(stats, shared[0], [heads_flip(shared[e], e) for e in reversed(range(1, partners))])
    stats = pair_stats(stats, context_flip(stats, 1))
    every = [stats] + [context_flip(stats, 2 * e) for e in reversed(range(1, planes))]
    *key_grads, keep, send = back_pass(
        lengths, mass, logits, turned, index_key, masked, every, partners, planes
    )
    got = context_flip(send, 1)
    key_parts = [key_grads[0]] + [heads_flip(key_grads[e], e) for e in reversed(range(1, partners))]
    sums = pair_sums(keep, got)
    query_parts = [sums[0]] + [context_flip(sums[e], 2 * e) for e in reversed(range(1, planes))]
    return last_sums(key_parts, query_parts, (own_rows, index_heads // contexts, width))


def fits(mesh):
    return mesh.shape["context"] == 8 and mesh.shape["heads"] == 4


def solution(mesh):
    placed = (
        P("context", "heads", None),
        P("context", None),
        P(None, "heads"),
        P(),
        P("heads", None, None),
        P("context", None),
        P("heads", None),
    )
    return jax.shard_map(
        block_device if fits(mesh) else general_on_device,
        mesh=mesh,
        in_specs=placed,
        out_specs=(P("heads", "context", None), P(("context", "heads"), None)),
        check_vma=False,
    )
```

```python
import functools
import math

import jax
import jax.numpy as jnp
from jax import lax
from jax.experimental import pallas as pl
from jax.experimental.pallas import tpu as pltpu
from jax.sharding import PartitionSpec as P

main_scale = 192.0 ** (-0.5)
loss_scale = 64.0
masked_low = -1e30
log2_e = math.log2(math.e)
lanes = 128
vmem_bytes = 20 * 1024 * 1024
most_bytes = 60 * 1024 * 1024
load_bytes = 58 * 1024 * 1024

def joined(part, axis, combine):
    gathered = jax.tree.map(lambda a: lax.all_gather(a, axis), part)

    def take(source):
        return jax.tree.map(lambda a: lax.dynamic_index_in_dim(a, source, 0, False), gathered)

    return lax.fori_loop(
        1, lax.axis_size(axis), lambda source, state: combine(state, take(source)), take(0)
    )


def head_mass(queries, lse_rows, len_rows, latent, first_key):
    row_count = queries.shape[0]
    block_rows = math.gcd(row_count, 64)
    steps_count = row_count // block_rows
    key_pos = first_key + jnp.arange(latent.shape[0], dtype=jnp.int32)

    def one_block(inputs):
        query_block, lse_block, len_block = inputs
        scores = (
            jnp.einsum("rhd,sd->rhs", query_block, latent, preferred_element_type=jnp.float32)
            * main_scale
        )
        summed = jnp.sum(jnp.exp(scores - lse_block[:, :, None]), axis=1)
        return jnp.where(key_pos[None, :] < len_block[:, None], summed, 0.0)

    stacked = lax.map(
        one_block,
        (
            queries.reshape((steps_count, block_rows) + queries.shape[1:]),
            lse_rows.reshape(steps_count, block_rows, lse_rows.shape[1]),
            len_rows.reshape(steps_count, block_rows),
        ),
    )
    return stacked.reshape(row_count, latent.shape[0])


def general_on_device(main_query, latent_keys, head_lse, lengths, index_query, index_key, index_weight):
    key_count = latent_keys.shape[0]
    first_key = lax.axis_index("context") * key_count
    own_rows = index_query.shape[0]
    row_first = lax.axis_index("heads") * own_rows
    partial_mass = head_mass(
        lax.all_gather(main_query, "context", axis=0, tiled=True),
        head_lse,
        lengths,
        latent_keys,
        first_key,
    )
    summed_mass = lax.psum(partial_mass, "heads")
    row_mass = lax.dynamic_slice_in_dim(summed_mass, row_first, own_rows, 0)
    own_len = lax.dynamic_slice_in_dim(lengths, row_first, own_rows, 0)
    visible = (first_key + jnp.arange(key_count, dtype=jnp.int32))[None, :] < own_len[:, None]
    heads_count = index_query.shape[1]
    width = index_query.shape[2]
    index_scale = width ** (-0.5)
    flat_query = index_query.reshape(own_rows * heads_count, width)
    block_keys = math.gcd(key_count, 512)
    block_total = key_count // block_keys
    key_blocks = index_key.reshape(block_total, block_keys, width)

    def block_dots(key_block):
        products = lax.dot_general(
            flat_query, key_block, (((1,), (1,)), ((), ())), preferred_element_type=jnp.float32
        )
        return products.reshape(own_rows, heads_count, key_block.shape[0])

    def block_logits(key_block):
        return (
            jnp.einsum(
                "tj,tjs->ts",
                index_weight,
                jax.nn.relu(block_dots(key_block)),
                precision=lax.Precision.HIGHEST,
            )
            * index_scale
        )

    logits = jnp.moveaxis(lax.map(block_logits, key_blocks), 0, 1).reshape(own_rows, key_count)
    local_top = jnp.max(jnp.where(visible, logits, masked_low), axis=1)
    mass_local = jnp.sum(row_mass, axis=1)
    local_exp = jnp.where(visible, jnp.exp(logits - local_top[:, None]), 0.0)

    def combine(first, second):
        highest = jnp.maximum(first[0], second[0])
        merged = first[1] * jnp.exp(first[0] - highest) + second[1] * jnp.exp(second[0] - highest)
        return (highest, merged, first[2] + second[2])

    top, share_sum, mass_total = joined(
        (local_top, jnp.sum(local_exp, axis=1), mass_local), "context", combine
    )
    weights_exp = jnp.where(visible, jnp.exp(logits - top[:, None]), 0.0)
    probability = weights_exp / share_sum[:, None]
    target = row_mass / mass_total[:, None]
    slopes = loss_scale * (probability - target)
    slope_blocks = slopes.reshape(own_rows, block_total, block_keys).transpose(1, 0, 2)

    def back_step(query_grad, inputs):
        key_block, slope_block = inputs
        products = block_dots(key_block)
        terms = jnp.where(
            products > 0, slope_block[:, None, :] * index_weight[:, :, None] * index_scale, 0.0
        )
        terms = terms.astype(jnp.bfloat16).reshape(own_rows * heads_count, key_block.shape[0])
        query_grad = query_grad + jnp.dot(terms, key_block, preferred_element_type=jnp.float32)
        key_grad = lax.dot_general(
            terms, flat_query, (((0,), (0,)), ((), ())), preferred_element_type=jnp.float32
        )
        return (query_grad, key_grad)

    start_grad = jnp.zeros((own_rows * heads_count, width), jnp.float32)
    query_grad, key_grads = lax.scan(back_step, start_grad, (key_blocks, slope_blocks))
    query_grad = query_grad.reshape(own_rows, heads_count, width)
    key_grad = key_grads.reshape(key_count, width)
    out_query = lax.psum_scatter(query_grad, "context", scatter_dimension=1, tiled=True)
    out_key = lax.psum_scatter(key_grad, "heads", scatter_dimension=0, tiled=True)
    return (out_query, out_key)


def local_call(kernel, out_shape, name, grid=None, in_specs=None, out_specs=None, scratch=(), flops=1, moved=0, room=vmem_bytes):
    settings = dict(
        out_shape=out_shape,
        scratch_shapes=list(scratch),
        name=name,
        compiler_params=pltpu.CompilerParams(vmem_limit_bytes=room),
        cost_estimate=pl.CostEstimate(flops=flops, bytes_accessed=1, transcendentals=0),
    )
    if grid is not None:
        settings["grid"] = grid
    if in_specs is not None:
        settings["in_specs"] = in_specs
    if out_specs is not None:
        settings["out_specs"] = out_specs
    return pl.pallas_call(kernel, **settings)


def whole():
    return pl.BlockSpec(memory_space=pltpu.VMEM)


def scalars():
    return pl.BlockSpec(memory_space=pltpu.SMEM)


def fixed(shape):
    return pl.BlockSpec(shape, lambda step: (0,) * len(shape))


def f32(shape):
    return jax.ShapeDtypeStruct(shape, jnp.float32)


def bf16(shape):
    return jax.ShapeDtypeStruct(shape, jnp.bfloat16)


def place():
    context = lax.axis_index("context")
    return context >> 1, context & 1, lax.axis_index("heads")


def hbm():
    return pl.BlockSpec(memory_space=pltpu.HBM)


def head_blocks(heads):
    first = heads * 5 // 8
    return ((0, first), (first, heads - first))


def packed_rows(rows, heads, width):
    return rows * heads * width // lanes


def pack_kernel(query_ref, out_ref, *block_refs):
    rows, heads, width = query_ref.shape
    columns = width // lanes
    stacked = jnp.swapaxes(query_ref[...].astype(jnp.float32), 0, 1).reshape(rows * heads, width)
    begin = 0
    for (first, count), block_ref in zip(head_blocks(heads), block_refs):
        total = rows * count
        block = stacked[rows * first : rows * first + total]
        rest = block[:, columns * lanes :]
        pieces = [block[:, i * lanes : (i + 1) * lanes] for i in range(columns)]
        pieces.append(jnp.concatenate([rest[: total // 2], rest[total // 2 :]], axis=1))
        place = 0
        for piece in pieces:
            piece = piece.astype(jnp.bfloat16)
            size = piece.shape[0]
            out_ref[begin + place : begin + place + size, :] = piece
            block_ref[place : place + size, :] = piece
            place += size
        begin += place


def packed_queries(queries):
    rows, heads, width = queries.shape
    blocks = [bf16((packed_rows(rows, count, width), lanes)) for _, count in head_blocks(heads)]
    return local_call(
        pack_kernel,
        [bf16((packed_rows(rows, heads, width), lanes))] + blocks,
        "pack_queries",
        in_specs=[whole()],
        out_specs=[whole()] * (1 + len(blocks)),
        flops=30_000_000_000,
    )(queries)


def pick_kernel(ends_ref, *refs):
    inner_refs, out_ref = refs[:-1], refs[-1]
    plane, _, _ = place()
    inner = (plane == 1) | (plane == 2)

    @pl.when(inner)
    def _():
        begin = 0
        for inner_ref in inner_refs:
            rows = inner_ref.shape[0]
            out_ref[begin : begin + rows, :] = inner_ref[...]
            begin += rows

    @pl.when(jnp.logical_not(inner))
    def _():
        out_ref[...] = ends_ref[...]


def picked(ends, inner):
    return local_call(
        pick_kernel,
        bf16(ends.shape),
        "pick_queries",
        in_specs=[whole()] * (1 + len(inner)),
        out_specs=whole(),
    )(ends, *inner)


def unpack(packed_ref, begin, wide_ref, row, total):
    width = wide_ref.shape[1]
    columns = width // lanes
    half = total // 2
    for i in range(columns):
        wide_ref[row : row + total, i * lanes : (i + 1) * lanes] = packed_ref[
            begin + i * total : begin + (i + 1) * total, :
        ]
    rest = packed_ref[begin + columns * total : begin + columns * total + half, :]
    wide_ref[row : row + half, columns * lanes :] = rest[:, : lanes // 2]
    wide_ref[row + half : row + total, columns * lanes :] = rest[:, lanes // 2 :]


def widened(column, width):
    return jnp.concatenate([column] * (width // lanes), axis=1)


def rows_at(ref, index, rows):
    return ref[pl.ds(pl.multiple_of(index * rows, rows), rows), :]


def visible_tile(length_ref, block, rows, first, width, key_count):
    positions = lax.axis_index("context") * key_count + first + lax.broadcasted_iota(jnp.int32, (rows, width), 1)
    return positions < widened(rows_at(length_ref, block, rows), width)


def chip_mass(length_ref, wide_ref, lse_ref, own_key_ref, pair_key_ref, context, heads, out_ref, before_ref=None):
    width, key_count = own_key_ref.shape
    first_head, head_count = heads
    rows = wide_ref.shape[0] // head_count
    tile = math.gcd(key_count, 512)
    plane, core, _ = place()
    lse = rows_at(lse_ref, context, rows)
    column = widened(rows_at(length_ref, context, rows), tile)
    spread = lax.broadcasted_iota(jnp.int32, (rows, tile), 1)
    for key_ref, half in ((own_key_ref, core), (pair_key_ref, 1 - core)):
        for first in range(0, key_count, tile):
            scores = jnp.dot(wide_ref[...], key_ref[:, first : first + tile], preferred_element_type=jnp.float32)
            summed = jnp.zeros((rows, tile), jnp.float32)
            for h in range(head_count):
                summed = summed + jnp.exp2(
                    scores[h * rows : (h + 1) * rows] * (main_scale * log2_e)
                    - lse[:, first_head + h : first_head + h + 1]
                )
            visible = (2 * plane + half) * key_count + first + spread < column
            mass = jnp.where(visible, summed, 0.0)
            columns = pl.ds(pl.multiple_of(half * key_count + first, tile), tile)
            if before_ref is not None:
                mass = mass + before_ref[:, columns]
            out_ref[:, columns] = mass


def mass_kernel(flip, blocks, length_ref, pack_ref, lse_ref, own_key_ref, pair_key_ref, out_ref, wide_ref):
    plane, core, _ = place()
    heads = (blocks[0][0], sum(count for _, count in blocks))
    rows = wide_ref.shape[0] // heads[1]
    begin = row = 0
    for _, count in blocks:
        unpack(pack_ref, begin, wide_ref, row, rows * count)
        begin += packed_rows(rows, count, wide_ref.shape[1])
        row += rows * count
    chip_mass(length_ref, wide_ref, lse_ref, own_key_ref, pair_key_ref, 2 * (plane ^ flip) + core, heads, out_ref)


def chunk_mass(lengths, pack, lse, keys, flip, blocks, rows, name, flops=1):
    width, key_count = keys[0].shape
    total = rows * sum(count for _, count in blocks)
    return local_call(
        functools.partial(mass_kernel, flip, blocks),
        f32((rows, 2 * key_count)),
        name,
        in_specs=[whole()] * 5,
        out_specs=whole(),
        scratch=[pltpu.VMEM((total, width), jnp.bfloat16)],
        flops=flops,
    )(lengths, pack, lse, *keys)


def share_kernel(
    heads, length_ref, pack_ref, lse_ref, own_key_ref, pair_key_ref, own_ref, near_ref, across_ref, before_ref, *refs
):
    outs = refs[:-2]
    wide_ref, chunks_ref = refs[-2:]
    plane, core, group = place()
    unpack(pack_ref, 0, wide_ref, 0, wide_ref.shape[0])
    chunks_ref[0] = own_ref[...]
    chunks_ref[1] = near_ref[...]
    chunks_ref[3] = across_ref[...]
    chip_mass(
        length_ref, wide_ref, lse_ref, own_key_ref, pair_key_ref, 2 * (plane ^ 2) + core, heads, chunks_ref.at[2],
        before_ref,
    )
    for e, out_ref in enumerate(outs):
        out_ref[...] = chunks_ref[plane ^ group ^ e].astype(out_ref.dtype)


def shared_mass(lengths, pack, lse, keys, own, near, across, before, heads, partners):
    width, _ = keys[0].shape
    rows, both = own.shape
    return local_call(
        functools.partial(share_kernel, heads),
        [f32((rows, both))] + [bf16((rows, both))] * (partners - 1),
        "mass_and_share",
        in_specs=[whole()] * 9,
        out_specs=[whole()] * partners,
        scratch=[pltpu.VMEM((rows * heads[1], width), jnp.bfloat16), pltpu.VMEM((4, rows, both), jnp.float32)],
    )(lengths, pack, lse, *keys, own, near, across, before)


def logits_kernel(length_ref, query_ref, key_ref, weight_ref, logits_ref, masked_ref, stats_ref):
    rows, key_count = logits_ref.shape
    heads = query_ref.shape[0] // rows
    tile = math.gcd(key_count, 256)
    group = lax.axis_index("heads")
    best = jnp.full((rows, 1), masked_low, jnp.float32)
    weights = widened(weight_ref[...], tile)
    for first in range(0, key_count, tile):
        dots = lax.dot_general(
            query_ref[...], key_ref[first : first + tile, :], (((1,), (1,)), ((), ())),
            preferred_element_type=jnp.float32,
        )
        masked = jnp.where(dots > 0, weights, 0.0)
        masked_ref[:, first : first + tile] = masked
        logits = jnp.sum((dots * masked).reshape(rows, heads, tile), axis=1)
        logits_ref[:, first : first + tile] = logits
        visible = visible_tile(length_ref, group, rows, first, tile, key_count)
        best = jnp.maximum(best, jnp.max(jnp.where(visible, logits, masked_low), axis=1, keepdims=True))
    visible = visible_tile(length_ref, group, rows, 0, key_count, key_count)
    total = jnp.sum(jnp.where(visible, jnp.exp(logits_ref[...] - best), 0.0), axis=1, keepdims=True)
    column = lax.broadcasted_iota(jnp.int32, (rows, lanes), 1)
    stats_ref[...] = jnp.where(column == 0, best, total)


def index_logits(lengths, flat_query, index_key, weight_wide, rows):
    key_count = index_key.shape[0]
    flat = flat_query.shape[0]
    return local_call(
        logits_kernel,
        [f32((rows, key_count)), f32((flat, key_count)), f32((rows, lanes))],
        "index_logits",
        in_specs=[whole()] * 4,
        out_specs=[whole()] * 3,
        moved=2 * index_key.size,
    )(lengths, flat_query, index_key, weight_wide)


def load_kernel(
    length_ref, lse_ref, weight_ref, query_hbm, key_hbm, latent_hbm,
    length_out, lse_out, weight_out, query_out, turned_out, key_out, latent_out, semaphores,
):
    copies = [
        pltpu.make_async_copy(source, target, semaphores.at[i])
        for i, (source, target) in enumerate(
            [(query_hbm, query_out), (key_hbm, key_out), (latent_hbm, latent_out)]
        )
    ]
    for copy in copies:
        copy.start()
    total = length_out.shape[0]
    spread = lax.broadcasted_iota(jnp.int32, (8, lanes), 0)
    for first in range(0, total, 8):
        column = jnp.zeros((8, lanes), jnp.int32)
        for i in range(8):
            column = jnp.where(spread == i, length_ref[first + i], column)
        length_out[first : first + 8, :] = column
    lse_out[...] = lse_ref[...].T * log2_e
    rows, heads = weight_ref.shape
    width = key_out.shape[1]
    weights = weight_ref[...].T * width ** (-0.5)
    for t in range(rows):
        weight_out[t * heads : (t + 1) * heads, :] = jnp.broadcast_to(weights[:, t : t + 1], (heads, lanes))
    copies[0].wait()
    turned_out[...] = query_out[...].reshape(rows * heads, width).astype(jnp.float32).T.astype(jnp.bfloat16)
    copies[1].wait()
    copies[2].wait()


def load_inputs(lengths, lse, weights, query, key, latent):
    rows, heads, width = query.shape
    flat = rows * heads
    return local_call(
        load_kernel,
        [
            jax.ShapeDtypeStruct((lengths.shape[0], lanes), jnp.int32),
            f32(lse.shape[::-1]),
            f32((flat, lanes)),
            bf16(query.shape),
            bf16((width, flat)),
            bf16(key.shape),
            bf16(latent.shape),
        ],
        "load_inputs",
        in_specs=[scalars(), whole(), whole(), hbm(), hbm(), hbm()],
        out_specs=[whole()] * 7,
        scratch=[pltpu.SemaphoreType.DMA((3,))],
        moved=4 * (key.size + latent.size),
    )(lengths, lse, weights, query, key, latent)


def join_kernel(stats_ref, own_ref, *refs):
    parts, (keep_ref, give_ref, out_ref) = refs[:-3], refs[-3:]
    mass = own_ref[...]
    for part in parts:
        mass = mass + part[...].astype(jnp.float32)
    rows, both = mass.shape
    low, high = mass[:, : both // 2], mass[:, both // 2 :]
    _, core, _ = place()
    keep_ref[...] = jnp.where(core == 0, low, high)
    give_ref[...] = jnp.where(core == 0, high, low)
    total = jnp.broadcast_to(jnp.sum(mass, axis=1, keepdims=True), (rows, lanes))
    nothing = jnp.zeros((rows, lanes), jnp.float32)
    totals = jnp.concatenate([jnp.where(core == 0, total, nothing), jnp.where(core == 0, nothing, total)], axis=0)
    column = lax.broadcasted_iota(jnp.int32, out_ref.shape, 1)
    out_ref[...] = jnp.where(column == 2, totals, stats_ref[...])


def joined_mass(stats, own, parts):
    rows, both = own.shape
    return local_call(
        join_kernel,
        [f32((rows, both // 2)), f32((rows, both // 2)), f32(stats.shape)],
        "join_mass",
        in_specs=[whole()] * (2 + len(parts)),
        out_specs=[whole()] * 3,
    )(stats, own, *parts)


def merge_kernel(*refs):
    out_ref = refs[-1]
    stats = [ref[...] for ref in refs[:-1]]
    top = functools.reduce(jnp.maximum, [s[:, 0:1] for s in stats])
    shares = sum(s[:, 1:2] * jnp.exp(s[:, 0:1] - top) for s in stats)
    column = lax.broadcasted_iota(jnp.int32, out_ref.shape, 1)
    out_ref[...] = jnp.where(column == 0, top, jnp.where(column == 1, shares, sum(stats)))


def merged_stats(stats):
    return local_call(
        merge_kernel, f32(stats[0].shape), "merge_stats", in_specs=[whole()] * len(stats), out_specs=whole()
    )(*stats)


def back_rows(half, length_ref, stats_ref, mass_ref, logits_ref, turned_ref, key_ref, masked_ref, slope_ref, store):
    rows, key_count = mass_ref.shape
    width = key_ref.shape[1]
    flat = turned_ref.shape[1] // 2
    tile = math.gcd(key_count, 256)
    stats = rows_at(stats_ref, half, rows)
    visible = visible_tile(length_ref, 2 * lax.axis_index("heads") + half, rows, 0, key_count, key_count)
    weights_exp = jnp.where(visible, jnp.exp(rows_at(logits_ref, half, rows) - stats[:, 0:1]), 0.0)
    slope_ref[...] = loss_scale * (weights_exp / stats[:, 1:2] - mass_ref[...] / stats[:, 2:3])
    begin = pl.multiple_of(half * flat, flat)
    turned = turned_ref[:, pl.ds(begin, flat)]
    query_grad = jnp.zeros((flat, width), jnp.float32)
    for first in range(0, key_count, tile):
        keys = key_ref[first : first + tile, :]
        slopes = jnp.broadcast_to(slope_ref[:, first : first + tile][:, None, :], (rows, flat // rows, tile))
        masked = masked_ref[pl.ds(begin, flat), first : first + tile]
        terms = (slopes.reshape(flat, tile) * masked).astype(jnp.bfloat16)
        query_grad = query_grad + jnp.dot(terms, keys, preferred_element_type=jnp.float32)
        store(first, tile, jnp.dot(turned, terms, preferred_element_type=jnp.float32))
    return query_grad


def back_own_kernel(
    length_ref, stats_ref, mass_ref, logits_ref, turned_ref, key_ref, masked_ref, query_out, key_out, slope_ref
):
    _, core, _ = place()

    def store(first, tile, key_grad):
        key_out[:, first : first + tile] = key_grad

    query_out[...] = back_rows(
        core, length_ref, stats_ref, mass_ref, logits_ref, turned_ref, key_ref, masked_ref, slope_ref, store
    )


def back_own(lengths, stats, mass, logits, turned, index_key, masked):
    rows, key_count = mass.shape
    width, flat = turned.shape
    return local_call(
        back_own_kernel,
        [f32((flat // 2, width)), f32((width, key_count))],
        "index_back_own",
        in_specs=[whole()] * 7,
        out_specs=[whole()] * 2,
        scratch=[pltpu.VMEM((rows, key_count), jnp.float32)],
    )(lengths, stats, mass, logits, turned, index_key, masked)


def back_pair_kernel(
    length_ref, stats_ref, mass_ref, logits_ref, turned_ref, key_ref, masked_ref, query_ref, before_ref, *refs
):
    partners = len(refs) - 4
    key_outs = refs[:partners]
    keep_ref, send_ref, slope_ref, grad_ref = refs[partners:]
    key_count, width = key_ref.shape
    _, core, group = place()

    def store(first, tile, key_grad):
        grad_ref[first : first + tile, :] = (before_ref[:, first : first + tile] + key_grad).T

    other = back_rows(
        1 - core, length_ref, stats_ref, mass_ref, logits_ref, turned_ref, key_ref, masked_ref, slope_ref, store
    )
    block = key_count // partners
    for e, out_ref in enumerate(key_outs):
        out_ref[...] = rows_at(grad_ref, group ^ e, block).astype(out_ref.dtype)
    planes, part, _ = keep_ref.shape
    rows = mass_ref.shape[0]
    for half, query_grad in ((core, query_ref[...]), (1 - core, other)):
        split = query_grad.reshape(rows, planes, 2, part // (2 * rows), width)
        place_of = pl.ds(pl.multiple_of(half * (part // 2), part // 2), part // 2)
        for plane in range(planes):
            low = split[:, plane, 0].reshape(part // 2, width)
            high = split[:, plane, 1].reshape(part // 2, width)
            keep_ref[plane, place_of, :] = jnp.where(core == 0, low, high)
            send_ref[plane, place_of, :] = jnp.where(core == 0, high, low).astype(jnp.bfloat16)


def back_pair(lengths, stats, mass, logits, turned, index_key, masked, query_grad, key_grad, partners, planes):
    rows, key_count = mass.shape
    width, flat = turned.shape
    part = flat // (2 * planes)
    return local_call(
        back_pair_kernel,
        [f32((key_count // partners, width))]
        + [bf16((key_count // partners, width))] * (partners - 1)
        + [f32((planes, part, width)), bf16((planes, part, width))],
        "index_back_pair",
        in_specs=[whole()] * 9,
        out_specs=[whole()] * (partners + 2),
        scratch=[pltpu.VMEM((rows, key_count), jnp.float32), pltpu.VMEM((key_count, width), jnp.float32)],
    )(lengths, stats, mass, logits, turned, index_key, masked, query_grad, key_grad)


def pair_kernel(keep_ref, got_ref, *outs):
    own_plane, _, _ = place()
    for e, out_ref in enumerate(outs):
        plane = own_plane ^ e
        out_ref[...] = (keep_ref[plane] + got_ref[plane].astype(jnp.float32)).astype(out_ref.dtype)


def pair_sums(keep, got):
    planes, part, width = keep.shape
    return local_call(
        pair_kernel,
        [f32((part, width))] + [bf16((part, width))] * (planes - 1),
        "pair_sums",
        in_specs=[whole(), whole()],
        out_specs=[whole()] * planes,
        moved=8 * keep.size,
    )(keep, got)


def last_kernel(key_parts, *refs):
    query_out, key_out = refs[-2:]
    key_refs, query_refs = refs[:key_parts], refs[key_parts:-2]
    key_out[...] = sum(ref[...].astype(jnp.float32) for ref in key_refs)
    query_out[...] = sum(ref[...].astype(jnp.float32) for ref in query_refs).reshape(query_out.shape)


def last_sums(key_parts, query_parts, query_shape):
    return local_call(
        functools.partial(last_kernel, len(key_parts)),
        [f32(query_shape), f32(key_parts[0].shape)],
        "last_sums",
        in_specs=[whole()] * (len(key_parts) + len(query_parts)),
        out_specs=[whole()] * 2,
        moved=8 * key_parts[0].size,
    )(*key_parts, *query_parts)


def after(array, *others):
    return lax.optimization_barrier((array, *others))[0]


def block_device(main_query, latent_keys, head_lse, lengths, index_query, index_key, index_weight):
    contexts = lax.axis_size("context")
    planes = contexts // 2
    partners = lax.axis_size("heads")
    context = lax.axis_index("context")
    rows, heads, _ = main_query.shape
    own_rows, index_heads, width = index_query.shape
    key_count = latent_keys.shape[0]
    flat = own_rows * index_heads

    def planes_move(array, pairs):
        return lax.ppermute(array, "context", [(2 * a + k, 2 * b + k) for a, b in pairs for k in (0, 1)])

    def context_flip(array, e):
        return lax.ppermute(array, "context", [(c, c ^ e) for c in range(contexts)])

    def heads_flip(array, e):
        return lax.ppermute(array, "heads", [(h, h ^ e) for h in range(partners)])

    keys_pair = context_flip(latent_keys.T, 1)
    pack, *inner = packed_queries(main_query)
    inner = [planes_move(block, [(1, 2), (2, 1), (0, 0), (3, 3)]) for block in inner]
    near = planes_move(pack, [(0, 1), (1, 0), (2, 3), (3, 2)])
    ends = planes_move(pack, [(0, 3), (3, 0)])
    lengths, lse, weight_wide, query, turned, index_key, keys = load_inputs(
        lengths, head_lse.T, index_weight, index_query, index_key, after(latent_keys, pack).T
    )
    keys = (keys, keys_pair)

    blocks = head_blocks(heads)

    def mass_of(pack, flip, blocks, *rest):
        return chunk_mass(lengths, pack, lse, keys, flip, blocks, rows, *rest)

    inner = [after(block, lse) for block in inner]
    far = [planes_move(block, [(0, 2), (3, 1), (1, 0), (2, 3)]) for block in inner]
    logits, masked, stats = index_logits(lengths, query.reshape(flat, width), index_key, weight_wide, own_rows)
    stats = merged_stats([stats, context_flip(stats, 1)])
    own_mass = mass_of(pack, 0, blocks, "mass_own")
    near_mass = mass_of(after(near, logits), 1, blocks, "mass_near", 100_000_000)
    across_mass = mass_of(picked(after(ends, own_mass, near_mass), inner), 3, blocks, "mass_across", 50_000_000)
    far_mass = mass_of(after(far[0], across_mass, stats), 2, blocks[:1], "mass_far", 1)
    shared = shared_mass(
        lengths, after(far[1], far_mass), lse, keys, own_mass, near_mass, across_mass, far_mass, blocks[1], partners
    )
    keep_mass, give_mass, stats = joined_mass(
        stats, shared[0], [heads_flip(shared[e], e) for e in (*reversed(range(1, partners - 1)), partners - 1)]
    )
    got_mass = context_flip(give_mass, 1)
    stats = merged_stats([stats] + [context_flip(stats, 2 * e) for e in reversed(range(1, planes))])
    back = (logits, turned, index_key, masked)
    query_grad, key_grad = back_own(lengths, stats, keep_mass, *back)
    *key_grads, keep, send = back_pair(
        lengths, context_flip(stats, 1), got_mass, *back, query_grad, key_grad, partners, planes
    )
    got = context_flip(send, 1)
    key_parts = [key_grads[0]] + [heads_flip(key_grads[e], e) for e in reversed(range(1, partners))]
    sums = pair_sums(keep, got)
    query_parts = [sums[0]] + [context_flip(sums[e], 2 * e) for e in reversed(range(1, planes))]
    return last_sums(key_parts, query_parts, (own_rows, index_heads // contexts, width))


def fits(mesh):
    return mesh.shape["context"] == 8 and mesh.shape["heads"] == 4


def solution(mesh):
    placed = (
        P("context", "heads", None),
        P("context", None),
        P(None, "heads"),
        P(),
        P("heads", None, None),
        P("context", None),
        P("heads", None),
    )
    return jax.shard_map(
        block_device if fits(mesh) else general_on_device,
        mesh=mesh,
        in_specs=placed,
        out_specs=(P("heads", "context", None), P(("context", "heads"), None)),
        check_vma=False,
    )
```

```python
import functools
import math

import jax
import jax.numpy as jnp
from jax import lax
from jax.experimental import pallas as pl
from jax.experimental.pallas import tpu as pltpu
from jax.sharding import PartitionSpec as P

main_scale = 192.0 ** (-0.5)
loss_scale = 64.0
masked_low = -1e30
log2_e = math.log2(math.e)
lanes = 128
vmem_bytes = 20 * 1024 * 1024
most_bytes = 60 * 1024 * 1024
load_bytes = 58 * 1024 * 1024

def joined(part, axis, combine):
    gathered = jax.tree.map(lambda a: lax.all_gather(a, axis), part)

    def take(source):
        return jax.tree.map(lambda a: lax.dynamic_index_in_dim(a, source, 0, False), gathered)

    return lax.fori_loop(
        1, lax.axis_size(axis), lambda source, state: combine(state, take(source)), take(0)
    )


def head_mass(queries, lse_rows, len_rows, latent, first_key):
    row_count = queries.shape[0]
    block_rows = math.gcd(row_count, 64)
    steps_count = row_count // block_rows
    key_pos = first_key + jnp.arange(latent.shape[0], dtype=jnp.int32)

    def one_block(inputs):
        query_block, lse_block, len_block = inputs
        scores = (
            jnp.einsum("rhd,sd->rhs", query_block, latent, preferred_element_type=jnp.float32)
            * main_scale
        )
        summed = jnp.sum(jnp.exp(scores - lse_block[:, :, None]), axis=1)
        return jnp.where(key_pos[None, :] < len_block[:, None], summed, 0.0)

    stacked = lax.map(
        one_block,
        (
            queries.reshape((steps_count, block_rows) + queries.shape[1:]),
            lse_rows.reshape(steps_count, block_rows, lse_rows.shape[1]),
            len_rows.reshape(steps_count, block_rows),
        ),
    )
    return stacked.reshape(row_count, latent.shape[0])


def general_on_device(main_query, latent_keys, head_lse, lengths, index_query, index_key, index_weight):
    key_count = latent_keys.shape[0]
    first_key = lax.axis_index("context") * key_count
    own_rows = index_query.shape[0]
    row_first = lax.axis_index("heads") * own_rows
    partial_mass = head_mass(
        lax.all_gather(main_query, "context", axis=0, tiled=True),
        head_lse,
        lengths,
        latent_keys,
        first_key,
    )
    summed_mass = lax.psum(partial_mass, "heads")
    row_mass = lax.dynamic_slice_in_dim(summed_mass, row_first, own_rows, 0)
    own_len = lax.dynamic_slice_in_dim(lengths, row_first, own_rows, 0)
    visible = (first_key + jnp.arange(key_count, dtype=jnp.int32))[None, :] < own_len[:, None]
    heads_count = index_query.shape[1]
    width = index_query.shape[2]
    index_scale = width ** (-0.5)
    flat_query = index_query.reshape(own_rows * heads_count, width)
    block_keys = math.gcd(key_count, 512)
    block_total = key_count // block_keys
    key_blocks = index_key.reshape(block_total, block_keys, width)

    def block_dots(key_block):
        products = lax.dot_general(
            flat_query, key_block, (((1,), (1,)), ((), ())), preferred_element_type=jnp.float32
        )
        return products.reshape(own_rows, heads_count, key_block.shape[0])

    def block_logits(key_block):
        return (
            jnp.einsum(
                "tj,tjs->ts",
                index_weight,
                jax.nn.relu(block_dots(key_block)),
                precision=lax.Precision.HIGHEST,
            )
            * index_scale
        )

    logits = jnp.moveaxis(lax.map(block_logits, key_blocks), 0, 1).reshape(own_rows, key_count)
    local_top = jnp.max(jnp.where(visible, logits, masked_low), axis=1)
    mass_local = jnp.sum(row_mass, axis=1)
    local_exp = jnp.where(visible, jnp.exp(logits - local_top[:, None]), 0.0)

    def combine(first, second):
        highest = jnp.maximum(first[0], second[0])
        merged = first[1] * jnp.exp(first[0] - highest) + second[1] * jnp.exp(second[0] - highest)
        return (highest, merged, first[2] + second[2])

    top, share_sum, mass_total = joined(
        (local_top, jnp.sum(local_exp, axis=1), mass_local), "context", combine
    )
    weights_exp = jnp.where(visible, jnp.exp(logits - top[:, None]), 0.0)
    probability = weights_exp / share_sum[:, None]
    target = row_mass / mass_total[:, None]
    slopes = loss_scale * (probability - target)
    slope_blocks = slopes.reshape(own_rows, block_total, block_keys).transpose(1, 0, 2)

    def back_step(query_grad, inputs):
        key_block, slope_block = inputs
        products = block_dots(key_block)
        terms = jnp.where(
            products > 0, slope_block[:, None, :] * index_weight[:, :, None] * index_scale, 0.0
        )
        terms = terms.astype(jnp.bfloat16).reshape(own_rows * heads_count, key_block.shape[0])
        query_grad = query_grad + jnp.dot(terms, key_block, preferred_element_type=jnp.float32)
        key_grad = lax.dot_general(
            terms, flat_query, (((0,), (0,)), ((), ())), preferred_element_type=jnp.float32
        )
        return (query_grad, key_grad)

    start_grad = jnp.zeros((own_rows * heads_count, width), jnp.float32)
    query_grad, key_grads = lax.scan(back_step, start_grad, (key_blocks, slope_blocks))
    query_grad = query_grad.reshape(own_rows, heads_count, width)
    key_grad = key_grads.reshape(key_count, width)
    out_query = lax.psum_scatter(query_grad, "context", scatter_dimension=1, tiled=True)
    out_key = lax.psum_scatter(key_grad, "heads", scatter_dimension=0, tiled=True)
    return (out_query, out_key)


def local_call(kernel, out_shape, name, grid=None, in_specs=None, out_specs=None, scratch=(), flops=1, moved=0, room=vmem_bytes):
    settings = dict(
        out_shape=out_shape,
        scratch_shapes=list(scratch),
        name=name,
        compiler_params=pltpu.CompilerParams(vmem_limit_bytes=room),
        cost_estimate=pl.CostEstimate(flops=flops, bytes_accessed=1, transcendentals=0),
    )
    if grid is not None:
        settings["grid"] = grid
    if in_specs is not None:
        settings["in_specs"] = in_specs
    if out_specs is not None:
        settings["out_specs"] = out_specs
    return pl.pallas_call(kernel, **settings)


def whole():
    return pl.BlockSpec(memory_space=pltpu.VMEM)


def scalars():
    return pl.BlockSpec(memory_space=pltpu.SMEM)


def fixed(shape):
    return pl.BlockSpec(shape, lambda step: (0,) * len(shape))


def f32(shape):
    return jax.ShapeDtypeStruct(shape, jnp.float32)


def bf16(shape):
    return jax.ShapeDtypeStruct(shape, jnp.bfloat16)


def place():
    context = lax.axis_index("context")
    return context >> 1, context & 1, lax.axis_index("heads")


def hbm():
    return pl.BlockSpec(memory_space=pltpu.HBM)


def head_blocks(heads):
    first = heads * 5 // 8
    return ((0, first), (first, heads - first))


def packed_rows(rows, heads, width):
    return rows * heads * width // lanes


def pack_kernel(query_ref, out_ref, *block_refs):
    rows, heads, width = query_ref.shape
    columns = width // lanes
    stacked = jnp.swapaxes(query_ref[...].astype(jnp.float32), 0, 1).reshape(rows * heads, width)
    begin = 0
    for (first, count), block_ref in zip(head_blocks(heads), block_refs):
        total = rows * count
        block = stacked[rows * first : rows * first + total]
        rest = block[:, columns * lanes :]
        pieces = [block[:, i * lanes : (i + 1) * lanes] for i in range(columns)]
        pieces.append(jnp.concatenate([rest[: total // 2], rest[total // 2 :]], axis=1))
        place = 0
        for piece in pieces:
            piece = piece.astype(jnp.bfloat16)
            size = piece.shape[0]
            out_ref[begin + place : begin + place + size, :] = piece
            block_ref[place : place + size, :] = piece
            place += size
        begin += place


def packed_queries(queries):
    rows, heads, width = queries.shape
    blocks = [bf16((packed_rows(rows, count, width), lanes)) for _, count in head_blocks(heads)]
    return local_call(
        pack_kernel,
        [bf16((packed_rows(rows, heads, width), lanes))] + blocks,
        "pack_queries",
        in_specs=[whole()],
        out_specs=[whole()] * (1 + len(blocks)),
        flops=30_000_000_000,
    )(queries)


def pick_kernel(ends_ref, *refs):
    inner_refs, out_ref = refs[:-1], refs[-1]
    plane, _, _ = place()
    inner = (plane == 1) | (plane == 2)

    @pl.when(inner)
    def _():
        begin = 0
        for inner_ref in inner_refs:
            rows = inner_ref.shape[0]
            out_ref[begin : begin + rows, :] = inner_ref[...]
            begin += rows

    @pl.when(jnp.logical_not(inner))
    def _():
        out_ref[...] = ends_ref[...]


def picked(ends, inner):
    return local_call(
        pick_kernel,
        bf16(ends.shape),
        "pick_queries",
        in_specs=[whole()] * (1 + len(inner)),
        out_specs=whole(),
    )(ends, *inner)


def unpack(packed_ref, begin, wide_ref, row, total):
    width = wide_ref.shape[1]
    columns = width // lanes
    half = total // 2
    for i in range(columns):
        wide_ref[row : row + total, i * lanes : (i + 1) * lanes] = packed_ref[
            begin + i * total : begin + (i + 1) * total, :
        ]
    rest = packed_ref[begin + columns * total : begin + columns * total + half, :]
    wide_ref[row : row + half, columns * lanes :] = rest[:, : lanes // 2]
    wide_ref[row + half : row + total, columns * lanes :] = rest[:, lanes // 2 :]


def widened(column, width):
    return jnp.concatenate([column] * (width // lanes), axis=1)


def rows_at(ref, index, rows):
    return ref[pl.ds(pl.multiple_of(index * rows, rows), rows), :]


def visible_tile(length_ref, block, rows, first, width, key_count):
    positions = lax.axis_index("context") * key_count + first + lax.broadcasted_iota(jnp.int32, (rows, width), 1)
    return positions < widened(rows_at(length_ref, block, rows), width)


def chip_mass(length_ref, wide_ref, lse_ref, own_key_ref, pair_key_ref, context, heads, out_ref, before_ref=None):
    width, key_count = own_key_ref.shape
    first_head, head_count = heads
    rows = wide_ref.shape[0] // head_count
    tile = math.gcd(key_count, 512)
    plane, core, _ = place()
    lse = rows_at(lse_ref, context, rows)
    column = widened(rows_at(length_ref, context, rows), tile)
    spread = lax.broadcasted_iota(jnp.int32, (rows, tile), 1)
    for key_ref, half in ((own_key_ref, core), (pair_key_ref, 1 - core)):
        for first in range(0, key_count, tile):
            scores = jnp.dot(wide_ref[...], key_ref[:, first : first + tile], preferred_element_type=jnp.float32)
            summed = jnp.zeros((rows, tile), jnp.float32)
            for h in range(head_count):
                summed = summed + jnp.exp2(
                    scores[h * rows : (h + 1) * rows] * (main_scale * log2_e)
                    - lse[:, first_head + h : first_head + h + 1]
                )
            visible = (2 * plane + half) * key_count + first + spread < column
            mass = jnp.where(visible, summed, 0.0)
            columns = pl.ds(pl.multiple_of(half * key_count + first, tile), tile)
            if before_ref is not None:
                mass = mass + before_ref[:, columns]
            out_ref[:, columns] = mass


def mass_kernel(flip, blocks, length_ref, pack_ref, lse_ref, own_key_ref, pair_key_ref, out_ref, wide_ref):
    plane, core, _ = place()
    heads = (blocks[0][0], sum(count for _, count in blocks))
    rows = wide_ref.shape[0] // heads[1]
    begin = row = 0
    for _, count in blocks:
        unpack(pack_ref, begin, wide_ref, row, rows * count)
        begin += packed_rows(rows, count, wide_ref.shape[1])
        row += rows * count
    chip_mass(length_ref, wide_ref, lse_ref, own_key_ref, pair_key_ref, 2 * (plane ^ flip) + core, heads, out_ref)


def chunk_mass(lengths, pack, lse, keys, flip, blocks, rows, name, flops=1):
    width, key_count = keys[0].shape
    total = rows * sum(count for _, count in blocks)
    return local_call(
        functools.partial(mass_kernel, flip, blocks),
        f32((rows, 2 * key_count)),
        name,
        in_specs=[whole()] * 5,
        out_specs=whole(),
        scratch=[pltpu.VMEM((total, width), jnp.bfloat16)],
        flops=flops,
    )(lengths, pack, lse, *keys)


def share_kernel(
    heads, length_ref, pack_ref, lse_ref, own_key_ref, pair_key_ref, own_ref, near_ref, across_ref, before_ref, *refs
):
    outs = refs[:-2]
    wide_ref, chunks_ref = refs[-2:]
    plane, core, group = place()
    unpack(pack_ref, 0, wide_ref, 0, wide_ref.shape[0])
    chunks_ref[0] = own_ref[...]
    chunks_ref[1] = near_ref[...]
    chunks_ref[3] = across_ref[...]
    chip_mass(
        length_ref, wide_ref, lse_ref, own_key_ref, pair_key_ref, 2 * (plane ^ 2) + core, heads, chunks_ref.at[2],
        before_ref,
    )
    for e, out_ref in enumerate(outs):
        out_ref[...] = chunks_ref[plane ^ group ^ e].astype(out_ref.dtype)


def shared_mass(lengths, pack, lse, keys, own, near, across, before, heads, partners):
    width, _ = keys[0].shape
    rows, both = own.shape
    return local_call(
        functools.partial(share_kernel, heads),
        [f32((rows, both))] + [bf16((rows, both))] * (partners - 1),
        "mass_and_share",
        in_specs=[whole()] * 9,
        out_specs=[whole()] * partners,
        scratch=[pltpu.VMEM((rows * heads[1], width), jnp.bfloat16), pltpu.VMEM((4, rows, both), jnp.float32)],
    )(lengths, pack, lse, *keys, own, near, across, before)


def logits_kernel(length_ref, query_ref, key_ref, weight_ref, logits_ref, masked_ref, stats_ref):
    rows, key_count = logits_ref.shape
    heads = query_ref.shape[0] // rows
    tile = math.gcd(key_count, 256)
    group = lax.axis_index("heads")
    best = jnp.full((rows, 1), masked_low, jnp.float32)
    weights = widened(weight_ref[...], tile)
    for first in range(0, key_count, tile):
        dots = lax.dot_general(
            query_ref[...], key_ref[first : first + tile, :], (((1,), (1,)), ((), ())),
            preferred_element_type=jnp.float32,
        )
        masked = jnp.where(dots > 0, weights, 0.0)
        masked_ref[:, first : first + tile] = masked
        logits = jnp.sum((dots * masked).reshape(rows, heads, tile), axis=1)
        logits_ref[:, first : first + tile] = logits
        visible = visible_tile(length_ref, group, rows, first, tile, key_count)
        best = jnp.maximum(best, jnp.max(jnp.where(visible, logits, masked_low), axis=1, keepdims=True))
    visible = visible_tile(length_ref, group, rows, 0, key_count, key_count)
    total = jnp.sum(jnp.where(visible, jnp.exp(logits_ref[...] - best), 0.0), axis=1, keepdims=True)
    column = lax.broadcasted_iota(jnp.int32, (rows, lanes), 1)
    stats_ref[...] = jnp.where(column == 0, best, total)


def index_logits(lengths, flat_query, index_key, weight_wide, rows):
    key_count = index_key.shape[0]
    flat = flat_query.shape[0]
    return local_call(
        logits_kernel,
        [f32((rows, key_count)), f32((flat, key_count)), f32((rows, lanes))],
        "index_logits",
        in_specs=[whole()] * 4,
        out_specs=[whole()] * 3,
        moved=2 * index_key.size,
    )(lengths, flat_query, index_key, weight_wide)


def load_kernel(
    length_ref, lse_ref, weight_ref, query_hbm, key_hbm, latent_hbm,
    length_out, lse_out, weight_out, query_out, turned_out, key_out, latent_out, semaphores,
):
    copies = [
        pltpu.make_async_copy(source, target, semaphores.at[i])
        for i, (source, target) in enumerate(
            [(query_hbm, query_out), (key_hbm, key_out), (latent_hbm, latent_out)]
        )
    ]
    for copy in copies:
        copy.start()
    total = length_out.shape[0]
    spread = lax.broadcasted_iota(jnp.int32, (8, lanes), 0)
    for first in range(0, total, 8):
        column = jnp.zeros((8, lanes), jnp.int32)
        for i in range(8):
            column = jnp.where(spread == i, length_ref[first + i], column)
        length_out[first : first + 8, :] = column
    lse_out[...] = lse_ref[...].T * log2_e
    rows, heads = weight_ref.shape
    width = key_out.shape[1]
    weights = weight_ref[...].T * width ** (-0.5)
    for t in range(rows):
        weight_out[t * heads : (t + 1) * heads, :] = jnp.broadcast_to(weights[:, t : t + 1], (heads, lanes))
    copies[0].wait()
    turned_out[...] = query_out[...].reshape(rows * heads, width).astype(jnp.float32).T.astype(jnp.bfloat16)
    copies[1].wait()
    copies[2].wait()


def load_inputs(lengths, lse, weights, query, key, latent):
    rows, heads, width = query.shape
    flat = rows * heads
    return local_call(
        load_kernel,
        [
            jax.ShapeDtypeStruct((lengths.shape[0], lanes), jnp.int32),
            f32(lse.shape[::-1]),
            f32((flat, lanes)),
            bf16(query.shape),
            bf16((width, flat)),
            bf16(key.shape),
            bf16(latent.shape),
        ],
        "load_inputs",
        in_specs=[scalars(), whole(), whole(), hbm(), hbm(), hbm()],
        out_specs=[whole()] * 7,
        scratch=[pltpu.SemaphoreType.DMA((3,))],
        moved=4 * (key.size + latent.size),
    )(lengths, lse, weights, query, key, latent)


def join_kernel(stats_ref, own_ref, *refs):
    parts, (keep_ref, give_ref, out_ref) = refs[:-3], refs[-3:]
    mass = own_ref[...]
    for part in parts:
        mass = mass + part[...].astype(jnp.float32)
    rows, both = mass.shape
    low, high = mass[:, : both // 2], mass[:, both // 2 :]
    _, core, _ = place()
    keep_ref[...] = jnp.where(core == 0, low, high)
    give_ref[...] = jnp.where(core == 0, high, low)
    total = jnp.broadcast_to(jnp.sum(mass, axis=1, keepdims=True), (rows, lanes))
    nothing = jnp.zeros((rows, lanes), jnp.float32)
    totals = jnp.concatenate([jnp.where(core == 0, total, nothing), jnp.where(core == 0, nothing, total)], axis=0)
    column = lax.broadcasted_iota(jnp.int32, out_ref.shape, 1)
    out_ref[...] = jnp.where(column == 2, totals, stats_ref[...])


def joined_mass(stats, own, parts):
    rows, both = own.shape
    return local_call(
        join_kernel,
        [f32((rows, both // 2)), f32((rows, both // 2)), f32(stats.shape)],
        "join_mass",
        in_specs=[whole()] * (2 + len(parts)),
        out_specs=[whole()] * 3,
    )(stats, own, *parts)


def merge_kernel(*refs):
    out_ref = refs[-1]
    stats = [ref[...] for ref in refs[:-1]]
    top = functools.reduce(jnp.maximum, [s[:, 0:1] for s in stats])
    shares = sum(s[:, 1:2] * jnp.exp(s[:, 0:1] - top) for s in stats)
    column = lax.broadcasted_iota(jnp.int32, out_ref.shape, 1)
    out_ref[...] = jnp.where(column == 0, top, jnp.where(column == 1, shares, sum(stats)))


def merged_stats(stats):
    return local_call(
        merge_kernel, f32(stats[0].shape), "merge_stats", in_specs=[whole()] * len(stats), out_specs=whole()
    )(*stats)


def back_rows(half, length_ref, stats_ref, mass_ref, logits_ref, turned_ref, key_ref, masked_ref, slope_ref, store):
    rows, key_count = mass_ref.shape
    width = key_ref.shape[1]
    flat = turned_ref.shape[1] // 2
    tile = math.gcd(key_count, 256)
    stats = rows_at(stats_ref, half, rows)
    visible = visible_tile(length_ref, 2 * lax.axis_index("heads") + half, rows, 0, key_count, key_count)
    weights_exp = jnp.where(visible, jnp.exp(rows_at(logits_ref, half, rows) - stats[:, 0:1]), 0.0)
    slope_ref[...] = loss_scale * (weights_exp / stats[:, 1:2] - mass_ref[...] / stats[:, 2:3])
    begin = pl.multiple_of(half * flat, flat)
    turned = turned_ref[:, pl.ds(begin, flat)]
    query_grad = jnp.zeros((flat, width), jnp.float32)
    for first in range(0, key_count, tile):
        keys = key_ref[first : first + tile, :]
        slopes = jnp.broadcast_to(slope_ref[:, first : first + tile][:, None, :], (rows, flat // rows, tile))
        masked = masked_ref[pl.ds(begin, flat), first : first + tile]
        terms = (slopes.reshape(flat, tile) * masked).astype(jnp.bfloat16)
        query_grad = query_grad + jnp.dot(terms, keys, preferred_element_type=jnp.float32)
        store(first, tile, jnp.dot(turned, terms, preferred_element_type=jnp.float32))
    return query_grad


def back_own_kernel(
    length_ref, stats_ref, mass_ref, logits_ref, turned_ref, key_ref, masked_ref, query_out, key_out, slope_ref
):
    _, core, _ = place()

    def store(first, tile, key_grad):
        key_out[:, first : first + tile] = key_grad

    query_out[...] = back_rows(
        core, length_ref, stats_ref, mass_ref, logits_ref, turned_ref, key_ref, masked_ref, slope_ref, store
    )


def back_own(lengths, stats, mass, logits, turned, index_key, masked):
    rows, key_count = mass.shape
    width, flat = turned.shape
    return local_call(
        back_own_kernel,
        [f32((flat // 2, width)), f32((width, key_count))],
        "index_back_own",
        in_specs=[whole()] * 7,
        out_specs=[whole()] * 2,
        scratch=[pltpu.VMEM((rows, key_count), jnp.float32)],
    )(lengths, stats, mass, logits, turned, index_key, masked)


def back_pair_kernel(
    length_ref, stats_ref, mass_ref, logits_ref, turned_ref, key_ref, masked_ref, query_ref, before_ref, *refs
):
    partners = len(refs) - 4
    key_outs = refs[:partners]
    keep_ref, send_ref, slope_ref, grad_ref = refs[partners:]
    key_count, width = key_ref.shape
    _, core, group = place()

    def store(first, tile, key_grad):
        grad_ref[first : first + tile, :] = (before_ref[:, first : first + tile] + key_grad).T

    other = back_rows(
        1 - core, length_ref, stats_ref, mass_ref, logits_ref, turned_ref, key_ref, masked_ref, slope_ref, store
    )
    block = key_count // partners
    for e, out_ref in enumerate(key_outs):
        out_ref[...] = rows_at(grad_ref, group ^ e, block).astype(out_ref.dtype)
    planes, part, _ = keep_ref.shape
    rows = mass_ref.shape[0]
    for half, query_grad in ((core, query_ref[...]), (1 - core, other)):
        split = query_grad.reshape(rows, planes, 2, part // (2 * rows), width)
        place_of = pl.ds(pl.multiple_of(half * (part // 2), part // 2), part // 2)
        for plane in range(planes):
            low = split[:, plane, 0].reshape(part // 2, width)
            high = split[:, plane, 1].reshape(part // 2, width)
            keep_ref[plane, place_of, :] = jnp.where(core == 0, low, high)
            send_ref[plane, place_of, :] = jnp.where(core == 0, high, low).astype(jnp.bfloat16)


def back_pair(lengths, stats, mass, logits, turned, index_key, masked, query_grad, key_grad, partners, planes):
    rows, key_count = mass.shape
    width, flat = turned.shape
    part = flat // (2 * planes)
    return local_call(
        back_pair_kernel,
        [f32((key_count // partners, width))]
        + [bf16((key_count // partners, width))] * (partners - 1)
        + [f32((planes, part, width)), bf16((planes, part, width))],
        "index_back_pair",
        in_specs=[whole()] * 9,
        out_specs=[whole()] * (partners + 2),
        scratch=[pltpu.VMEM((rows, key_count), jnp.float32), pltpu.VMEM((key_count, width), jnp.float32)],
    )(lengths, stats, mass, logits, turned, index_key, masked, query_grad, key_grad)


def pair_kernel(keep_ref, got_ref, *outs):
    own_plane, _, _ = place()
    for e, out_ref in enumerate(outs):
        plane = own_plane ^ e
        out_ref[...] = (keep_ref[plane] + got_ref[plane].astype(jnp.float32)).astype(out_ref.dtype)


def pair_sums(keep, got):
    planes, part, width = keep.shape
    return local_call(
        pair_kernel,
        [f32((part, width))] + [bf16((part, width))] * (planes - 1),
        "pair_sums",
        in_specs=[whole(), whole()],
        out_specs=[whole()] * planes,
        moved=8 * keep.size,
    )(keep, got)


def last_kernel(key_parts, *refs):
    query_out, key_out = refs[-2:]
    key_refs, query_refs = refs[:key_parts], refs[key_parts:-2]
    key_out[...] = sum(ref[...].astype(jnp.float32) for ref in key_refs)
    query_out[...] = sum(ref[...].astype(jnp.float32) for ref in query_refs).reshape(query_out.shape)


def last_sums(key_parts, query_parts, query_shape):
    return local_call(
        functools.partial(last_kernel, len(key_parts)),
        [f32(query_shape), f32(key_parts[0].shape)],
        "last_sums",
        in_specs=[whole()] * (len(key_parts) + len(query_parts)),
        out_specs=[whole()] * 2,
        moved=8 * key_parts[0].size,
    )(*key_parts, *query_parts)


def after(array, *others):
    return lax.optimization_barrier((array, *others))[0]


def block_device(main_query, latent_keys, head_lse, lengths, index_query, index_key, index_weight):
    contexts = lax.axis_size("context")
    planes = contexts // 2
    partners = lax.axis_size("heads")
    context = lax.axis_index("context")
    rows, heads, _ = main_query.shape
    own_rows, index_heads, width = index_query.shape
    key_count = latent_keys.shape[0]
    flat = own_rows * index_heads

    def planes_move(array, pairs):
        return lax.ppermute(array, "context", [(2 * a + k, 2 * b + k) for a, b in pairs for k in (0, 1)])

    def context_flip(array, e):
        return lax.ppermute(array, "context", [(c, c ^ e) for c in range(contexts)])

    def heads_flip(array, e):
        return lax.ppermute(array, "heads", [(h, h ^ e) for h in range(partners)])

    keys_pair = context_flip(latent_keys.T, 1)
    pack, *inner = packed_queries(main_query)
    inner = [planes_move(block, [(1, 2), (2, 1), (0, 0), (3, 3)]) for block in inner]
    near = planes_move(pack, [(0, 1), (1, 0), (2, 3), (3, 2)])
    ends = planes_move(pack, [(0, 3), (3, 0)])
    lengths, lse, weight_wide, query, turned, index_key, keys = load_inputs(
        lengths, head_lse.T, index_weight, index_query, index_key, after(latent_keys, pack).T
    )
    keys = (keys, keys_pair)

    blocks = head_blocks(heads)

    def mass_of(pack, flip, blocks, *rest):
        return chunk_mass(lengths, pack, lse, keys, flip, blocks, rows, *rest)

    inner = [after(block, lse) for block in inner]
    far = [planes_move(block, [(0, 2), (3, 1), (1, 0), (2, 3)]) for block in inner]
    logits, masked, stats = index_logits(lengths, query.reshape(flat, width), index_key, weight_wide, own_rows)
    stats = merged_stats([stats, context_flip(stats, 1)])
    own_mass = mass_of(pack, 0, blocks, "mass_own")
    near_mass = mass_of(after(near, logits), 1, blocks, "mass_near", 100_000_000)
    across_mass = mass_of(picked(after(ends, own_mass, near_mass), inner), 3, blocks, "mass_across", 50_000_000)
    far_mass = mass_of(after(far[0], across_mass, stats), 2, blocks[:1], "mass_far", 1)
    shared = shared_mass(
        lengths, after(far[1], far_mass), lse, keys, own_mass, near_mass, across_mass, far_mass, blocks[1], partners
    )
    keep_mass, give_mass, stats = joined_mass(
        stats, shared[0], [heads_flip(shared[e], e) for e in (*reversed(range(1, partners - 1)), partners - 1)]
    )
    got_mass = context_flip(give_mass, 1)
    stats = merged_stats([stats] + [context_flip(stats, 2 * e) for e in reversed(range(1, planes))])
    back = (logits, turned, index_key, masked)
    query_grad, key_grad = back_own(lengths, stats, keep_mass, *back)
    *key_grads, keep, send = back_pair(
        lengths, context_flip(stats, 1), got_mass, *back, query_grad, key_grad, partners, planes
    )
    got = context_flip(send, 1)
    key_parts = [key_grads[0]] + [heads_flip(key_grads[e], e) for e in range(1, partners)]
    sums = pair_sums(keep, got)
    query_parts = [sums[0]] + [context_flip(sums[e], 2 * e) for e in reversed(range(1, planes))]
    return last_sums(key_parts, query_parts, (own_rows, index_heads // contexts, width))


def fits(mesh):
    return mesh.shape["context"] == 8 and mesh.shape["heads"] == 4


def solution(mesh):
    placed = (
        P("context", "heads", None),
        P("context", None),
        P(None, "heads"),
        P(),
        P("heads", None, None),
        P("context", None),
        P("heads", None),
    )
    return jax.shard_map(
        block_device if fits(mesh) else general_on_device,
        mesh=mesh,
        in_specs=placed,
        out_specs=(P("heads", "context", None), P(("context", "heads"), None)),
        check_vma=False,
    )
```

```python
import functools
import math

import jax
import jax.numpy as jnp
from jax import lax
from jax.experimental import pallas as pl
from jax.experimental.pallas import tpu as pltpu
from jax.sharding import PartitionSpec as P

main_scale = 192.0 ** (-0.5)
loss_scale = 64.0
masked_low = -1e30
log2_e = math.log2(math.e)
lanes = 128
vmem_bytes = 20 * 1024 * 1024

def joined(part, axis, combine):
    gathered = jax.tree.map(lambda a: lax.all_gather(a, axis), part)

    def take(source):
        return jax.tree.map(lambda a: lax.dynamic_index_in_dim(a, source, 0, False), gathered)

    return lax.fori_loop(
        1, lax.axis_size(axis), lambda source, state: combine(state, take(source)), take(0)
    )


def head_mass(queries, lse_rows, len_rows, latent, first_key):
    row_count = queries.shape[0]
    block_rows = math.gcd(row_count, 64)
    steps_count = row_count // block_rows
    key_pos = first_key + jnp.arange(latent.shape[0], dtype=jnp.int32)

    def one_block(inputs):
        query_block, lse_block, len_block = inputs
        scores = (
            jnp.einsum("rhd,sd->rhs", query_block, latent, preferred_element_type=jnp.float32)
            * main_scale
        )
        summed = jnp.sum(jnp.exp(scores - lse_block[:, :, None]), axis=1)
        return jnp.where(key_pos[None, :] < len_block[:, None], summed, 0.0)

    stacked = lax.map(
        one_block,
        (
            queries.reshape((steps_count, block_rows) + queries.shape[1:]),
            lse_rows.reshape(steps_count, block_rows, lse_rows.shape[1]),
            len_rows.reshape(steps_count, block_rows),
        ),
    )
    return stacked.reshape(row_count, latent.shape[0])


def general_on_device(main_query, latent_keys, head_lse, lengths, index_query, index_key, index_weight):
    key_count = latent_keys.shape[0]
    first_key = lax.axis_index("context") * key_count
    own_rows = index_query.shape[0]
    row_first = lax.axis_index("heads") * own_rows
    partial_mass = head_mass(
        lax.all_gather(main_query, "context", axis=0, tiled=True),
        head_lse,
        lengths,
        latent_keys,
        first_key,
    )
    summed_mass = lax.psum(partial_mass, "heads")
    row_mass = lax.dynamic_slice_in_dim(summed_mass, row_first, own_rows, 0)
    own_len = lax.dynamic_slice_in_dim(lengths, row_first, own_rows, 0)
    visible = (first_key + jnp.arange(key_count, dtype=jnp.int32))[None, :] < own_len[:, None]
    heads_count = index_query.shape[1]
    width = index_query.shape[2]
    index_scale = width ** (-0.5)
    flat_query = index_query.reshape(own_rows * heads_count, width)
    block_keys = math.gcd(key_count, 512)
    block_total = key_count // block_keys
    key_blocks = index_key.reshape(block_total, block_keys, width)

    def block_dots(key_block):
        products = lax.dot_general(
            flat_query, key_block, (((1,), (1,)), ((), ())), preferred_element_type=jnp.float32
        )
        return products.reshape(own_rows, heads_count, key_block.shape[0])

    def block_logits(key_block):
        return (
            jnp.einsum(
                "tj,tjs->ts",
                index_weight,
                jax.nn.relu(block_dots(key_block)),
                precision=lax.Precision.HIGHEST,
            )
            * index_scale
        )

    logits = jnp.moveaxis(lax.map(block_logits, key_blocks), 0, 1).reshape(own_rows, key_count)
    local_top = jnp.max(jnp.where(visible, logits, masked_low), axis=1)
    mass_local = jnp.sum(row_mass, axis=1)
    local_exp = jnp.where(visible, jnp.exp(logits - local_top[:, None]), 0.0)

    def combine(first, second):
        highest = jnp.maximum(first[0], second[0])
        merged = first[1] * jnp.exp(first[0] - highest) + second[1] * jnp.exp(second[0] - highest)
        return (highest, merged, first[2] + second[2])

    top, share_sum, mass_total = joined(
        (local_top, jnp.sum(local_exp, axis=1), mass_local), "context", combine
    )
    weights_exp = jnp.where(visible, jnp.exp(logits - top[:, None]), 0.0)
    probability = weights_exp / share_sum[:, None]
    target = row_mass / mass_total[:, None]
    slopes = loss_scale * (probability - target)
    slope_blocks = slopes.reshape(own_rows, block_total, block_keys).transpose(1, 0, 2)

    def back_step(query_grad, inputs):
        key_block, slope_block = inputs
        products = block_dots(key_block)
        terms = jnp.where(
            products > 0, slope_block[:, None, :] * index_weight[:, :, None] * index_scale, 0.0
        )
        terms = terms.astype(jnp.bfloat16).reshape(own_rows * heads_count, key_block.shape[0])
        query_grad = query_grad + jnp.dot(terms, key_block, preferred_element_type=jnp.float32)
        key_grad = lax.dot_general(
            terms, flat_query, (((0,), (0,)), ((), ())), preferred_element_type=jnp.float32
        )
        return (query_grad, key_grad)

    start_grad = jnp.zeros((own_rows * heads_count, width), jnp.float32)
    query_grad, key_grads = lax.scan(back_step, start_grad, (key_blocks, slope_blocks))
    query_grad = query_grad.reshape(own_rows, heads_count, width)
    key_grad = key_grads.reshape(key_count, width)
    out_query = lax.psum_scatter(query_grad, "context", scatter_dimension=1, tiled=True)
    out_key = lax.psum_scatter(key_grad, "heads", scatter_dimension=0, tiled=True)
    return (out_query, out_key)


def local_call(kernel, out_shape, name, in_specs, out_specs, scratch=(), flops=1):
    return pl.pallas_call(
        kernel,
        out_shape=out_shape,
        in_specs=in_specs,
        out_specs=out_specs,
        scratch_shapes=list(scratch),
        name=name,
        compiler_params=pltpu.CompilerParams(vmem_limit_bytes=vmem_bytes),
        cost_estimate=pl.CostEstimate(flops=flops, bytes_accessed=1, transcendentals=0),
    )


def whole():
    return pl.BlockSpec(memory_space=pltpu.VMEM)


def scalars():
    return pl.BlockSpec(memory_space=pltpu.SMEM)


def f32(shape):
    return jax.ShapeDtypeStruct(shape, jnp.float32)


def bf16(shape):
    return jax.ShapeDtypeStruct(shape, jnp.bfloat16)


def place():
    context = lax.axis_index("context")
    return context >> 1, context & 1, lax.axis_index("heads")


def hbm():
    return pl.BlockSpec(memory_space=pltpu.HBM)


def head_blocks(heads):
    first = heads * 5 // 8
    return ((0, first), (first, heads - first))


def packed_rows(rows, heads, width):
    return rows * heads * width // lanes


def pack_kernel(query_ref, out_ref, *block_refs):
    rows, heads, width = query_ref.shape
    columns = width // lanes
    stacked = jnp.swapaxes(query_ref[...].astype(jnp.float32), 0, 1).reshape(rows * heads, width)
    begin = 0
    for (first, count), block_ref in zip(head_blocks(heads), block_refs):
        total = rows * count
        block = stacked[rows * first : rows * first + total]
        rest = block[:, columns * lanes :]
        pieces = [block[:, i * lanes : (i + 1) * lanes] for i in range(columns)]
        pieces.append(jnp.concatenate([rest[: total // 2], rest[total // 2 :]], axis=1))
        place = 0
        for piece in pieces:
            piece = piece.astype(jnp.bfloat16)
            size = piece.shape[0]
            out_ref[begin + place : begin + place + size, :] = piece
            block_ref[place : place + size, :] = piece
            place += size
        begin += place


def packed_queries(queries):
    rows, heads, width = queries.shape
    blocks = [bf16((packed_rows(rows, count, width), lanes)) for _, count in head_blocks(heads)]
    return local_call(
        pack_kernel,
        [bf16((packed_rows(rows, heads, width), lanes))] + blocks,
        "pack_queries",
        in_specs=[whole()],
        out_specs=[whole()] * (1 + len(blocks)),
        flops=30_000_000_000,
    )(queries)


def pick_kernel(ends_ref, *refs):
    inner_refs, out_ref = refs[:-1], refs[-1]
    plane, _, _ = place()
    inner = (plane == 1) | (plane == 2)

    @pl.when(inner)
    def _():
        begin = 0
        for inner_ref in inner_refs:
            rows = inner_ref.shape[0]
            out_ref[begin : begin + rows, :] = inner_ref[...]
            begin += rows

    @pl.when(jnp.logical_not(inner))
    def _():
        out_ref[...] = ends_ref[...]


def picked(ends, inner):
    return local_call(
        pick_kernel,
        bf16(ends.shape),
        "pick_queries",
        in_specs=[whole()] * (1 + len(inner)),
        out_specs=whole(),
    )(ends, *inner)


def unpack(packed_ref, begin, wide_ref, row, total):
    width = wide_ref.shape[1]
    columns = width // lanes
    half = total // 2
    for i in range(columns):
        wide_ref[row : row + total, i * lanes : (i + 1) * lanes] = packed_ref[
            begin + i * total : begin + (i + 1) * total, :
        ]
    rest = packed_ref[begin + columns * total : begin + columns * total + half, :]
    wide_ref[row : row + half, columns * lanes :] = rest[:, : lanes // 2]
    wide_ref[row + half : row + total, columns * lanes :] = rest[:, lanes // 2 :]


def widened(column, width):
    return jnp.concatenate([column] * (width // lanes), axis=1)


def rows_at(ref, index, rows):
    return ref[pl.ds(pl.multiple_of(index * rows, rows), rows), :]


def visible_tile(length_ref, block, rows, first, width, key_count):
    positions = lax.axis_index("context") * key_count + first + lax.broadcasted_iota(jnp.int32, (rows, width), 1)
    return positions < widened(rows_at(length_ref, block, rows), width)


def chip_mass(length_ref, wide_ref, lse_ref, own_key_ref, pair_key_ref, context, heads, out_ref, before_ref=None):
    width, key_count = own_key_ref.shape
    first_head, head_count = heads
    rows = wide_ref.shape[0] // head_count
    tile = math.gcd(key_count, 512)
    plane, core, _ = place()
    lse = rows_at(lse_ref, context, rows)
    column = widened(rows_at(length_ref, context, rows), tile)
    spread = lax.broadcasted_iota(jnp.int32, (rows, tile), 1)
    for key_ref, half in ((own_key_ref, core), (pair_key_ref, 1 - core)):
        for first in range(0, key_count, tile):
            scores = jnp.dot(wide_ref[...], key_ref[:, first : first + tile], preferred_element_type=jnp.float32)
            summed = jnp.zeros((rows, tile), jnp.float32)
            for h in range(head_count):
                summed = summed + jnp.exp2(
                    scores[h * rows : (h + 1) * rows] * (main_scale * log2_e)
                    - lse[:, first_head + h : first_head + h + 1]
                )
            visible = (2 * plane + half) * key_count + first + spread < column
            mass = jnp.where(visible, summed, 0.0)
            columns = pl.ds(pl.multiple_of(half * key_count + first, tile), tile)
            if before_ref is not None:
                mass = mass + before_ref[:, columns]
            out_ref[:, columns] = mass


def mass_kernel(flip, blocks, length_ref, pack_ref, lse_ref, own_key_ref, pair_key_ref, out_ref, wide_ref):
    plane, core, _ = place()
    heads = (blocks[0][0], sum(count for _, count in blocks))
    rows = wide_ref.shape[0] // heads[1]
    begin = row = 0
    for _, count in blocks:
        unpack(pack_ref, begin, wide_ref, row, rows * count)
        begin += packed_rows(rows, count, wide_ref.shape[1])
        row += rows * count
    chip_mass(length_ref, wide_ref, lse_ref, own_key_ref, pair_key_ref, 2 * (plane ^ flip) + core, heads, out_ref)


def chunk_mass(lengths, pack, lse, keys, flip, blocks, rows, name):
    width, key_count = keys[0].shape
    total = rows * sum(count for _, count in blocks)
    return local_call(
        functools.partial(mass_kernel, flip, blocks),
        f32((rows, 2 * key_count)),
        name,
        in_specs=[whole()] * 5,
        out_specs=whole(),
        scratch=[pltpu.VMEM((total, width), jnp.bfloat16)],
    )(lengths, pack, lse, *keys)


def share_kernel(
    heads, length_ref, pack_ref, lse_ref, own_key_ref, pair_key_ref, own_ref, near_ref, across_ref, before_ref, *refs
):
    outs = refs[:-2]
    wide_ref, chunks_ref = refs[-2:]
    plane, core, group = place()
    unpack(pack_ref, 0, wide_ref, 0, wide_ref.shape[0])
    chunks_ref[0] = own_ref[...]
    chunks_ref[1] = near_ref[...]
    chunks_ref[3] = across_ref[...]
    chip_mass(
        length_ref, wide_ref, lse_ref, own_key_ref, pair_key_ref, 2 * (plane ^ 2) + core, heads, chunks_ref.at[2],
        before_ref,
    )
    for e, out_ref in enumerate(outs):
        out_ref[...] = chunks_ref[plane ^ group ^ e].astype(out_ref.dtype)


def shared_mass(lengths, pack, lse, keys, own, near, across, before, heads, partners):
    width, _ = keys[0].shape
    rows, both = own.shape
    return local_call(
        functools.partial(share_kernel, heads),
        [f32((rows, both))] + [bf16((rows, both))] * (partners - 1),
        "mass_and_share",
        in_specs=[whole()] * 9,
        out_specs=[whole()] * partners,
        scratch=[pltpu.VMEM((rows * heads[1], width), jnp.bfloat16), pltpu.VMEM((4, rows, both), jnp.float32)],
    )(lengths, pack, lse, *keys, own, near, across, before)


def logits_kernel(length_ref, query_ref, key_ref, weight_ref, logits_ref, masked_ref, stats_ref):
    rows, key_count = logits_ref.shape
    heads = query_ref.shape[0] // rows
    tile = math.gcd(key_count, 256)
    group = lax.axis_index("heads")
    best = jnp.full((rows, 1), masked_low, jnp.float32)
    weights = widened(weight_ref[...], tile)
    for first in range(0, key_count, tile):
        dots = lax.dot_general(
            query_ref[...], key_ref[first : first + tile, :], (((1,), (1,)), ((), ())),
            preferred_element_type=jnp.float32,
        )
        masked = jnp.where(dots > 0, weights, 0.0)
        masked_ref[:, first : first + tile] = masked
        logits = jnp.sum((dots * masked).reshape(rows, heads, tile), axis=1)
        logits_ref[:, first : first + tile] = logits
        visible = visible_tile(length_ref, group, rows, first, tile, key_count)
        best = jnp.maximum(best, jnp.max(jnp.where(visible, logits, masked_low), axis=1, keepdims=True))
    visible = visible_tile(length_ref, group, rows, 0, key_count, key_count)
    total = jnp.sum(jnp.where(visible, jnp.exp(logits_ref[...] - best), 0.0), axis=1, keepdims=True)
    column = lax.broadcasted_iota(jnp.int32, (rows, lanes), 1)
    stats_ref[...] = jnp.where(column == 0, best, total)


def index_logits(lengths, flat_query, index_key, weight_wide, rows):
    key_count = index_key.shape[0]
    flat = flat_query.shape[0]
    return local_call(
        logits_kernel,
        [f32((rows, key_count)), f32((flat, key_count)), f32((rows, lanes))],
        "index_logits",
        in_specs=[whole()] * 4,
        out_specs=[whole()] * 3,
    )(lengths, flat_query, index_key, weight_wide)


def load_kernel(
    length_ref, lse_ref, weight_ref, query_hbm, key_hbm, latent_hbm,
    length_out, lse_out, weight_out, query_out, turned_out, key_out, latent_out, semaphores,
):
    copies = [
        pltpu.make_async_copy(source, target, semaphores.at[i])
        for i, (source, target) in enumerate(
            [(query_hbm, query_out), (key_hbm, key_out), (latent_hbm, latent_out)]
        )
    ]
    for copy in copies:
        copy.start()
    total = length_out.shape[0]
    spread = lax.broadcasted_iota(jnp.int32, (8, lanes), 0)
    for first in range(0, total, 8):
        column = jnp.zeros((8, lanes), jnp.int32)
        for i in range(8):
            column = jnp.where(spread == i, length_ref[first + i], column)
        length_out[first : first + 8, :] = column
    lse_out[...] = lse_ref[...].T * log2_e
    rows, heads = weight_ref.shape
    width = key_out.shape[1]
    weights = weight_ref[...].T * width ** (-0.5)
    for t in range(rows):
        weight_out[t * heads : (t + 1) * heads, :] = jnp.broadcast_to(weights[:, t : t + 1], (heads, lanes))
    copies[0].wait()
    turned_out[...] = query_out[...].reshape(rows * heads, width).astype(jnp.float32).T.astype(jnp.bfloat16)
    copies[1].wait()
    copies[2].wait()


def load_inputs(lengths, lse, weights, query, key, latent):
    rows, heads, width = query.shape
    flat = rows * heads
    return local_call(
        load_kernel,
        [
            jax.ShapeDtypeStruct((lengths.shape[0], lanes), jnp.int32),
            f32(lse.shape[::-1]),
            f32((flat, lanes)),
            bf16(query.shape),
            bf16((width, flat)),
            bf16(key.shape),
            bf16(latent.shape),
        ],
        "load_inputs",
        in_specs=[scalars(), whole(), whole(), hbm(), hbm(), hbm()],
        out_specs=[whole()] * 7,
        scratch=[pltpu.SemaphoreType.DMA((3,))],
    )(lengths, lse, weights, query, key, latent)


def join_kernel(stats_ref, own_ref, *refs):
    parts, (keep_ref, give_ref, out_ref) = refs[:-3], refs[-3:]
    mass = own_ref[...]
    for part in parts:
        mass = mass + part[...].astype(jnp.float32)
    rows, both = mass.shape
    low, high = mass[:, : both // 2], mass[:, both // 2 :]
    _, core, _ = place()
    keep_ref[...] = jnp.where(core == 0, low, high)
    give_ref[...] = jnp.where(core == 0, high, low)
    total = jnp.broadcast_to(jnp.sum(mass, axis=1, keepdims=True), (rows, lanes))
    nothing = jnp.zeros((rows, lanes), jnp.float32)
    totals = jnp.concatenate([jnp.where(core == 0, total, nothing), jnp.where(core == 0, nothing, total)], axis=0)
    column = lax.broadcasted_iota(jnp.int32, out_ref.shape, 1)
    out_ref[...] = jnp.where(column == 2, totals, stats_ref[...])


def joined_mass(stats, own, parts):
    rows, both = own.shape
    return local_call(
        join_kernel,
        [f32((rows, both // 2)), f32((rows, both // 2)), f32(stats.shape)],
        "join_mass",
        in_specs=[whole()] * (2 + len(parts)),
        out_specs=[whole()] * 3,
    )(stats, own, *parts)


def merge_kernel(*refs):
    out_ref = refs[-1]
    stats = [ref[...] for ref in refs[:-1]]
    top = functools.reduce(jnp.maximum, [s[:, 0:1] for s in stats])
    shares = sum(s[:, 1:2] * jnp.exp(s[:, 0:1] - top) for s in stats)
    column = lax.broadcasted_iota(jnp.int32, out_ref.shape, 1)
    out_ref[...] = jnp.where(column == 0, top, jnp.where(column == 1, shares, sum(stats)))


def merged_stats(stats):
    return local_call(
        merge_kernel, f32(stats[0].shape), "merge_stats", in_specs=[whole()] * len(stats), out_specs=whole()
    )(*stats)


def back_rows(half, length_ref, stats_ref, mass_ref, logits_ref, turned_ref, key_ref, masked_ref, slope_ref, store):
    rows, key_count = mass_ref.shape
    width = key_ref.shape[1]
    flat = turned_ref.shape[1] // 2
    tile = math.gcd(key_count, 256)
    stats = rows_at(stats_ref, half, rows)
    visible = visible_tile(length_ref, 2 * lax.axis_index("heads") + half, rows, 0, key_count, key_count)
    weights_exp = jnp.where(visible, jnp.exp(rows_at(logits_ref, half, rows) - stats[:, 0:1]), 0.0)
    slope_ref[...] = loss_scale * (weights_exp / stats[:, 1:2] - mass_ref[...] / stats[:, 2:3])
    begin = pl.multiple_of(half * flat, flat)
    turned = turned_ref[:, pl.ds(begin, flat)]
    query_grad = jnp.zeros((flat, width), jnp.float32)
    for first in range(0, key_count, tile):
        keys = key_ref[first : first + tile, :]
        slopes = jnp.broadcast_to(slope_ref[:, first : first + tile][:, None, :], (rows, flat // rows, tile))
        masked = masked_ref[pl.ds(begin, flat), first : first + tile]
        terms = (slopes.reshape(flat, tile) * masked).astype(jnp.bfloat16)
        query_grad = query_grad + jnp.dot(terms, keys, preferred_element_type=jnp.float32)
        store(first, tile, jnp.dot(turned, terms, preferred_element_type=jnp.float32))
    return query_grad


def back_own_kernel(
    length_ref, stats_ref, mass_ref, logits_ref, turned_ref, key_ref, masked_ref, query_out, key_out, slope_ref
):
    _, core, _ = place()

    def store(first, tile, key_grad):
        key_out[:, first : first + tile] = key_grad

    query_out[...] = back_rows(
        core, length_ref, stats_ref, mass_ref, logits_ref, turned_ref, key_ref, masked_ref, slope_ref, store
    )


def back_own(lengths, stats, mass, logits, turned, index_key, masked):
    rows, key_count = mass.shape
    width, flat = turned.shape
    return local_call(
        back_own_kernel,
        [f32((flat // 2, width)), f32((width, key_count))],
        "index_back_own",
        in_specs=[whole()] * 7,
        out_specs=[whole()] * 2,
        scratch=[pltpu.VMEM((rows, key_count), jnp.float32)],
    )(lengths, stats, mass, logits, turned, index_key, masked)


def back_pair_kernel(
    length_ref, stats_ref, mass_ref, logits_ref, turned_ref, key_ref, masked_ref, query_ref, before_ref, *refs
):
    partners = len(refs) - 4
    key_outs = refs[:partners]
    keep_ref, send_ref, slope_ref, grad_ref = refs[partners:]
    key_count, width = key_ref.shape
    _, core, group = place()

    def store(first, tile, key_grad):
        grad_ref[first : first + tile, :] = (before_ref[:, first : first + tile] + key_grad).T

    other = back_rows(
        1 - core, length_ref, stats_ref, mass_ref, logits_ref, turned_ref, key_ref, masked_ref, slope_ref, store
    )
    block = key_count // partners
    for e, out_ref in enumerate(key_outs):
        out_ref[...] = rows_at(grad_ref, group ^ e, block).astype(out_ref.dtype)
    planes, part, _ = keep_ref.shape
    rows = mass_ref.shape[0]
    for half, query_grad in ((core, query_ref[...]), (1 - core, other)):
        split = query_grad.reshape(rows, planes, 2, part // (2 * rows), width)
        place_of = pl.ds(pl.multiple_of(half * (part // 2), part // 2), part // 2)
        for plane in range(planes):
            low = split[:, plane, 0].reshape(part // 2, width)
            high = split[:, plane, 1].reshape(part // 2, width)
            keep_ref[plane, place_of, :] = jnp.where(core == 0, low, high)
            send_ref[plane, place_of, :] = jnp.where(core == 0, high, low).astype(jnp.bfloat16)


def back_pair(lengths, stats, mass, logits, turned, index_key, masked, query_grad, key_grad, partners, planes):
    rows, key_count = mass.shape
    width, flat = turned.shape
    part = flat // (2 * planes)
    return local_call(
        back_pair_kernel,
        [f32((key_count // partners, width))]
        + [bf16((key_count // partners, width))] * (partners - 1)
        + [f32((planes, part, width)), bf16((planes, part, width))],
        "index_back_pair",
        in_specs=[whole()] * 9,
        out_specs=[whole()] * (partners + 2),
        scratch=[pltpu.VMEM((rows, key_count), jnp.float32), pltpu.VMEM((key_count, width), jnp.float32)],
    )(lengths, stats, mass, logits, turned, index_key, masked, query_grad, key_grad)


def pair_kernel(keep_ref, got_ref, *outs):
    own_plane, _, _ = place()
    for e, out_ref in enumerate(outs):
        plane = own_plane ^ e
        out_ref[...] = (keep_ref[plane] + got_ref[plane].astype(jnp.float32)).astype(out_ref.dtype)


def pair_sums(keep, got):
    planes, part, width = keep.shape
    return local_call(
        pair_kernel,
        [f32((part, width))] + [bf16((part, width))] * (planes - 1),
        "pair_sums",
        in_specs=[whole(), whole()],
        out_specs=[whole()] * planes,
    )(keep, got)


def last_kernel(key_parts, *refs):
    query_out, key_out = refs[-2:]
    key_refs, query_refs = refs[:key_parts], refs[key_parts:-2]
    key_out[...] = sum(ref[...].astype(jnp.float32) for ref in key_refs)
    query_out[...] = sum(ref[...].astype(jnp.float32) for ref in query_refs).reshape(query_out.shape)


def last_sums(key_parts, query_parts, query_shape):
    return local_call(
        functools.partial(last_kernel, len(key_parts)),
        [f32(query_shape), f32(key_parts[0].shape)],
        "last_sums",
        in_specs=[whole()] * (len(key_parts) + len(query_parts)),
        out_specs=[whole()] * 2,
    )(*key_parts, *query_parts)


def after(array, *others):
    return lax.optimization_barrier((array, *others))[0]


def block_device(main_query, latent_keys, head_lse, lengths, index_query, index_key, index_weight):
    contexts = lax.axis_size("context")
    planes = contexts // 2
    partners = lax.axis_size("heads")
    context = lax.axis_index("context")
    rows, heads, _ = main_query.shape
    own_rows, index_heads, width = index_query.shape
    key_count = latent_keys.shape[0]
    flat = own_rows * index_heads

    def planes_move(array, pairs):
        return lax.ppermute(array, "context", [(2 * a + k, 2 * b + k) for a, b in pairs for k in (0, 1)])

    def context_flip(array, e):
        return lax.ppermute(array, "context", [(c, c ^ e) for c in range(contexts)])

    def heads_flip(array, e):
        return lax.ppermute(array, "heads", [(h, h ^ e) for h in range(partners)])

    keys_pair = context_flip(latent_keys.T, 1)
    pack, *inner = packed_queries(main_query)
    inner = [planes_move(block, [(1, 2), (2, 1), (0, 0), (3, 3)]) for block in inner]
    near = planes_move(pack, [(0, 1), (1, 0), (2, 3), (3, 2)])
    ends = planes_move(pack, [(0, 3), (3, 0)])
    lengths, lse, weight_wide, query, turned, index_key, keys = load_inputs(
        lengths, head_lse.T, index_weight, index_query, index_key, after(latent_keys, pack).T
    )
    keys = (keys, keys_pair)

    blocks = head_blocks(heads)

    def mass_of(pack, flip, blocks, *rest):
        return chunk_mass(lengths, pack, lse, keys, flip, blocks, rows, *rest)

    inner[1] = after(inner[1], lse)
    far = [planes_move(block, [(0, 2), (3, 1), (1, 0), (2, 3)]) for block in inner]
    logits, masked, stats = index_logits(lengths, query.reshape(flat, width), index_key, weight_wide, own_rows)
    stats = merged_stats([stats, context_flip(stats, 1)])
    own_mass = mass_of(pack, 0, blocks, "mass_own")
    near_mass = mass_of(after(near, logits), 1, blocks, "mass_near")
    across_mass = mass_of(picked(after(ends, own_mass, near_mass), inner), 3, blocks, "mass_across")
    far_mass = mass_of(after(far[0], across_mass, stats), 2, blocks[:1], "mass_far")
    shared = shared_mass(
        lengths, after(far[1], far_mass), lse, keys, own_mass, near_mass, across_mass, far_mass, blocks[1], partners
    )
    keep_mass, give_mass, stats = joined_mass(
        stats, shared[0], [heads_flip(shared[e], e) for e in (*reversed(range(1, partners - 1)), partners - 1)]
    )
    got_mass = context_flip(give_mass, 1)
    stats = merged_stats([stats] + [context_flip(stats, 2 * e) for e in reversed(range(1, planes))])
    back = (logits, turned, index_key, masked)
    query_grad, key_grad = back_own(lengths, stats, keep_mass, *back)
    *key_grads, keep, send = back_pair(
        lengths, context_flip(stats, 1), got_mass, *back, query_grad, key_grad, partners, planes
    )
    got = context_flip(send, 1)
    key_parts = [key_grads[0]] + [heads_flip(key_grads[e], e) for e in range(1, partners)]
    sums = pair_sums(keep, got)
    query_parts = [sums[0]] + [context_flip(sums[e], 2 * e) for e in reversed(range(1, planes))]
    return last_sums(key_parts, query_parts, (own_rows, index_heads // contexts, width))


def fits(mesh):
    return mesh.shape["context"] == 8 and mesh.shape["heads"] == 4


def solution(mesh):
    placed = (
        P("context", "heads", None),
        P("context", None),
        P(None, "heads"),
        P(),
        P("heads", None, None),
        P("context", None),
        P("heads", None),
    )
    return jax.shard_map(
        block_device if fits(mesh) else general_on_device,
        mesh=mesh,
        in_specs=placed,
        out_specs=(P("heads", "context", None), P(("context", "heads"), None)),
        check_vma=False,
    )
```

```python
import functools
import math

import jax
import jax.numpy as jnp
from jax import lax
from jax.experimental import pallas as pl
from jax.experimental.pallas import tpu as pltpu
from jax.sharding import PartitionSpec as P

main_scale = 192.0 ** (-0.5)
loss_scale = 64.0
masked_low = -1e30
log2_e = math.log2(math.e)
lanes = 128
vmem_bytes = 20 * 1024 * 1024

def joined(part, axis, combine):
    gathered = jax.tree.map(lambda a: lax.all_gather(a, axis), part)

    def take(source):
        return jax.tree.map(lambda a: lax.dynamic_index_in_dim(a, source, 0, False), gathered)

    return lax.fori_loop(
        1, lax.axis_size(axis), lambda source, state: combine(state, take(source)), take(0)
    )


def head_mass(queries, lse_rows, len_rows, latent, first_key):
    row_count = queries.shape[0]
    block_rows = math.gcd(row_count, 64)
    steps_count = row_count // block_rows
    key_pos = first_key + jnp.arange(latent.shape[0], dtype=jnp.int32)

    def one_block(inputs):
        query_block, lse_block, len_block = inputs
        scores = (
            jnp.einsum("rhd,sd->rhs", query_block, latent, preferred_element_type=jnp.float32)
            * main_scale
        )
        summed = jnp.sum(jnp.exp(scores - lse_block[:, :, None]), axis=1)
        return jnp.where(key_pos[None, :] < len_block[:, None], summed, 0.0)

    stacked = lax.map(
        one_block,
        (
            queries.reshape((steps_count, block_rows) + queries.shape[1:]),
            lse_rows.reshape(steps_count, block_rows, lse_rows.shape[1]),
            len_rows.reshape(steps_count, block_rows),
        ),
    )
    return stacked.reshape(row_count, latent.shape[0])


def general_on_device(main_query, latent_keys, head_lse, lengths, index_query, index_key, index_weight):
    key_count = latent_keys.shape[0]
    first_key = lax.axis_index("context") * key_count
    own_rows = index_query.shape[0]
    row_first = lax.axis_index("heads") * own_rows
    partial_mass = head_mass(
        lax.all_gather(main_query, "context", axis=0, tiled=True),
        head_lse,
        lengths,
        latent_keys,
        first_key,
    )
    summed_mass = lax.psum(partial_mass, "heads")
    row_mass = lax.dynamic_slice_in_dim(summed_mass, row_first, own_rows, 0)
    own_len = lax.dynamic_slice_in_dim(lengths, row_first, own_rows, 0)
    visible = (first_key + jnp.arange(key_count, dtype=jnp.int32))[None, :] < own_len[:, None]
    heads_count = index_query.shape[1]
    width = index_query.shape[2]
    index_scale = width ** (-0.5)
    flat_query = index_query.reshape(own_rows * heads_count, width)
    block_keys = math.gcd(key_count, 512)
    block_total = key_count // block_keys
    key_blocks = index_key.reshape(block_total, block_keys, width)

    def block_dots(key_block):
        products = lax.dot_general(
            flat_query, key_block, (((1,), (1,)), ((), ())), preferred_element_type=jnp.float32
        )
        return products.reshape(own_rows, heads_count, key_block.shape[0])

    def block_logits(key_block):
        return (
            jnp.einsum(
                "tj,tjs->ts",
                index_weight,
                jax.nn.relu(block_dots(key_block)),
                precision=lax.Precision.HIGHEST,
            )
            * index_scale
        )

    logits = jnp.moveaxis(lax.map(block_logits, key_blocks), 0, 1).reshape(own_rows, key_count)
    local_top = jnp.max(jnp.where(visible, logits, masked_low), axis=1)
    mass_local = jnp.sum(row_mass, axis=1)
    local_exp = jnp.where(visible, jnp.exp(logits - local_top[:, None]), 0.0)

    def combine(first, second):
        highest = jnp.maximum(first[0], second[0])
        merged = first[1] * jnp.exp(first[0] - highest) + second[1] * jnp.exp(second[0] - highest)
        return (highest, merged, first[2] + second[2])

    top, share_sum, mass_total = joined(
        (local_top, jnp.sum(local_exp, axis=1), mass_local), "context", combine
    )
    weights_exp = jnp.where(visible, jnp.exp(logits - top[:, None]), 0.0)
    probability = weights_exp / share_sum[:, None]
    target = row_mass / mass_total[:, None]
    slopes = loss_scale * (probability - target)
    slope_blocks = slopes.reshape(own_rows, block_total, block_keys).transpose(1, 0, 2)

    def back_step(query_grad, inputs):
        key_block, slope_block = inputs
        products = block_dots(key_block)
        terms = jnp.where(
            products > 0, slope_block[:, None, :] * index_weight[:, :, None] * index_scale, 0.0
        )
        terms = terms.astype(jnp.bfloat16).reshape(own_rows * heads_count, key_block.shape[0])
        query_grad = query_grad + jnp.dot(terms, key_block, preferred_element_type=jnp.float32)
        key_grad = lax.dot_general(
            terms, flat_query, (((0,), (0,)), ((), ())), preferred_element_type=jnp.float32
        )
        return (query_grad, key_grad)

    start_grad = jnp.zeros((own_rows * heads_count, width), jnp.float32)
    query_grad, key_grads = lax.scan(back_step, start_grad, (key_blocks, slope_blocks))
    query_grad = query_grad.reshape(own_rows, heads_count, width)
    key_grad = key_grads.reshape(key_count, width)
    out_query = lax.psum_scatter(query_grad, "context", scatter_dimension=1, tiled=True)
    out_key = lax.psum_scatter(key_grad, "heads", scatter_dimension=0, tiled=True)
    return (out_query, out_key)


def local_call(kernel, out_shape, name, in_specs, out_specs, scratch=(), flops=1):
    return pl.pallas_call(
        kernel,
        out_shape=out_shape,
        in_specs=in_specs,
        out_specs=out_specs,
        scratch_shapes=list(scratch),
        name=name,
        compiler_params=pltpu.CompilerParams(vmem_limit_bytes=vmem_bytes),
        cost_estimate=pl.CostEstimate(flops=flops, bytes_accessed=1, transcendentals=0),
    )


def whole():
    return pl.BlockSpec(memory_space=pltpu.VMEM)


def scalars():
    return pl.BlockSpec(memory_space=pltpu.SMEM)


def f32(shape):
    return jax.ShapeDtypeStruct(shape, jnp.float32)


def bf16(shape):
    return jax.ShapeDtypeStruct(shape, jnp.bfloat16)


def place():
    context = lax.axis_index("context")
    return context >> 1, context & 1, lax.axis_index("heads")


def hbm():
    return pl.BlockSpec(memory_space=pltpu.HBM)


def head_blocks(heads):
    first = heads * 5 // 8
    return ((0, first), (first, heads - first))


def packed_rows(rows, heads, width):
    return rows * heads * width // lanes


def pack_kernel(query_ref, out_ref, *block_refs):
    rows, heads, width = query_ref.shape
    columns = width // lanes
    stacked = jnp.swapaxes(query_ref[...].astype(jnp.float32), 0, 1).reshape(rows * heads, width)
    begin = 0
    for (first, count), block_ref in zip(head_blocks(heads), block_refs):
        total = rows * count
        block = stacked[rows * first : rows * first + total]
        rest = block[:, columns * lanes :]
        pieces = [block[:, i * lanes : (i + 1) * lanes] for i in range(columns)]
        pieces.append(jnp.concatenate([rest[: total // 2], rest[total // 2 :]], axis=1))
        place = 0
        for piece in pieces:
            piece = piece.astype(jnp.bfloat16)
            size = piece.shape[0]
            out_ref[begin + place : begin + place + size, :] = piece
            block_ref[place : place + size, :] = piece
            place += size
        begin += place


def packed_queries(queries):
    rows, heads, width = queries.shape
    blocks = [bf16((packed_rows(rows, count, width), lanes)) for _, count in head_blocks(heads)]
    return local_call(
        pack_kernel,
        [bf16((packed_rows(rows, heads, width), lanes))] + blocks,
        "pack_queries",
        in_specs=[whole()],
        out_specs=[whole()] * (1 + len(blocks)),
        flops=30_000_000_000,
    )(queries)


def pick_kernel(ends_ref, *refs):
    inner_refs, out_ref = refs[:-1], refs[-1]
    plane, _, _ = place()
    inner = (plane == 1) | (plane == 2)

    @pl.when(inner)
    def _():
        begin = 0
        for inner_ref in inner_refs:
            rows = inner_ref.shape[0]
            out_ref[begin : begin + rows, :] = inner_ref[...]
            begin += rows

    @pl.when(jnp.logical_not(inner))
    def _():
        out_ref[...] = ends_ref[...]


def picked(ends, inner):
    return local_call(
        pick_kernel,
        bf16(ends.shape),
        "pick_queries",
        in_specs=[whole()] * (1 + len(inner)),
        out_specs=whole(),
    )(ends, *inner)


def unpack(packed_ref, begin, wide_ref, row, total):
    width = wide_ref.shape[1]
    columns = width // lanes
    half = total // 2
    for i in range(columns):
        wide_ref[row : row + total, i * lanes : (i + 1) * lanes] = packed_ref[
            begin + i * total : begin + (i + 1) * total, :
        ]
    rest = packed_ref[begin + columns * total : begin + columns * total + half, :]
    wide_ref[row : row + half, columns * lanes :] = rest[:, : lanes // 2]
    wide_ref[row + half : row + total, columns * lanes :] = rest[:, lanes // 2 :]


def widened(column, width):
    return jnp.concatenate([column] * (width // lanes), axis=1)


def rows_at(ref, index, rows):
    return ref[pl.ds(pl.multiple_of(index * rows, rows), rows), :]


def visible_tile(length_ref, block, rows, first, width, key_count):
    positions = lax.axis_index("context") * key_count + first + lax.broadcasted_iota(jnp.int32, (rows, width), 1)
    return positions < widened(rows_at(length_ref, block, rows), width)


def chip_mass(length_ref, wide_ref, lse_ref, own_key_ref, pair_key_ref, context, heads, out_ref, before_ref=None):
    width, key_count = own_key_ref.shape
    first_head, head_count = heads
    rows = wide_ref.shape[0] // head_count
    tile = math.gcd(key_count, 512)
    plane, core, _ = place()
    lse = rows_at(lse_ref, context, rows)
    column = widened(rows_at(length_ref, context, rows), tile)
    spread = lax.broadcasted_iota(jnp.int32, (rows, tile), 1)
    for key_ref, half in ((own_key_ref, core), (pair_key_ref, 1 - core)):
        for first in range(0, key_count, tile):
            scores = jnp.dot(wide_ref[...], key_ref[:, first : first + tile], preferred_element_type=jnp.float32)
            summed = jnp.zeros((rows, tile), jnp.float32)
            for h in range(head_count):
                summed = summed + jnp.exp2(
                    scores[h * rows : (h + 1) * rows] * (main_scale * log2_e)
                    - lse[:, first_head + h : first_head + h + 1]
                )
            visible = (2 * plane + half) * key_count + first + spread < column
            mass = jnp.where(visible, summed, 0.0)
            columns = pl.ds(pl.multiple_of(half * key_count + first, tile), tile)
            if before_ref is not None:
                mass = mass + before_ref[:, columns]
            out_ref[:, columns] = mass


def mass_kernel(flip, blocks, length_ref, pack_ref, lse_ref, own_key_ref, pair_key_ref, out_ref, wide_ref):
    plane, core, _ = place()
    heads = (blocks[0][0], sum(count for _, count in blocks))
    rows = wide_ref.shape[0] // heads[1]
    begin = row = 0
    for _, count in blocks:
        unpack(pack_ref, begin, wide_ref, row, rows * count)
        begin += packed_rows(rows, count, wide_ref.shape[1])
        row += rows * count
    chip_mass(length_ref, wide_ref, lse_ref, own_key_ref, pair_key_ref, 2 * (plane ^ flip) + core, heads, out_ref)


def chunk_mass(lengths, pack, lse, keys, flip, blocks, rows, name):
    width, key_count = keys[0].shape
    total = rows * sum(count for _, count in blocks)
    return local_call(
        functools.partial(mass_kernel, flip, blocks),
        f32((rows, 2 * key_count)),
        name,
        in_specs=[whole()] * 5,
        out_specs=whole(),
        scratch=[pltpu.VMEM((total, width), jnp.bfloat16)],
    )(lengths, pack, lse, *keys)


def share_kernel(
    heads, length_ref, pack_ref, lse_ref, own_key_ref, pair_key_ref, own_ref, near_ref, across_ref, before_ref, *refs
):
    outs = refs[:-2]
    wide_ref, chunks_ref = refs[-2:]
    plane, core, group = place()
    unpack(pack_ref, 0, wide_ref, 0, wide_ref.shape[0])
    chunks_ref[0] = own_ref[...]
    chunks_ref[1] = near_ref[...]
    chunks_ref[3] = across_ref[...]
    chip_mass(
        length_ref, wide_ref, lse_ref, own_key_ref, pair_key_ref, 2 * (plane ^ 2) + core, heads, chunks_ref.at[2],
        before_ref,
    )
    for e, out_ref in enumerate(outs):
        out_ref[...] = chunks_ref[plane ^ group ^ e].astype(out_ref.dtype)


def shared_mass(lengths, pack, lse, keys, own, near, across, before, heads, partners):
    width, _ = keys[0].shape
    rows, both = own.shape
    return local_call(
        functools.partial(share_kernel, heads),
        [f32((rows, both))] + [bf16((rows, both))] * (partners - 1),
        "mass_and_share",
        in_specs=[whole()] * 9,
        out_specs=[whole()] * partners,
        scratch=[pltpu.VMEM((rows * heads[1], width), jnp.bfloat16), pltpu.VMEM((4, rows, both), jnp.float32)],
    )(lengths, pack, lse, *keys, own, near, across, before)


def logits_kernel(length_ref, query_ref, key_ref, weight_ref, logits_ref, masked_ref, stats_ref):
    rows, key_count = logits_ref.shape
    heads = query_ref.shape[0] // rows
    tile = math.gcd(key_count, 256)
    group = lax.axis_index("heads")
    best = jnp.full((rows, 1), masked_low, jnp.float32)
    weights = widened(weight_ref[...], tile)
    for first in range(0, key_count, tile):
        dots = lax.dot_general(
            query_ref[...], key_ref[first : first + tile, :], (((1,), (1,)), ((), ())),
            preferred_element_type=jnp.float32,
        )
        masked = jnp.where(dots > 0, weights, 0.0)
        masked_ref[:, first : first + tile] = masked
        logits = jnp.sum((dots * masked).reshape(rows, heads, tile), axis=1)
        logits_ref[:, first : first + tile] = logits
        visible = visible_tile(length_ref, group, rows, first, tile, key_count)
        best = jnp.maximum(best, jnp.max(jnp.where(visible, logits, masked_low), axis=1, keepdims=True))
    visible = visible_tile(length_ref, group, rows, 0, key_count, key_count)
    total = jnp.sum(jnp.where(visible, jnp.exp(logits_ref[...] - best), 0.0), axis=1, keepdims=True)
    column = lax.broadcasted_iota(jnp.int32, (rows, lanes), 1)
    stats_ref[...] = jnp.where(column == 0, best, total)


def index_logits(lengths, flat_query, index_key, weight_wide, rows):
    key_count = index_key.shape[0]
    flat = flat_query.shape[0]
    return local_call(
        logits_kernel,
        [f32((rows, key_count)), f32((flat, key_count)), f32((rows, lanes))],
        "index_logits",
        in_specs=[whole()] * 4,
        out_specs=[whole()] * 3,
    )(lengths, flat_query, index_key, weight_wide)


def load_kernel(
    length_ref, lse_ref, weight_ref, query_hbm, key_hbm, latent_hbm,
    length_out, lse_out, weight_out, query_out, turned_out, key_out, latent_out, semaphores,
):
    copies = [
        pltpu.make_async_copy(source, target, semaphores.at[i])
        for i, (source, target) in enumerate(
            [(query_hbm, query_out), (key_hbm, key_out), (latent_hbm, latent_out)]
        )
    ]
    for copy in copies:
        copy.start()
    total = length_out.shape[0]
    spread = lax.broadcasted_iota(jnp.int32, (8, lanes), 0)
    for first in range(0, total, 8):
        column = jnp.zeros((8, lanes), jnp.int32)
        for i in range(8):
            column = jnp.where(spread == i, length_ref[first + i], column)
        length_out[first : first + 8, :] = column
    lse_out[...] = lse_ref[...].T * log2_e
    rows, heads = weight_ref.shape
    width = key_out.shape[1]
    weights = weight_ref[...].T * width ** (-0.5)
    for t in range(rows):
        weight_out[t * heads : (t + 1) * heads, :] = jnp.broadcast_to(weights[:, t : t + 1], (heads, lanes))
    copies[0].wait()
    turned_out[...] = query_out[...].reshape(rows * heads, width).astype(jnp.float32).T.astype(jnp.bfloat16)
    copies[1].wait()
    copies[2].wait()


def load_inputs(lengths, lse, weights, query, key, latent):
    rows, heads, width = query.shape
    flat = rows * heads
    return local_call(
        load_kernel,
        [
            jax.ShapeDtypeStruct((lengths.shape[0], lanes), jnp.int32),
            f32(lse.shape[::-1]),
            f32((flat, lanes)),
            bf16(query.shape),
            bf16((width, flat)),
            bf16(key.shape),
            bf16(latent.shape),
        ],
        "load_inputs",
        in_specs=[scalars(), whole(), whole(), hbm(), hbm(), hbm()],
        out_specs=[whole()] * 7,
        scratch=[pltpu.SemaphoreType.DMA((3,))],
    )(lengths, lse, weights, query, key, latent)


def join_kernel(stats_ref, own_ref, *refs):
    parts, (keep_ref, give_ref, out_ref) = refs[:-3], refs[-3:]
    mass = own_ref[...]
    for part in parts:
        mass = mass + part[...].astype(jnp.float32)
    rows, both = mass.shape
    low, high = mass[:, : both // 2], mass[:, both // 2 :]
    _, core, _ = place()
    keep_ref[...] = jnp.where(core == 0, low, high)
    give_ref[...] = jnp.where(core == 0, high, low)
    total = jnp.broadcast_to(jnp.sum(mass, axis=1, keepdims=True), (rows, lanes))
    nothing = jnp.zeros((rows, lanes), jnp.float32)
    totals = jnp.concatenate([jnp.where(core == 0, total, nothing), jnp.where(core == 0, nothing, total)], axis=0)
    column = lax.broadcasted_iota(jnp.int32, out_ref.shape, 1)
    out_ref[...] = jnp.where(column == 2, totals, stats_ref[...])


def joined_mass(stats, own, parts):
    rows, both = own.shape
    return local_call(
        join_kernel,
        [f32((rows, both // 2)), f32((rows, both // 2)), f32(stats.shape)],
        "join_mass",
        in_specs=[whole()] * (2 + len(parts)),
        out_specs=[whole()] * 3,
    )(stats, own, *parts)


def merge_kernel(*refs):
    out_ref = refs[-1]
    stats = [ref[...] for ref in refs[:-1]]
    top = functools.reduce(jnp.maximum, [s[:, 0:1] for s in stats])
    shares = sum(s[:, 1:2] * jnp.exp(s[:, 0:1] - top) for s in stats)
    column = lax.broadcasted_iota(jnp.int32, out_ref.shape, 1)
    out_ref[...] = jnp.where(column == 0, top, jnp.where(column == 1, shares, sum(stats)))


def merged_stats(stats):
    return local_call(
        merge_kernel, f32(stats[0].shape), "merge_stats", in_specs=[whole()] * len(stats), out_specs=whole()
    )(*stats)


def back_rows(half, length_ref, stats_ref, mass_ref, logits_ref, turned_ref, key_ref, masked_ref, slope_ref, store):
    rows, key_count = mass_ref.shape
    width = key_ref.shape[1]
    flat = turned_ref.shape[1] // 2
    tile = math.gcd(key_count, 256)
    stats = rows_at(stats_ref, half, rows)
    visible = visible_tile(length_ref, 2 * lax.axis_index("heads") + half, rows, 0, key_count, key_count)
    weights_exp = jnp.where(visible, jnp.exp(rows_at(logits_ref, half, rows) - stats[:, 0:1]), 0.0)
    slope_ref[...] = loss_scale * (weights_exp / stats[:, 1:2] - mass_ref[...] / stats[:, 2:3])
    begin = pl.multiple_of(half * flat, flat)
    turned = turned_ref[:, pl.ds(begin, flat)]
    query_grad = jnp.zeros((flat, width), jnp.float32)
    for first in range(0, key_count, tile):
        keys = key_ref[first : first + tile, :]
        slopes = jnp.broadcast_to(slope_ref[:, first : first + tile][:, None, :], (rows, flat // rows, tile))
        masked = masked_ref[pl.ds(begin, flat), first : first + tile]
        terms = (slopes.reshape(flat, tile) * masked).astype(jnp.bfloat16)
        query_grad = query_grad + jnp.dot(terms, keys, preferred_element_type=jnp.float32)
        store(first, tile, jnp.dot(turned, terms, preferred_element_type=jnp.float32))
    return query_grad


def back_own_kernel(
    length_ref, stats_ref, mass_ref, logits_ref, turned_ref, key_ref, masked_ref, query_out, key_out, slope_ref
):
    _, core, _ = place()

    def store(first, tile, key_grad):
        key_out[:, first : first + tile] = key_grad

    query_out[...] = back_rows(
        core, length_ref, stats_ref, mass_ref, logits_ref, turned_ref, key_ref, masked_ref, slope_ref, store
    )


def back_own(lengths, stats, mass, logits, turned, index_key, masked):
    rows, key_count = mass.shape
    width, flat = turned.shape
    return local_call(
        back_own_kernel,
        [f32((flat // 2, width)), f32((width, key_count))],
        "index_back_own",
        in_specs=[whole()] * 7,
        out_specs=[whole()] * 2,
        scratch=[pltpu.VMEM((rows, key_count), jnp.float32)],
    )(lengths, stats, mass, logits, turned, index_key, masked)


def back_pair_kernel(
    length_ref, stats_ref, mass_ref, logits_ref, turned_ref, key_ref, masked_ref, query_ref, before_ref, *refs
):
    partners = len(refs) - 4
    key_outs = refs[:partners]
    keep_ref, send_ref, slope_ref, grad_ref = refs[partners:]
    key_count, width = key_ref.shape
    _, core, group = place()

    def store(first, tile, key_grad):
        grad_ref[first : first + tile, :] = (before_ref[:, first : first + tile] + key_grad).T

    other = back_rows(
        1 - core, length_ref, stats_ref, mass_ref, logits_ref, turned_ref, key_ref, masked_ref, slope_ref, store
    )
    block = key_count // partners
    for e, out_ref in enumerate(key_outs):
        out_ref[...] = rows_at(grad_ref, group ^ e, block).astype(out_ref.dtype)
    planes, part, _ = keep_ref.shape
    rows = mass_ref.shape[0]
    for half, query_grad in ((core, query_ref[...]), (1 - core, other)):
        split = query_grad.reshape(rows, planes, 2, part // (2 * rows), width)
        place_of = pl.ds(pl.multiple_of(half * (part // 2), part // 2), part // 2)
        for plane in range(planes):
            low = split[:, plane, 0].reshape(part // 2, width)
            high = split[:, plane, 1].reshape(part // 2, width)
            keep_ref[plane, place_of, :] = jnp.where(core == 0, low, high)
            send_ref[plane, place_of, :] = jnp.where(core == 0, high, low).astype(jnp.bfloat16)


def back_pair(lengths, stats, mass, logits, turned, index_key, masked, query_grad, key_grad, partners, planes):
    rows, key_count = mass.shape
    width, flat = turned.shape
    part = flat // (2 * planes)
    return local_call(
        back_pair_kernel,
        [f32((key_count // partners, width))]
        + [bf16((key_count // partners, width))] * (partners - 1)
        + [f32((planes, part, width)), bf16((planes, part, width))],
        "index_back_pair",
        in_specs=[whole()] * 9,
        out_specs=[whole()] * (partners + 2),
        scratch=[pltpu.VMEM((rows, key_count), jnp.float32), pltpu.VMEM((key_count, width), jnp.float32)],
    )(lengths, stats, mass, logits, turned, index_key, masked, query_grad, key_grad)


def pair_kernel(keep_ref, got_ref, *outs):
    own_plane, _, _ = place()
    for e, out_ref in enumerate(outs):
        plane = own_plane ^ e
        out_ref[...] = (keep_ref[plane] + got_ref[plane].astype(jnp.float32)).astype(out_ref.dtype)


def pair_sums(keep, got):
    planes, part, width = keep.shape
    return local_call(
        pair_kernel,
        [f32((part, width))] + [bf16((part, width))] * (planes - 1),
        "pair_sums",
        in_specs=[whole(), whole()],
        out_specs=[whole()] * planes,
    )(keep, got)


def sum_kernel(*refs):
    out_ref = refs[-1]
    out_ref[...] = sum(ref[...].astype(jnp.float32) for ref in refs[:-1]).reshape(out_ref.shape)


def summed(parts, shape, name):
    return local_call(sum_kernel, f32(shape), name, in_specs=[whole()] * len(parts), out_specs=whole())(*parts)


def after(array, *others):
    return lax.optimization_barrier((array, *others))[0]


def block_device(main_query, latent_keys, head_lse, lengths, index_query, index_key, index_weight):
    contexts = lax.axis_size("context")
    planes = contexts // 2
    partners = lax.axis_size("heads")
    context = lax.axis_index("context")
    rows, heads, _ = main_query.shape
    own_rows, index_heads, width = index_query.shape
    key_count = latent_keys.shape[0]
    flat = own_rows * index_heads

    def planes_move(array, pairs):
        return lax.ppermute(array, "context", [(2 * a + k, 2 * b + k) for a, b in pairs for k in (0, 1)])

    def context_flip(array, e):
        return lax.ppermute(array, "context", [(c, c ^ e) for c in range(contexts)])

    def heads_flip(array, e):
        return lax.ppermute(array, "heads", [(h, h ^ e) for h in range(partners)])

    keys_pair = context_flip(latent_keys.T, 1)
    pack, *inner = packed_queries(main_query)
    inner = [planes_move(block, [(1, 2), (2, 1), (0, 0), (3, 3)]) for block in inner]
    near = planes_move(pack, [(0, 1), (1, 0), (2, 3), (3, 2)])
    ends = planes_move(pack, [(0, 3), (3, 0)])
    lengths, lse, weight_wide, query, turned, index_key, keys = load_inputs(
        lengths, head_lse.T, index_weight, index_query, index_key, after(latent_keys, pack).T
    )
    keys = (keys, keys_pair)

    blocks = head_blocks(heads)

    def mass_of(pack, flip, blocks, *rest):
        return chunk_mass(lengths, pack, lse, keys, flip, blocks, rows, *rest)

    inner[1] = after(inner[1], lse)
    far = [planes_move(block, [(0, 2), (3, 1), (1, 0), (2, 3)]) for block in inner]
    logits, masked, stats = index_logits(lengths, query.reshape(flat, width), index_key, weight_wide, own_rows)
    stats = merged_stats([stats, context_flip(stats, 1)])
    own_mass = mass_of(pack, 0, blocks, "mass_own")
    near_mass = mass_of(after(near, logits), 1, blocks, "mass_near")
    across_mass = mass_of(picked(after(ends, own_mass, near_mass), inner), 3, blocks, "mass_across")
    far_mass = mass_of(after(far[0], across_mass, stats), 2, blocks[:1], "mass_far")
    shared = shared_mass(
        lengths, after(far[1], far_mass), lse, keys, own_mass, near_mass, across_mass, far_mass, blocks[1], partners
    )
    keep_mass, give_mass, stats = joined_mass(
        stats, shared[0], [heads_flip(shared[e], e) for e in (*reversed(range(1, partners - 1)), partners - 1)]
    )
    got_mass = context_flip(give_mass, 1)
    stats = merged_stats([stats] + [context_flip(stats, 2 * e) for e in reversed(range(1, planes))])
    back = (logits, turned, index_key, masked)
    query_grad, key_grad = back_own(lengths, stats, keep_mass, *back)
    *key_grads, keep, send = back_pair(
        lengths, context_flip(stats, 1), got_mass, *back, query_grad, key_grad, partners, planes
    )
    sums = pair_sums(keep, context_flip(send, 1))
    key_grads[-1] = after(key_grads[-1], sums[0])
    key_parts = [key_grads[0]] + [heads_flip(key_grads[e], e) for e in range(1, partners)]
    query_parts = [sums[0]] + [context_flip(sums[e], 2 * e) for e in reversed(range(1, planes))]
    out_key = summed(key_parts, key_parts[0].shape, "key_sums")
    query_parts[1] = after(query_parts[1], out_key)
    return summed(query_parts, (own_rows, index_heads // contexts, width), "query_sums"), out_key


def fits(mesh):
    return mesh.shape["context"] == 8 and mesh.shape["heads"] == 4


def solution(mesh):
    placed = (
        P("context", "heads", None),
        P("context", None),
        P(None, "heads"),
        P(),
        P("heads", None, None),
        P("context", None),
        P("heads", None),
    )
    return jax.shard_map(
        block_device if fits(mesh) else general_on_device,
        mesh=mesh,
        in_specs=placed,
        out_specs=(P("heads", "context", None), P(("context", "heads"), None)),
        check_vma=False,
    )
```

```python
import functools
import math

import jax
import jax.numpy as jnp
from jax import lax
from jax.experimental import pallas as pl
from jax.experimental.pallas import tpu as pltpu
from jax.sharding import PartitionSpec as P

main_scale = 192.0 ** (-0.5)
loss_scale = 64.0
masked_low = -1e30
log2_e = math.log2(math.e)
lanes = 128
vmem_bytes = 32 * 1024 * 1024

def joined(part, axis, combine):
    gathered = jax.tree.map(lambda a: lax.all_gather(a, axis), part)

    def take(source):
        return jax.tree.map(lambda a: lax.dynamic_index_in_dim(a, source, 0, False), gathered)

    return lax.fori_loop(
        1, lax.axis_size(axis), lambda source, state: combine(state, take(source)), take(0)
    )


def head_mass(queries, lse_rows, len_rows, latent, first_key):
    row_count = queries.shape[0]
    block_rows = math.gcd(row_count, 64)
    steps_count = row_count // block_rows
    key_pos = first_key + jnp.arange(latent.shape[0], dtype=jnp.int32)

    def one_block(inputs):
        query_block, lse_block, len_block = inputs
        scores = (
            jnp.einsum("rhd,sd->rhs", query_block, latent, preferred_element_type=jnp.float32)
            * main_scale
        )
        summed = jnp.sum(jnp.exp(scores - lse_block[:, :, None]), axis=1)
        return jnp.where(key_pos[None, :] < len_block[:, None], summed, 0.0)

    stacked = lax.map(
        one_block,
        (
            queries.reshape((steps_count, block_rows) + queries.shape[1:]),
            lse_rows.reshape(steps_count, block_rows, lse_rows.shape[1]),
            len_rows.reshape(steps_count, block_rows),
        ),
    )
    return stacked.reshape(row_count, latent.shape[0])


def general_on_device(main_query, latent_keys, head_lse, lengths, index_query, index_key, index_weight):
    key_count = latent_keys.shape[0]
    first_key = lax.axis_index("context") * key_count
    own_rows = index_query.shape[0]
    row_first = lax.axis_index("heads") * own_rows
    partial_mass = head_mass(
        lax.all_gather(main_query, "context", axis=0, tiled=True),
        head_lse,
        lengths,
        latent_keys,
        first_key,
    )
    summed_mass = lax.psum(partial_mass, "heads")
    row_mass = lax.dynamic_slice_in_dim(summed_mass, row_first, own_rows, 0)
    own_len = lax.dynamic_slice_in_dim(lengths, row_first, own_rows, 0)
    visible = (first_key + jnp.arange(key_count, dtype=jnp.int32))[None, :] < own_len[:, None]
    heads_count = index_query.shape[1]
    width = index_query.shape[2]
    index_scale = width ** (-0.5)
    flat_query = index_query.reshape(own_rows * heads_count, width)
    block_keys = math.gcd(key_count, 512)
    block_total = key_count // block_keys
    key_blocks = index_key.reshape(block_total, block_keys, width)

    def block_dots(key_block):
        products = lax.dot_general(
            flat_query, key_block, (((1,), (1,)), ((), ())), preferred_element_type=jnp.float32
        )
        return products.reshape(own_rows, heads_count, key_block.shape[0])

    def block_logits(key_block):
        return (
            jnp.einsum(
                "tj,tjs->ts",
                index_weight,
                jax.nn.relu(block_dots(key_block)),
                precision=lax.Precision.HIGHEST,
            )
            * index_scale
        )

    logits = jnp.moveaxis(lax.map(block_logits, key_blocks), 0, 1).reshape(own_rows, key_count)
    local_top = jnp.max(jnp.where(visible, logits, masked_low), axis=1)
    mass_local = jnp.sum(row_mass, axis=1)
    local_exp = jnp.where(visible, jnp.exp(logits - local_top[:, None]), 0.0)

    def combine(first, second):
        highest = jnp.maximum(first[0], second[0])
        merged = first[1] * jnp.exp(first[0] - highest) + second[1] * jnp.exp(second[0] - highest)
        return (highest, merged, first[2] + second[2])

    top, share_sum, mass_total = joined(
        (local_top, jnp.sum(local_exp, axis=1), mass_local), "context", combine
    )
    weights_exp = jnp.where(visible, jnp.exp(logits - top[:, None]), 0.0)
    probability = weights_exp / share_sum[:, None]
    target = row_mass / mass_total[:, None]
    slopes = loss_scale * (probability - target)
    slope_blocks = slopes.reshape(own_rows, block_total, block_keys).transpose(1, 0, 2)

    def back_step(query_grad, inputs):
        key_block, slope_block = inputs
        products = block_dots(key_block)
        terms = jnp.where(
            products > 0, slope_block[:, None, :] * index_weight[:, :, None] * index_scale, 0.0
        )
        terms = terms.astype(jnp.bfloat16).reshape(own_rows * heads_count, key_block.shape[0])
        query_grad = query_grad + jnp.dot(terms, key_block, preferred_element_type=jnp.float32)
        key_grad = lax.dot_general(
            terms, flat_query, (((0,), (0,)), ((), ())), preferred_element_type=jnp.float32
        )
        return (query_grad, key_grad)

    start_grad = jnp.zeros((own_rows * heads_count, width), jnp.float32)
    query_grad, key_grads = lax.scan(back_step, start_grad, (key_blocks, slope_blocks))
    query_grad = query_grad.reshape(own_rows, heads_count, width)
    key_grad = key_grads.reshape(key_count, width)
    out_query = lax.psum_scatter(query_grad, "context", scatter_dimension=1, tiled=True)
    out_key = lax.psum_scatter(key_grad, "heads", scatter_dimension=0, tiled=True)
    return (out_query, out_key)


def local_call(kernel, out_shape, name, in_specs, out_specs, scratch=(), flops=1):
    return pl.pallas_call(
        kernel,
        out_shape=out_shape,
        in_specs=in_specs,
        out_specs=out_specs,
        scratch_shapes=list(scratch),
        name=name,
        compiler_params=pltpu.CompilerParams(vmem_limit_bytes=vmem_bytes),
        cost_estimate=pl.CostEstimate(flops=flops, bytes_accessed=1, transcendentals=0),
    )


def whole():
    return pl.BlockSpec(memory_space=pltpu.VMEM)


def scalars():
    return pl.BlockSpec(memory_space=pltpu.SMEM)


def f32(shape):
    return jax.ShapeDtypeStruct(shape, jnp.float32)


def bf16(shape):
    return jax.ShapeDtypeStruct(shape, jnp.bfloat16)


def place():
    context = lax.axis_index("context")
    return context >> 1, context & 1, lax.axis_index("heads")


def hbm():
    return pl.BlockSpec(memory_space=pltpu.HBM)


def head_blocks(heads):
    first = heads * 5 // 8
    return ((0, first), (first, heads - first))


def packed_rows(rows, heads, width):
    return rows * heads * width // lanes


def pack_kernel(query_ref, out_ref, *block_refs):
    rows, heads, width = query_ref.shape
    columns = width // lanes
    stacked = jnp.swapaxes(query_ref[...].astype(jnp.float32), 0, 1).reshape(rows * heads, width)
    begin = 0
    for (first, count), block_ref in zip(head_blocks(heads), block_refs):
        total = rows * count
        block = stacked[rows * first : rows * first + total]
        rest = block[:, columns * lanes :]
        pieces = [block[:, i * lanes : (i + 1) * lanes] for i in range(columns)]
        pieces.append(jnp.concatenate([rest[: total // 2], rest[total // 2 :]], axis=1))
        place = 0
        for piece in pieces:
            piece = piece.astype(jnp.bfloat16)
            size = piece.shape[0]
            out_ref[begin + place : begin + place + size, :] = piece
            block_ref[place : place + size, :] = piece
            place += size
        begin += place


def packed_queries(queries):
    rows, heads, width = queries.shape
    blocks = [bf16((packed_rows(rows, count, width), lanes)) for _, count in head_blocks(heads)]
    return local_call(
        pack_kernel,
        [bf16((packed_rows(rows, heads, width), lanes))] + blocks,
        "pack_queries",
        in_specs=[whole()],
        out_specs=[whole()] * (1 + len(blocks)),
        flops=30_000_000_000,
    )(queries)


def pick_kernel(ends_ref, *refs):
    inner_refs, out_ref = refs[:-1], refs[-1]
    plane, _, _ = place()
    inner = (plane == 1) | (plane == 2)

    @pl.when(inner)
    def _():
        begin = 0
        for inner_ref in inner_refs:
            rows = inner_ref.shape[0]
            out_ref[begin : begin + rows, :] = inner_ref[...]
            begin += rows

    @pl.when(jnp.logical_not(inner))
    def _():
        out_ref[...] = ends_ref[...]


def picked(ends, inner):
    return local_call(
        pick_kernel,
        bf16(ends.shape),
        "pick_queries",
        in_specs=[whole()] * (1 + len(inner)),
        out_specs=whole(),
    )(ends, *inner)


def unpack(packed_ref, begin, wide_ref, row, total):
    width = wide_ref.shape[1]
    columns = width // lanes
    half = total // 2
    for i in range(columns):
        wide_ref[row : row + total, i * lanes : (i + 1) * lanes] = packed_ref[
            begin + i * total : begin + (i + 1) * total, :
        ]
    rest = packed_ref[begin + columns * total : begin + columns * total + half, :]
    wide_ref[row : row + half, columns * lanes :] = rest[:, : lanes // 2]
    wide_ref[row + half : row + total, columns * lanes :] = rest[:, lanes // 2 :]


def widened(column, width):
    return jnp.concatenate([column] * (width // lanes), axis=1)


def rows_at(ref, index, rows):
    return ref[pl.ds(pl.multiple_of(index * rows, rows), rows), :]


def visible_tile(length_ref, block, rows, first, width, key_count):
    positions = lax.axis_index("context") * key_count + first + lax.broadcasted_iota(jnp.int32, (rows, width), 1)
    return positions < widened(rows_at(length_ref, block, rows), width)


def chip_mass(length_ref, wide_ref, lse_ref, own_key_ref, pair_key_ref, context, heads, out_ref, before_ref=None):
    width, key_count = own_key_ref.shape
    first_head, head_count = heads
    rows = wide_ref.shape[0] // head_count
    tile = math.gcd(key_count, 512)
    plane, core, _ = place()
    lse = rows_at(lse_ref, context, rows)
    column = widened(rows_at(length_ref, context, rows), tile)
    spread = lax.broadcasted_iota(jnp.int32, (rows, tile), 1)
    for key_ref, half in ((own_key_ref, core), (pair_key_ref, 1 - core)):
        for first in range(0, key_count, tile):
            scores = jnp.dot(wide_ref[...], key_ref[:, first : first + tile], preferred_element_type=jnp.float32)
            summed = jnp.zeros((rows, tile), jnp.float32)
            for h in range(head_count):
                summed = summed + jnp.exp2(
                    scores[h * rows : (h + 1) * rows] * (main_scale * log2_e)
                    - lse[:, first_head + h : first_head + h + 1]
                )
            visible = (2 * plane + half) * key_count + first + spread < column
            mass = jnp.where(visible, summed, 0.0)
            columns = pl.ds(pl.multiple_of(half * key_count + first, tile), tile)
            if before_ref is not None:
                mass = mass + before_ref[:, columns]
            out_ref[:, columns] = mass


def mass_kernel(flip, blocks, length_ref, pack_ref, lse_ref, own_key_ref, pair_key_ref, out_ref, wide_ref):
    plane, core, _ = place()
    heads = (blocks[0][0], sum(count for _, count in blocks))
    rows = wide_ref.shape[0] // heads[1]
    begin = row = 0
    for _, count in blocks:
        unpack(pack_ref, begin, wide_ref, row, rows * count)
        begin += packed_rows(rows, count, wide_ref.shape[1])
        row += rows * count
    chip_mass(length_ref, wide_ref, lse_ref, own_key_ref, pair_key_ref, 2 * (plane ^ flip) + core, heads, out_ref)


def chunk_mass(lengths, pack, lse, keys, flip, blocks, rows, name):
    width, key_count = keys[0].shape
    total = rows * sum(count for _, count in blocks)
    return local_call(
        functools.partial(mass_kernel, flip, blocks),
        f32((rows, 2 * key_count)),
        name,
        in_specs=[whole()] * 5,
        out_specs=whole(),
        scratch=[pltpu.VMEM((total, width), jnp.bfloat16)],
    )(lengths, pack, lse, *keys)


def share_kernel(
    heads, length_ref, pack_ref, lse_ref, own_key_ref, pair_key_ref, own_ref, near_ref, across_ref, before_ref, *refs
):
    outs = refs[:-2]
    wide_ref, chunks_ref = refs[-2:]
    plane, core, group = place()
    unpack(pack_ref, 0, wide_ref, 0, wide_ref.shape[0])
    chunks_ref[0] = own_ref[...]
    chunks_ref[1] = near_ref[...]
    chunks_ref[3] = across_ref[...]
    chip_mass(
        length_ref, wide_ref, lse_ref, own_key_ref, pair_key_ref, 2 * (plane ^ 2) + core, heads, chunks_ref.at[2],
        before_ref,
    )
    for e, out_ref in enumerate(outs):
        out_ref[...] = chunks_ref[plane ^ group ^ e].astype(out_ref.dtype)


def shared_mass(lengths, pack, lse, keys, own, near, across, before, heads, partners):
    width, _ = keys[0].shape
    rows, both = own.shape
    return local_call(
        functools.partial(share_kernel, heads),
        [f32((rows, both))] + [bf16((rows, both))] * (partners - 1),
        "mass_and_share",
        in_specs=[whole()] * 9,
        out_specs=[whole()] * partners,
        scratch=[pltpu.VMEM((rows * heads[1], width), jnp.bfloat16), pltpu.VMEM((4, rows, both), jnp.float32)],
    )(lengths, pack, lse, *keys, own, near, across, before)


def logits_kernel(length_ref, query_ref, key_ref, weight_ref, logits_ref, masked_ref, stats_ref):
    rows, key_count = logits_ref.shape
    heads = query_ref.shape[0] // rows
    tile = math.gcd(key_count, 256)
    group = lax.axis_index("heads")
    best = jnp.full((rows, 1), masked_low, jnp.float32)
    weights = widened(weight_ref[...], tile)
    for first in range(0, key_count, tile):
        dots = lax.dot_general(
            query_ref[...], key_ref[first : first + tile, :], (((1,), (1,)), ((), ())),
            preferred_element_type=jnp.float32,
        )
        masked = jnp.where(dots > 0, weights, 0.0)
        masked_ref[:, first : first + tile] = masked
        logits = jnp.sum((dots * masked).reshape(rows, heads, tile), axis=1)
        logits_ref[:, first : first + tile] = logits
        visible = visible_tile(length_ref, group, rows, first, tile, key_count)
        best = jnp.maximum(best, jnp.max(jnp.where(visible, logits, masked_low), axis=1, keepdims=True))
    visible = visible_tile(length_ref, group, rows, 0, key_count, key_count)
    total = jnp.sum(jnp.where(visible, jnp.exp(logits_ref[...] - best), 0.0), axis=1, keepdims=True)
    column = lax.broadcasted_iota(jnp.int32, (rows, lanes), 1)
    stats_ref[...] = jnp.where(column == 0, best, total)


def index_logits(lengths, flat_query, index_key, weight_wide, rows):
    key_count = index_key.shape[0]
    flat = flat_query.shape[0]
    return local_call(
        logits_kernel,
        [f32((rows, key_count)), f32((flat, key_count)), f32((rows, lanes))],
        "index_logits",
        in_specs=[whole()] * 4,
        out_specs=[whole()] * 3,
    )(lengths, flat_query, index_key, weight_wide)


def load_kernel(
    length_ref, lse_ref, weight_ref, query_hbm, key_hbm, latent_hbm,
    length_out, lse_out, weight_out, query_out, turned_out, key_out, latent_out, semaphores,
):
    copies = [
        pltpu.make_async_copy(source, target, semaphores.at[i])
        for i, (source, target) in enumerate(
            [(query_hbm, query_out), (key_hbm, key_out), (latent_hbm, latent_out)]
        )
    ]
    for copy in copies:
        copy.start()
    total = length_out.shape[0]
    spread = lax.broadcasted_iota(jnp.int32, (8, lanes), 0)
    for first in range(0, total, 8):
        column = jnp.zeros((8, lanes), jnp.int32)
        for i in range(8):
            column = jnp.where(spread == i, length_ref[first + i], column)
        length_out[first : first + 8, :] = column
    lse_out[...] = lse_ref[...].T * log2_e
    rows, heads = weight_ref.shape
    width = key_out.shape[1]
    weights = weight_ref[...].T * width ** (-0.5)
    for t in range(rows):
        weight_out[t * heads : (t + 1) * heads, :] = jnp.broadcast_to(weights[:, t : t + 1], (heads, lanes))
    copies[0].wait()
    turned_out[...] = query_out[...].reshape(rows * heads, width).astype(jnp.float32).T.astype(jnp.bfloat16)
    copies[1].wait()
    copies[2].wait()


def load_inputs(lengths, lse, weights, query, key, latent):
    rows, heads, width = query.shape
    flat = rows * heads
    return local_call(
        load_kernel,
        [
            jax.ShapeDtypeStruct((lengths.shape[0], lanes), jnp.int32),
            f32(lse.shape[::-1]),
            f32((flat, lanes)),
            bf16(query.shape),
            bf16((width, flat)),
            bf16(key.shape),
            bf16(latent.shape),
        ],
        "load_inputs",
        in_specs=[scalars(), whole(), whole(), hbm(), hbm(), hbm()],
        out_specs=[whole()] * 7,
        scratch=[pltpu.SemaphoreType.DMA((3,))],
    )(lengths, lse, weights, query, key, latent)


def join_kernel(stats_ref, own_ref, *refs):
    parts, (keep_ref, give_ref, out_ref) = refs[:-3], refs[-3:]
    mass = own_ref[...]
    for part in parts:
        mass = mass + part[...].astype(jnp.float32)
    rows, both = mass.shape
    low, high = mass[:, : both // 2], mass[:, both // 2 :]
    _, core, _ = place()
    keep_ref[...] = jnp.where(core == 0, low, high)
    give_ref[...] = jnp.where(core == 0, high, low)
    total = jnp.broadcast_to(jnp.sum(mass, axis=1, keepdims=True), (rows, lanes))
    nothing = jnp.zeros((rows, lanes), jnp.float32)
    totals = jnp.concatenate([jnp.where(core == 0, total, nothing), jnp.where(core == 0, nothing, total)], axis=0)
    column = lax.broadcasted_iota(jnp.int32, out_ref.shape, 1)
    out_ref[...] = jnp.where(column == 2, totals, stats_ref[...])


def joined_mass(stats, own, parts):
    rows, both = own.shape
    return local_call(
        join_kernel,
        [f32((rows, both // 2)), f32((rows, both // 2)), f32(stats.shape)],
        "join_mass",
        in_specs=[whole()] * (2 + len(parts)),
        out_specs=[whole()] * 3,
    )(stats, own, *parts)


def merge_kernel(*refs):
    out_ref = refs[-1]
    stats = [ref[...] for ref in refs[:-1]]
    top = functools.reduce(jnp.maximum, [s[:, 0:1] for s in stats])
    shares = sum(s[:, 1:2] * jnp.exp(s[:, 0:1] - top) for s in stats)
    column = lax.broadcasted_iota(jnp.int32, out_ref.shape, 1)
    out_ref[...] = jnp.where(column == 0, top, jnp.where(column == 1, shares, sum(stats)))


def merged_stats(stats):
    return local_call(
        merge_kernel, f32(stats[0].shape), "merge_stats", in_specs=[whole()] * len(stats), out_specs=whole()
    )(*stats)


def back_rows(half, length_ref, stats_ref, mass_ref, logits_ref, turned_ref, key_ref, masked_ref, slope_ref, store):
    rows, key_count = mass_ref.shape
    width = key_ref.shape[1]
    flat = turned_ref.shape[1] // 2
    tile = math.gcd(key_count, 256)
    stats = rows_at(stats_ref, half, rows)
    visible = visible_tile(length_ref, 2 * lax.axis_index("heads") + half, rows, 0, key_count, key_count)
    weights_exp = jnp.where(visible, jnp.exp(rows_at(logits_ref, half, rows) - stats[:, 0:1]), 0.0)
    slope_ref[...] = loss_scale * (weights_exp / stats[:, 1:2] - mass_ref[...] / stats[:, 2:3])
    begin = pl.multiple_of(half * flat, flat)
    turned = turned_ref[:, pl.ds(begin, flat)]
    query_grad = jnp.zeros((flat, width), jnp.float32)
    for first in range(0, key_count, tile):
        keys = key_ref[first : first + tile, :]
        slopes = jnp.broadcast_to(slope_ref[:, first : first + tile][:, None, :], (rows, flat // rows, tile))
        masked = masked_ref[pl.ds(begin, flat), first : first + tile]
        terms = (slopes.reshape(flat, tile) * masked).astype(jnp.bfloat16)
        query_grad = query_grad + jnp.dot(terms, keys, preferred_element_type=jnp.float32)
        store(first, tile, jnp.dot(turned, terms, preferred_element_type=jnp.float32))
    return query_grad


def back_own_kernel(
    length_ref, stats_ref, mass_ref, logits_ref, turned_ref, key_ref, masked_ref, query_out, key_out, slope_ref
):
    _, core, _ = place()

    def store(first, tile, key_grad):
        key_out[:, first : first + tile] = key_grad

    query_out[...] = back_rows(
        core, length_ref, stats_ref, mass_ref, logits_ref, turned_ref, key_ref, masked_ref, slope_ref, store
    )


def back_own(lengths, stats, mass, logits, turned, index_key, masked):
    rows, key_count = mass.shape
    width, flat = turned.shape
    return local_call(
        back_own_kernel,
        [f32((flat // 2, width)), f32((width, key_count))],
        "index_back_own",
        in_specs=[whole()] * 7,
        out_specs=[whole()] * 2,
        scratch=[pltpu.VMEM((rows, key_count), jnp.float32)],
    )(lengths, stats, mass, logits, turned, index_key, masked)


def back_pair_kernel(
    length_ref, stats_ref, mass_ref, logits_ref, turned_ref, key_ref, masked_ref, query_ref, before_ref, *refs
):
    partners = len(refs) - 4
    key_outs = refs[:partners]
    keep_ref, send_ref, slope_ref, grad_ref = refs[partners:]
    key_count, width = key_ref.shape
    _, core, group = place()

    def store(first, tile, key_grad):
        grad_ref[first : first + tile, :] = (before_ref[:, first : first + tile] + key_grad).T

    other = back_rows(
        1 - core, length_ref, stats_ref, mass_ref, logits_ref, turned_ref, key_ref, masked_ref, slope_ref, store
    )
    block = key_count // partners
    for e, out_ref in enumerate(key_outs):
        out_ref[...] = rows_at(grad_ref, group ^ e, block).astype(out_ref.dtype)
    planes, part, _ = keep_ref.shape
    rows = mass_ref.shape[0]
    for half, query_grad in ((core, query_ref[...]), (1 - core, other)):
        split = query_grad.reshape(rows, planes, 2, part // (2 * rows), width)
        place_of = pl.ds(pl.multiple_of(half * (part // 2), part // 2), part // 2)
        for plane in range(planes):
            low = split[:, plane, 0].reshape(part // 2, width)
            high = split[:, plane, 1].reshape(part // 2, width)
            keep_ref[plane, place_of, :] = jnp.where(core == 0, low, high)
            send_ref[plane, place_of, :] = jnp.where(core == 0, high, low).astype(jnp.bfloat16)


def back_pair(lengths, stats, mass, logits, turned, index_key, masked, query_grad, key_grad, partners, planes):
    rows, key_count = mass.shape
    width, flat = turned.shape
    part = flat // (2 * planes)
    return local_call(
        back_pair_kernel,
        [f32((key_count // partners, width))]
        + [bf16((key_count // partners, width))] * (partners - 1)
        + [f32((planes, part, width)), bf16((planes, part, width))],
        "index_back_pair",
        in_specs=[whole()] * 9,
        out_specs=[whole()] * (partners + 2),
        scratch=[pltpu.VMEM((rows, key_count), jnp.float32), pltpu.VMEM((key_count, width), jnp.float32)],
    )(lengths, stats, mass, logits, turned, index_key, masked, query_grad, key_grad)


def pair_kernel(keep_ref, got_ref, *outs):
    own_plane, _, _ = place()
    for e, out_ref in enumerate(outs):
        plane = own_plane ^ e
        out_ref[...] = (keep_ref[plane] + got_ref[plane].astype(jnp.float32)).astype(out_ref.dtype)


def pair_sums(keep, got):
    planes, part, width = keep.shape
    return local_call(
        pair_kernel,
        [f32((part, width))] + [bf16((part, width))] * (planes - 1),
        "pair_sums",
        in_specs=[whole(), whole()],
        out_specs=[whole()] * planes,
    )(keep, got)


def sum_kernel(*refs):
    out_ref = refs[-1]
    out_ref[...] = sum(ref[...].astype(jnp.float32) for ref in refs[:-1]).reshape(out_ref.shape)


def summed(parts, shape, name):
    return local_call(sum_kernel, f32(shape), name, in_specs=[whole()] * len(parts), out_specs=whole())(*parts)


def after(array, *others):
    return lax.optimization_barrier((array, *others))[0]


def block_device(main_query, latent_keys, head_lse, lengths, index_query, index_key, index_weight):
    contexts = lax.axis_size("context")
    planes = contexts // 2
    partners = lax.axis_size("heads")
    context = lax.axis_index("context")
    rows, heads, _ = main_query.shape
    own_rows, index_heads, width = index_query.shape
    key_count = latent_keys.shape[0]
    flat = own_rows * index_heads

    def planes_move(array, pairs):
        return lax.ppermute(array, "context", [(2 * a + k, 2 * b + k) for a, b in pairs for k in (0, 1)])

    def context_flip(array, e):
        return lax.ppermute(array, "context", [(c, c ^ e) for c in range(contexts)])

    def heads_flip(array, e):
        return lax.ppermute(array, "heads", [(h, h ^ e) for h in range(partners)])

    keys_pair = context_flip(latent_keys.T, 1)
    pack, *inner = packed_queries(main_query)
    inner = [planes_move(block, [(1, 2), (2, 1), (0, 0), (3, 3)]) for block in inner]
    near = planes_move(pack, [(0, 1), (1, 0), (2, 3), (3, 2)])
    ends = planes_move(pack, [(0, 3), (3, 0)])
    lengths, lse, weight_wide, query, turned, index_key, keys = load_inputs(
        lengths, head_lse.T, index_weight, index_query, index_key, after(latent_keys, pack).T
    )
    keys = (keys, keys_pair)

    blocks = head_blocks(heads)

    def mass_of(pack, flip, blocks, *rest):
        return chunk_mass(lengths, pack, lse, keys, flip, blocks, rows, *rest)

    inner[1] = after(inner[1], lse)
    far = [planes_move(block, [(0, 2), (3, 1), (1, 0), (2, 3)]) for block in inner]
    logits, masked, stats = index_logits(lengths, query.reshape(flat, width), index_key, weight_wide, own_rows)
    stats = merged_stats([stats, context_flip(stats, 1)])
    own_mass = mass_of(pack, 0, blocks, "mass_own")
    near_mass = mass_of(after(near, logits), 1, blocks, "mass_near")
    across_mass = mass_of(picked(after(ends, own_mass, near_mass), inner), 3, blocks, "mass_across")
    far_mass = mass_of(after(far[0], across_mass, stats), 2, blocks[:1], "mass_far")
    shared = shared_mass(
        lengths, after(far[1], far_mass), lse, keys, own_mass, near_mass, across_mass, far_mass, blocks[1], partners
    )
    keep_mass, give_mass, stats = joined_mass(
        stats, shared[0], [heads_flip(shared[e], e) for e in (*reversed(range(1, partners - 1)), partners - 1)]
    )
    got_mass = context_flip(give_mass, 1)
    stats = merged_stats([stats] + [context_flip(stats, 2 * e) for e in reversed(range(1, planes))])
    back = (logits, turned, index_key, masked)
    query_grad, key_grad = back_own(lengths, stats, keep_mass, *back)
    *key_grads, keep, send = back_pair(
        lengths, context_flip(stats, 1), got_mass, *back, query_grad, key_grad, partners, planes
    )
    sums = pair_sums(keep, context_flip(send, 1))
    key_grads[-1] = after(key_grads[-1], sums[0])
    key_parts = [key_grads[0]] + [heads_flip(key_grads[e], e) for e in range(1, partners)]
    query_parts = [sums[0]] + [context_flip(sums[e], 2 * e) for e in reversed(range(1, planes))]
    out_key = summed(key_parts, key_parts[0].shape, "key_sums")
    query_parts[1] = after(query_parts[1], out_key)
    return summed(query_parts, (own_rows, index_heads // contexts, width), "query_sums"), out_key


def fits(mesh):
    return mesh.shape["context"] == 8 and mesh.shape["heads"] == 4


def solution(mesh):
    placed = (
        P("context", "heads", None),
        P("context", None),
        P(None, "heads"),
        P(),
        P("heads", None, None),
        P("context", None),
        P("heads", None),
    )
    return jax.shard_map(
        block_device if fits(mesh) else general_on_device,
        mesh=mesh,
        in_specs=placed,
        out_specs=(P("heads", "context", None), P(("context", "heads"), None)),
        check_vma=False,
    )
```
